32 devices in a mesh: lon: 8 (over z, y), lat: 4 (over x, core).
Axes of the slice: x: 2, y: 2, z: 4, core: 2. Of those that a mesh axis runs over, the one named last changes fastest.
Arguments:
- queries: bfloat16 [64, 128, 256], P('lat', 'lon'), may hold values from -11 to 11
- key_values: bfloat16 [2, 64, 128, 256], P(None, 'lat', 'lon'), may hold values from -11 to 11
- pole_mask: int32 [8], replicated, may hold values 0 or 1
- sea_mask: int32 [8, 16], replicated, may hold values 0 or 1
- reg_queries: bfloat16 [256, 256], replicated, may hold values from -21 to 21
- reg_keys: bfloat16 [256, 256], replicated, may hold values from -6 to 6
Outputs:
- attended: bfloat16 [64, 128, 256], P('lat', 'lon')
- reg_out: bfloat16 [256, 256], replicated
The draws below stay inside these ranges and needn't reach their ends.
All inputs are finite; a program needn't handle non-finite values.
Results may differ from the reference program's by a relative error of at most 0.0048.
Values may be sent and summed in bfloat16 or wider, within the bound.
No kernel may reach another device: no remote copies, remote signals or barrier semaphores. Data moves between devices by JAX's collectives and lax.ppermute only.
A program may use at most 64 MiB of HBM per device.

```python
import jax
import jax.numpy as jnp
from jax import lax

HEADS = 4
HEAD_DIM = 64
NREG = 256
RADIUS = 6
TILE = 8
QROWS = 16
CHANNELS = 256
NLAT = 64
NLON = 128


def shared_keys(key):
    base = jax.random.fold_in(key, 7)
    first = jax.random.fold_in(base, 0)
    return jnp.clip(jax.random.normal(first, (NLAT, NLON, HEADS * HEAD_DIM), jnp.float32), -6.0, 6.0)


def draw_key_values(key, part):
    channels = HEADS * HEAD_DIM
    keys_drawn = shared_keys(key)
    value_key = jax.random.fold_in(key, 9)
    values_drawn = jnp.clip(jax.random.normal(value_key, (NLAT, NLON, channels), jnp.float32), -6.0, 6.0)
    return jnp.stack([keys_drawn, values_drawn]).astype(jnp.bfloat16)


def draw_queries(key, part):
    channels = HEADS * HEAD_DIM
    noise_key = jax.random.fold_in(key, 13)
    drawn = jnp.clip(jax.random.normal(noise_key, (NLAT, NLON, channels), jnp.float32), -6.0, 6.0)
    return drawn.astype(jnp.bfloat16)


def draw_reg_queries(key, part):
    channels = HEADS * HEAD_DIM
    noise_key = jax.random.fold_in(key, 17)
    drawn = 3.5 * jnp.clip(jax.random.normal(noise_key, (NREG, channels), jnp.float32), -6.0, 6.0)
    return drawn.astype(jnp.bfloat16)


def touch_ends(result, own_key, low, high):
    longest = result.shape.index(max(result.shape))
    spots = []
    for shift in (0, 1):
        where = [jax.random.randint(jax.random.fold_in(own_key, axis), (), 0, length) for axis, length in enumerate(result.shape)]
        where[longest] = (where[longest] + shift) % result.shape[longest]
        spots.append(tuple(where))
    return result.at[spots[0]].set(low).at[spots[1]].set(high)


def bell_draw(stream_key, extent, deviation, bound, kind=jnp.bfloat16):
    return jnp.clip(deviation * jax.random.normal(stream_key, extent, jnp.float32), -bound, bound).astype(kind)


def setup_inputs(seed: int = 0) -> dict:
    key_list = jax.random.split(jax.random.key(seed), 7)
    queries = draw_queries(jax.random.fold_in(key_list[6], 71), 0)
    key_values = draw_key_values(jax.random.fold_in(key_list[6], 71), 0)
    pole_mask = touch_ends((jax.random.randint(key_list[2], (NLAT // TILE,), 0, 4) < 3).astype(jnp.int32), jax.random.fold_in(key_list[2], 1), 0, 1)
    sea_mask = touch_ends((jax.random.randint(key_list[3], (NLAT // TILE, NLON // TILE), 0, 3) < 2).astype(jnp.int32), jax.random.fold_in(key_list[3], 1), 0, 1)
    reg_queries = draw_reg_queries(jax.random.fold_in(key_list[6], 71), 0)
    reg_keys = bell_draw(key_list[5], (NREG, CHANNELS), 1.0, 6.0)
    return {"queries": queries, "key_values": key_values, "pole_mask": pole_mask, "sea_mask": sea_mask, "reg_queries": reg_queries, "reg_keys": reg_keys}


def cell_keep(pole_mask, sea_mask):
    tiles = pole_mask[:, None] * sea_mask
    return jnp.repeat(jnp.repeat(tiles, TILE, axis=0), TILE, axis=1)


def register_pass(reg_queries, key_values):
    scale_factor = HEAD_DIM ** -0.5
    heads_query = reg_queries.astype(jnp.float32).reshape(NREG, HEADS, HEAD_DIM)
    block_count = NLAT // QROWS
    block_keys = key_values[0].reshape(block_count, QROWS * NLON, HEADS, HEAD_DIM)
    block_values = key_values[1].reshape(block_count, QROWS * NLON, HEADS, HEAD_DIM)

    def block_scores(keys_block):
        return jnp.einsum("rhd,khd->hrk", heads_query, keys_block.astype(jnp.float32)) * scale_factor

    def step_max(running, keys_block):
        return jnp.maximum(running, jnp.max(block_scores(keys_block), axis=2)), None

    highest, unused = lax.scan(step_max, jnp.full((HEADS, NREG), -jnp.inf, jnp.float32), block_keys)

    def step_sum(running, block_pair):
        weights = jnp.exp(block_scores(block_pair[0]) - highest[:, :, None])
        rounded = lax.optimization_barrier(weights.astype(jnp.bfloat16)).astype(jnp.float32)
        added = jnp.einsum("hrk,khd->rhd", rounded, block_pair[1].astype(jnp.float32))
        return (running[0] + jnp.sum(weights, axis=2), running[1] + added), None

    initial = (jnp.zeros((HEADS, NREG), jnp.float32), jnp.zeros((NREG, HEADS, HEAD_DIM), jnp.float32))
    (weight_sums, weighted), unused = lax.scan(step_sum, initial, (block_keys, block_values))
    return (weighted / weight_sums.T[:, :, None]).astype(jnp.bfloat16).reshape(NREG, HEADS * HEAD_DIM)


def reference(queries, key_values, pole_mask, sea_mask, reg_queries, reg_keys):
    scale_factor = HEAD_DIM ** -0.5
    channels = HEADS * HEAD_DIM
    span = 2 * RADIUS + 1
    reg_values = register_pass(reg_queries, key_values)
    keep = cell_keep(pole_mask, sea_mask)
    padded = jnp.pad(key_values, ((0, 0), (RADIUS, RADIUS), (0, 0), (0, 0)))
    padded = jnp.concatenate([padded[:, :, NLON - RADIUS:], padded, padded[:, :, :RADIUS]], axis=2)
    keep_pad = jnp.pad(keep, ((RADIUS, RADIUS), (0, 0)))
    keep_pad = jnp.concatenate([keep_pad[:, NLON - RADIUS:], keep_pad, keep_pad[:, :RADIUS]], axis=1)
    reg_key_heads = reg_keys.astype(jnp.float32).reshape(NREG, HEADS, HEAD_DIM)
    reg_value_heads = reg_values.astype(jnp.float32).reshape(NREG, HEADS, HEAD_DIM)
    offsets = jnp.arange(span * span, dtype=jnp.int32)

    def one_block(first_row):
        block_queries = lax.dynamic_slice_in_dim(queries, first_row, QROWS, 0).astype(jnp.float32)
        block_queries = block_queries.reshape(QROWS, NLON, HEADS, HEAD_DIM)

        def shifted(offset):
            lat_shift = offset // span
            lon_shift = offset % span
            zero_index = jnp.zeros((), jnp.int32)
            window = lax.dynamic_slice(padded, (zero_index, first_row + lat_shift, lon_shift, zero_index), (2, QROWS, NLON, channels))
            mask_window = lax.dynamic_slice(keep_pad, (first_row + lat_shift, lon_shift), (QROWS, NLON))
            return window, mask_window

        def near_score(offset):
            window, mask_window = shifted(offset)
            keys_here = window[0].astype(jnp.float32).reshape(QROWS, NLON, HEADS, HEAD_DIM)
            scores = jnp.sum(block_queries * keys_here, axis=3) * scale_factor
            return jnp.where(mask_window[:, :, None] > 0, scores, -jnp.inf)

        near_scores = lax.map(near_score, offsets)
        reg_scores = jnp.einsum("ijhd,rhd->ijhr", block_queries, reg_key_heads) * scale_factor
        highest = jnp.maximum(jnp.max(near_scores, axis=0), jnp.max(reg_scores, axis=3))
        near_weights = jnp.exp(near_scores - highest[None])
        reg_weights = jnp.exp(reg_scores - highest[:, :, :, None])
        weight_sums = jnp.sum(near_weights, axis=0) + jnp.sum(reg_weights, axis=3)
        near_rounded = lax.optimization_barrier(near_weights.astype(jnp.bfloat16)).astype(jnp.float32)
        reg_rounded = lax.optimization_barrier(reg_weights.astype(jnp.bfloat16)).astype(jnp.float32)

        def add_offset(running, offset):
            window, unused_mask = shifted(offset)
            values_here = window[1].astype(jnp.float32).reshape(QROWS, NLON, HEADS, HEAD_DIM)
            weight_here = lax.dynamic_index_in_dim(near_rounded, offset, 0, keepdims=False)
            return running + weight_here[..., None] * values_here, None

        start_value = jnp.einsum("ijhr,rhd->ijhd", reg_rounded, reg_value_heads)
        mixture, unused = lax.scan(add_offset, start_value, offsets)
        return (mixture / weight_sums[..., None]).astype(jnp.bfloat16).reshape(QROWS, NLON, channels)

    starts = jnp.arange(NLAT // QROWS, dtype=jnp.int32) * QROWS
    attended = lax.map(one_block, starts).reshape(NLAT, NLON, channels)
    return (attended, reg_values)
```

```python
import functools

import jax
import jax.numpy as jnp
from jax import lax
from jax.experimental import pallas as pl
from jax.experimental.pallas import tpu as pltpu
from jax.sharding import PartitionSpec as P

HEADS = 4
HEAD_DIM = 64
NREG = 256
RADIUS = 6
TILE = 8
PAIR = 2 * HEAD_DIM
SIDE = 8
STATS = 16
AUG = 128
MASKED = -8192.0
SCALE = HEAD_DIM ** (-0.5)

BF16 = jnp.bfloat16
F32 = jnp.float32
NT = (((1,), (1,)), ((), ()))
TN = (((0,), (0,)), ((), ()))
VMEM = pl.BlockSpec(memory_space=pltpu.VMEM)
SMEM = pl.BlockSpec(memory_space=pltpu.SMEM)


def dot(a, b, dims):
    return lax.dot_general(a, b, dims, preferred_element_type=F32)


def iota(shape, axis):
    return lax.broadcasted_iota(jnp.int32, shape, axis)


def call(kernel, out, args, specs, scratch=(), flops=0, limit=16):
    size = sum(a.size * a.dtype.itemsize for a in args)
    return pl.pallas_call(
        kernel,
        out_shape=out,
        in_specs=specs,
        out_specs=jax.tree.map(lambda _: VMEM, out),
        scratch_shapes=scratch,
        compiler_params=pltpu.CompilerParams(vmem_limit_bytes=limit * 2**20),
        cost_estimate=pl.CostEstimate(flops=flops, bytes_accessed=size, transcendentals=0),
    )(*args)


def pack(values, tops, sums, out_ref):
    rows = iota((STATS, values.shape[1]), 0)
    stats = jnp.zeros((STATS, values.shape[1]), F32)
    for j in range(2):
        high = sums[j].astype(BF16).astype(F32)
        for row, value in ((j, tops[j]), (2 + 2 * j, high), (3 + 2 * j, sums[j] - high)):
            stats = jnp.where(rows == row, value, stats)
    out_ref[:PAIR] = values.astype(BF16)
    out_ref[PAIR:] = stats.astype(BF16)


def register_kernel(place, own, other, queries, out_ref):
    lanes = pl.ds(pl.multiple_of(place[0] * PAIR, PAIR), PAIR)
    keys = jnp.concatenate([own[0, :, lanes], other[0, :, lanes]], axis=0)
    vals = jnp.concatenate([own[1, :, lanes], other[1, :, lanes]], axis=0)
    scaled = queries[:, lanes] * jnp.asarray(SCALE, BF16)
    first = iota(scaled.shape, 1) < HEAD_DIM
    parts, tops, sums = [], [], []
    for j in range(2):
        mine = jnp.where(first == (j == 0), scaled, jnp.zeros_like(scaled))
        scores = dot(keys, mine, NT)
        top = jnp.max(scores, axis=0, keepdims=True).astype(BF16).astype(F32)
        weights = jnp.exp(scores - top)
        sums.append(jnp.sum(weights, axis=0, keepdims=True))
        tops.append(top)
        parts.append(dot(vals, weights.astype(BF16), TN))
    upper = iota(parts[0].shape, 0) < HEAD_DIM
    pack(jnp.where(upper, parts[0], parts[1]), tops, sums, out_ref)


def merge_kernel(bits, last, place, *refs):
    payloads, out_ref = refs[:-1], refs[-1]
    found = [(r[:PAIR].astype(F32), r[PAIR:].astype(F32)) for r in payloads]
    for level, bit in enumerate(bits):
        swap = place[1 + bit] == 1
        step = 1 << level
        for low in range(len(found)):
            if not low & step:
                a, b = found[low], found[low + step]
                found[low] = tuple(jnp.where(swap, v, u) for u, v in zip(a, b))
                found[low + step] = tuple(jnp.where(swap, u, v) for u, v in zip(a, b))
    upper = iota((PAIR, found[0][0].shape[1]), 0) < HEAD_DIM
    tops, sums, factors = [], [], []
    for j in range(2):
        each = [stats[j : j + 1] for _, stats in found]
        top = functools.reduce(jnp.maximum, each)
        factor = [jnp.exp(e - top) for e in each]
        totals = [
            f * (stats[2 + 2 * j : 3 + 2 * j] + stats[3 + 2 * j : 4 + 2 * j])
            for f, (_, stats) in zip(factor, found)
        ]
        tops.append(top)
        sums.append(functools.reduce(jnp.add, totals))
        factors.append(factor)
    merged = functools.reduce(
        jnp.add,
        [values * jnp.where(upper, f, g) for f, g, (values, _) in zip(*factors, found)],
    )
    if last:
        out_ref[...] = (merged / jnp.where(upper, sums[0], sums[1])).astype(BF16)
    else:
        pack(merged, tops, sums, out_ref)


def segments(rows, cols):
    return (
        (rows * cols, cols, 0, 0),
        (RADIUS * cols, cols, "core", 0),
        (rows * SIDE, SIDE, 0, "a"),
        (rows * SIDE, SIDE, 0, "b"),
        (RADIUS * SIDE, SIDE, "core", "a"),
        (RADIUS * SIDE, SIDE, "core", "b"),
        (RADIUS * cols, cols, "cross", 0),
        (RADIUS * SIDE, SIDE, "cross", "a"),
        (RADIUS * SIDE, SIDE, "cross", "b"),
    )


def mask_kernel(rows, cols, nbits, place, pole, sea, out_ref):
    lat, lon = place[1 + nbits], place[2 + nbits]
    lat_odd, lon_odd = lat % 2, lon % 2
    starts = {
        0: 0,
        "core": jnp.where(lat_odd == 0, rows, -RADIUS),
        "cross": jnp.where(lat_odd == 0, -RADIUS, rows),
        "a": jnp.where(lon_odd == 0, cols, -SIDE),
        "b": jnp.where(lon_odd == 0, -SIDE, cols),
    }
    bands, tiles = sea.shape
    down, across = rows // TILE, cols // TILE
    lane = iota((1, AUG), 1)
    closed = jnp.zeros((1, AUG), F32)
    for i in range(down + 2):
        band = lat * down - 1 + i
        inside = (band >= 0) & (band < bands)
        band = jnp.clip(band, 0, bands - 1)
        for j in range(across + 2):
            tile = (lon * across - 1 + j + tiles) % tiles
            open_ = inside & (pole[band] * sea[band, tile] > 0)
            at = rows + cols + i * (across + 2) + j
            closed = jnp.where(lane == at, jnp.where(open_, 0.0, MASKED), closed)
    offset = 0
    for count, width, down_name, across_name in segments(rows, cols):
        index = iota((count, AUG), 0)
        row = starts[down_name] + index // width
        col = starts[across_name] + index % width
        lanes = iota((count, AUG), 1)
        apart = jnp.where(lanes < rows, lanes - row, lanes - rows - col)
        far = (lanes < rows + cols) & (jnp.abs(apart) > RADIUS)
        cell = ((row + TILE) // TILE) * (across + 2) + (col + TILE) // TILE
        value = jnp.where(lanes - (rows + cols) == cell, closed, 0.0)
        out_ref[offset : offset + count] = jnp.where(far, MASKED, value).astype(BF16)
        offset += count


def near_kernel(rows, cols, nbits, place, q_ref, own, core, a, b, corner, cross, mask, reg_keys,
                acc_ref, scale_ref, reg_ref, kbuf, vbuf):
    cells = mask.shape[0]
    lat = place[1 + nbits]
    taken = pl.ds(pl.multiple_of(jnp.where(lat % 2 == 0, 0, (rows - RADIUS) * cols), 16), RADIUS * cols)
    offset = 0
    for ref, index in ((own, slice(None)), (core, taken), (a, slice(None)), (b, slice(None)),
                       (corner, slice(None)), (cross, slice(None))):
        keys, vals = ref[0, index], ref[1, index]
        end = offset + keys.shape[0]
        for p in range(2):
            kbuf[p, offset:end, :PAIR] = keys[:, p * PAIR : (p + 1) * PAIR]
        vbuf[offset:end] = vals
        offset = end
    for p in range(2):
        kbuf[p, :cells, PAIR:] = mask[...]
        kbuf[p, cells:, :PAIR] = reg_keys[:, p * PAIR : (p + 1) * PAIR]
        kbuf[p, cells:, PAIR:] = jnp.zeros((NREG, AUG), BF16)
    count = rows * cols
    query = iota((count, AUG), 0)
    lane = iota((count, AUG), 1)
    tiles = (rows // TILE + 2) * (cols // TILE + 2)
    hot = (lane == query // cols) | (lane - rows == query % cols)
    hot = hot | ((lane >= rows + cols) & (lane < rows + cols + tiles))
    hot = jnp.where(hot, 1.0, 0.0).astype(BF16)
    first = iota((count, PAIR), 1) < HEAD_DIM
    for p in range(2):
        scaled = q_ref[:, p * PAIR : (p + 1) * PAIR] * jnp.asarray(SCALE, BF16)
        mixed, totals = [], []
        for j in range(2):
            mine = jnp.where(first == (j == 0), scaled, jnp.zeros_like(scaled))
            scores = dot(jnp.concatenate([mine, hot], axis=1), kbuf[p], NT)
            weights = jnp.exp(scores - jnp.max(scores, axis=1, keepdims=True))
            totals.append(jnp.sum(weights, axis=1, keepdims=True))
            rounded = weights.astype(BF16)
            reg_ref[2 * p + j] = rounded[:, cells:]
            mixed.append(
                jnp.dot(rounded[:, :cells], vbuf[:, p * PAIR : (p + 1) * PAIR], preferred_element_type=F32)
            )
        acc_ref[:, p * PAIR : (p + 1) * PAIR] = jnp.where(first, *mixed)
        scale_ref[:, p * PAIR : (p + 1) * PAIR] = 1.0 / jnp.where(first, *totals)


def final_kernel(place, acc, scale, reg_weights, mine, other, out_ref, reg_out_ref):
    here = place[0] == 0
    first = iota((acc.shape[0], PAIR), 1) < HEAD_DIM
    for p in range(2):
        lanes = slice(p * PAIR, (p + 1) * PAIR)
        vals = jnp.where(here == (p == 0), mine[...], other[...])
        added = jnp.where(first, dot(reg_weights[2 * p], vals, NT), dot(reg_weights[2 * p + 1], vals, NT))
        out_ref[:, lanes] = ((acc[:, lanes] + added) * scale[:, lanes]).astype(BF16)
        reg_out_ref[:, lanes] = vals.astype(F32).T.astype(BF16)


def shards(queries, key_values, pole_mask, sea_mask, reg_queries, reg_keys):
    rows, cols, channels = queries.shape
    lats, lons = lax.axis_size("lat"), lax.axis_size("lon")
    devices = lats * lons
    assert lats == 4 and lons & (lons - 1) == 0 and lons > 1
    nbits = devices.bit_length() - 1
    lat, lon = lax.axis_index("lat"), lax.axis_index("lon")
    flat = lon * lats + lat
    bits = [(flat >> b) & 1 for b in range(nbits)]
    half = functools.reduce(jnp.bitwise_xor, bits)
    place = jnp.stack([half, *bits, lat, lon]).astype(jnp.int32)
    everyone = ("lon", "lat")

    def swap(x, mask):
        return lax.ppermute(x, everyone, [(i, i ^ mask) for i in range(devices)])

    cells = rows * cols
    own = key_values.reshape(2, cells, channels)
    core = swap(own, 1)

    near_cols = lax.dynamic_slice_in_dim(key_values, (1 - lon % 2) * (cols - SIDE), SIDE, 2)
    far_cols = lax.dynamic_slice_in_dim(key_values, (lon % 2) * (cols - SIDE), SIDE, 2)
    side_a = swap(near_cols, lats)
    side_b = lax.ppermute(
        far_cols, "lon", [(i, (i + 1 if i % 2 else i - 1) % lons) for i in range(lons)]
    )

    payload = call(
        register_kernel,
        jax.ShapeDtypeStruct((PAIR + STATS, NREG), BF16),
        (place, own, core, reg_queries),
        [SMEM, VMEM, VMEM, VMEM],
        flops=4 * 2 * cells * NREG * 2 * PAIR,
    )

    core_first = (1 - lat % 2) * (rows - RADIUS)
    cross_first = (lat % 2) * (rows - RADIUS)

    def edge(shard, start):
        taken = lax.dynamic_slice_in_dim(shard, start, RADIUS, 1)
        return taken.reshape(2, RADIUS * shard.shape[2], channels)

    corner = swap(jnp.concatenate([edge(side_a, core_first), edge(side_b, core_first)], axis=1), 1)
    cross = swap(
        jnp.concatenate(
            [edge(key_values, cross_first), edge(side_a, cross_first), edge(side_b, cross_first)], axis=1
        ),
        3,
    )

    mask = call(
        functools.partial(mask_kernel, rows, cols, nbits),
        jax.ShapeDtypeStruct((sum(s[0] for s in segments(rows, cols)), AUG), BF16),
        (place, pole_mask, sea_mask),
        [SMEM, SMEM, SMEM],
    )

    stages = [tuple(range(b, min(b + 2, nbits))) for b in range(1, nbits, 2)]
    for stage in stages:
        gathered = [payload]
        for chosen in range(1, 1 << len(stage)):
            flips = [b for k, b in enumerate(stage) if chosen >> k & 1]
            gathered.append(swap(payload, sum(1 << b for b in flips) + len(flips) % 2))
        last = stage is stages[-1]
        payload = call(
            functools.partial(merge_kernel, stage, last),
            jax.ShapeDtypeStruct((PAIR if last else PAIR + STATS, NREG), BF16),
            (place, *gathered),
            [SMEM] + [VMEM] * len(gathered),
        )

    square = jax.ShapeDtypeStruct((cells, channels), F32)
    acc, scale, reg_weights = call(
        functools.partial(near_kernel, rows, cols, nbits),
        (square, square, jax.ShapeDtypeStruct((HEADS, cells, NREG), BF16)),
        (
            place,
            queries.reshape(cells, channels),
            own,
            core,
            side_a.reshape(2, rows * SIDE, channels),
            side_b.reshape(2, rows * SIDE, channels),
            corner,
            cross,
            mask,
            reg_keys,
        ),
        [SMEM] + [VMEM] * 9,
        scratch=[
            pltpu.VMEM((2, mask.shape[0] + NREG, PAIR + AUG), BF16),
            pltpu.VMEM((mask.shape[0], channels), BF16),
        ],
        flops=2 * 2 * cells * mask.shape[0] * channels * 2,
        limit=32,
    )
    other = swap(payload, 1)
    attended, reg_out = call(
        final_kernel,
        (
            jax.ShapeDtypeStruct((cells, channels), BF16),
            jax.ShapeDtypeStruct((NREG, channels), BF16),
        ),
        (place, acc, scale, reg_weights, payload, other),
        [SMEM] + [VMEM] * 5,
        flops=2 * cells * NREG * channels * 2,
    )
    return attended.reshape(rows, cols, channels), reg_out


def solution(mesh):
    return jax.shard_map(
        shards,
        mesh=mesh,
        in_specs=(P("lat", "lon", None), P(None, "lat", "lon", None), P(), P(), P(), P()),
        out_specs=(P("lat", "lon", None), P()),
        check_vma=False,
    )
```

```python
import functools

import jax
import jax.numpy as jnp
from jax import lax
from jax.experimental import pallas as pl
from jax.experimental.pallas import tpu as pltpu
from jax.sharding import PartitionSpec as P

HEADS = 4
HEAD_DIM = 64
NREG = 256
RADIUS = 6
TILE = 8
PAIR = 2 * HEAD_DIM
SIDE = 8
STATS = 16
AUG = 128
MASKED = -8192.0
SCALE = HEAD_DIM ** (-0.5)

BF16 = jnp.bfloat16
F32 = jnp.float32
NT = (((1,), (1,)), ((), ()))
TN = (((0,), (0,)), ((), ()))
VMEM = pl.BlockSpec(memory_space=pltpu.VMEM)
SMEM = pl.BlockSpec(memory_space=pltpu.SMEM)


def dot(a, b, dims):
    return lax.dot_general(a, b, dims, preferred_element_type=F32)


def iota(shape, axis):
    return lax.broadcasted_iota(jnp.int32, shape, axis)


def call(kernel, out, args, specs, scratch=(), flops=0, limit=16):
    size = sum(a.size * a.dtype.itemsize for a in args)
    return pl.pallas_call(
        kernel,
        out_shape=out,
        in_specs=specs,
        out_specs=jax.tree.map(lambda _: VMEM, out),
        scratch_shapes=scratch,
        compiler_params=pltpu.CompilerParams(vmem_limit_bytes=limit * 2**20),
        cost_estimate=pl.CostEstimate(flops=flops, bytes_accessed=size, transcendentals=0),
    )(*args)


def pack(values, tops, sums, out_ref):
    rows = iota((STATS, values.shape[1]), 0)
    stats = jnp.zeros((STATS, values.shape[1]), F32)
    for j in range(2):
        high = sums[j].astype(BF16).astype(F32)
        for row, value in ((j, tops[j]), (2 + 2 * j, high), (3 + 2 * j, sums[j] - high)):
            stats = jnp.where(rows == row, value, stats)
    out_ref[:PAIR] = values.astype(BF16)
    out_ref[PAIR:] = stats.astype(BF16)


def register_kernel(place, own, other, queries, out_ref):
    lanes = pl.ds(pl.multiple_of(place[0] * PAIR, PAIR), PAIR)
    keys = jnp.concatenate([own[0, :, lanes], other[0, :, lanes]], axis=0)
    vals = jnp.concatenate([own[1, :, lanes], other[1, :, lanes]], axis=0)
    scaled = queries[:, lanes] * jnp.asarray(SCALE, BF16)
    first = iota(scaled.shape, 1) < HEAD_DIM
    parts, tops, sums = [], [], []
    for j in range(2):
        mine = jnp.where(first == (j == 0), scaled, jnp.zeros_like(scaled))
        scores = dot(keys, mine, NT)
        top = jnp.max(scores, axis=0, keepdims=True).astype(BF16).astype(F32)
        weights = jnp.exp(scores - top)
        sums.append(jnp.sum(weights, axis=0, keepdims=True))
        tops.append(top)
        parts.append(dot(vals, weights.astype(BF16), TN))
    upper = iota(parts[0].shape, 0) < HEAD_DIM
    pack(jnp.where(upper, parts[0], parts[1]), tops, sums, out_ref)


def merge_kernel(bits, last, place, *refs):
    payloads, out_ref = refs[:-1], refs[-1]
    found = [(r[:PAIR].astype(F32), r[PAIR:].astype(F32)) for r in payloads]
    for level, bit in enumerate(bits):
        swap = place[1 + bit] == 1
        step = 1 << level
        for low in range(len(found)):
            if not low & step:
                a, b = found[low], found[low + step]
                found[low] = tuple(jnp.where(swap, v, u) for u, v in zip(a, b))
                found[low + step] = tuple(jnp.where(swap, u, v) for u, v in zip(a, b))
    upper = iota((PAIR, found[0][0].shape[1]), 0) < HEAD_DIM
    tops, sums, factors = [], [], []
    for j in range(2):
        each = [stats[j : j + 1] for _, stats in found]
        top = functools.reduce(jnp.maximum, each)
        factor = [jnp.exp(e - top) for e in each]
        totals = [
            f * (stats[2 + 2 * j : 3 + 2 * j] + stats[3 + 2 * j : 4 + 2 * j])
            for f, (_, stats) in zip(factor, found)
        ]
        tops.append(top)
        sums.append(functools.reduce(jnp.add, totals))
        factors.append(factor)
    merged = functools.reduce(
        jnp.add,
        [values * jnp.where(upper, f, g) for f, g, (values, _) in zip(*factors, found)],
    )
    if last:
        out_ref[...] = (merged / jnp.where(upper, sums[0], sums[1])).astype(BF16)
    else:
        pack(merged, tops, sums, out_ref)


def segments(rows, cols):
    return (
        (rows * cols, cols, 0, 0),
        (RADIUS * cols, cols, "core", 0),
        (rows * SIDE, SIDE, 0, "a"),
        (rows * SIDE, SIDE, 0, "b"),
        (RADIUS * SIDE, SIDE, "core", "a"),
        (RADIUS * SIDE, SIDE, "core", "b"),
        (RADIUS * cols, cols, "cross", 0),
        (RADIUS * SIDE, SIDE, "cross", "a"),
        (RADIUS * SIDE, SIDE, "cross", "b"),
    )


def mask_kernel(rows, cols, nbits, place, pole, sea, out_ref):
    lat, lon = place[1 + nbits], place[2 + nbits]
    lat_odd, lon_odd = lat % 2, lon % 2
    starts = {
        0: 0,
        "core": jnp.where(lat_odd == 0, rows, -RADIUS),
        "cross": jnp.where(lat_odd == 0, -RADIUS, rows),
        "a": jnp.where(lon_odd == 0, cols, -SIDE),
        "b": jnp.where(lon_odd == 0, -SIDE, cols),
    }
    bands, tiles = sea.shape
    down, across = rows // TILE, cols // TILE
    lane = iota((1, AUG), 1)
    closed = jnp.zeros((1, AUG), F32)
    for i in range(down + 2):
        band = lat * down - 1 + i
        inside = (band >= 0) & (band < bands)
        band = jnp.clip(band, 0, bands - 1)
        for j in range(across + 2):
            tile = (lon * across - 1 + j + tiles) % tiles
            open_ = inside & (pole[band] * sea[band, tile] > 0)
            at = rows + cols + i * (across + 2) + j
            closed = jnp.where(lane == at, jnp.where(open_, 0.0, MASKED), closed)
    offset = 0
    for count, width, down_name, across_name in segments(rows, cols):
        index = iota((count, AUG), 0)
        row = starts[down_name] + index // width
        col = starts[across_name] + index % width
        lanes = iota((count, AUG), 1)
        apart = jnp.where(lanes < rows, lanes - row, lanes - rows - col)
        far = (lanes < rows + cols) & (jnp.abs(apart) > RADIUS)
        cell = ((row + TILE) // TILE) * (across + 2) + (col + TILE) // TILE
        value = jnp.where(lanes - (rows + cols) == cell, closed, 0.0)
        out_ref[offset : offset + count] = jnp.where(far, MASKED, value).astype(BF16)
        offset += count


def near_kernel(rows, cols, nbits, place, q_ref, own, core, a, b, corner, cross, mask, reg_keys,
                acc_ref, scale_ref, reg_ref, kbuf, vbuf):
    cells = mask.shape[0]
    lat = place[1 + nbits]
    taken = pl.ds(pl.multiple_of(jnp.where(lat % 2 == 0, 0, (rows - RADIUS) * cols), 16), RADIUS * cols)
    offset = 0
    for ref, index in ((own, slice(None)), (core, taken), (a, slice(None)), (b, slice(None)),
                       (corner, slice(None)), (cross, slice(None))):
        keys, vals = ref[0, index], ref[1, index]
        end = offset + keys.shape[0]
        for p in range(2):
            kbuf[p, offset:end, :PAIR] = keys[:, p * PAIR : (p + 1) * PAIR]
        vbuf[offset:end] = vals
        offset = end
    for p in range(2):
        kbuf[p, :cells, PAIR:] = mask[...]
        kbuf[p, cells:, :PAIR] = reg_keys[:, p * PAIR : (p + 1) * PAIR]
        kbuf[p, cells:, PAIR:] = jnp.zeros((NREG, AUG), BF16)
    count = rows * cols
    query = iota((count, AUG), 0)
    lane = iota((count, AUG), 1)
    tiles = (rows // TILE + 2) * (cols // TILE + 2)
    hot = (lane == query // cols) | (lane - rows == query % cols)
    hot = hot | ((lane >= rows + cols) & (lane < rows + cols + tiles))
    hot = jnp.where(hot, 1.0, 0.0).astype(BF16)
    first = iota((count, PAIR), 1) < HEAD_DIM
    for p in range(2):
        scaled = q_ref[:, p * PAIR : (p + 1) * PAIR] * jnp.asarray(SCALE, BF16)
        mixed, totals = [], []
        for j in range(2):
            mine = jnp.where(first == (j == 0), scaled, jnp.zeros_like(scaled))
            scores = dot(jnp.concatenate([mine, hot], axis=1), kbuf[p], NT)
            weights = jnp.exp(scores - jnp.max(scores, axis=1, keepdims=True))
            totals.append(jnp.sum(weights, axis=1, keepdims=True))
            rounded = weights.astype(BF16)
            reg_ref[2 * p + j] = rounded[:, cells:]
            mixed.append(
                jnp.dot(rounded[:, :cells], vbuf[:, p * PAIR : (p + 1) * PAIR], preferred_element_type=F32)
            )
        acc_ref[:, p * PAIR : (p + 1) * PAIR] = jnp.where(first, *mixed)
        scale_ref[:, p * PAIR : (p + 1) * PAIR] = 1.0 / jnp.where(first, *totals)


def final_kernel(place, acc, scale, reg_weights, mine, other, out_ref, reg_out_ref):
    here = place[0] == 0
    first = iota((acc.shape[0], PAIR), 1) < HEAD_DIM
    for p in range(2):
        lanes = slice(p * PAIR, (p + 1) * PAIR)
        vals = jnp.where(here == (p == 0), mine[...], other[...])
        added = jnp.where(first, dot(reg_weights[2 * p], vals, NT), dot(reg_weights[2 * p + 1], vals, NT))
        out_ref[:, lanes] = ((acc[:, lanes] + added) * scale[:, lanes]).astype(BF16)
        reg_out_ref[:, lanes] = vals.astype(F32).T.astype(BF16)


def shards(queries, key_values, pole_mask, sea_mask, reg_queries, reg_keys):
    rows, cols, channels = queries.shape
    lats, lons = lax.axis_size("lat"), lax.axis_size("lon")
    devices = lats * lons
    assert lats == 4 and lons & (lons - 1) == 0 and lons > 1
    nbits = devices.bit_length() - 1
    lat, lon = lax.axis_index("lat"), lax.axis_index("lon")
    flat = lon * lats + lat
    bits = [(flat >> b) & 1 for b in range(nbits)]
    half = functools.reduce(jnp.bitwise_xor, bits)
    place = jnp.stack([half, *bits, lat, lon]).astype(jnp.int32)
    everyone = ("lon", "lat")

    def swap(x, mask):
        return lax.ppermute(x, everyone, [(i, i ^ mask) for i in range(devices)])

    cells = rows * cols
    own = key_values.reshape(2, cells, channels)
    core = swap(own, 1)

    near_cols = lax.dynamic_slice_in_dim(key_values, (1 - lon % 2) * (cols - SIDE), SIDE, 2)
    far_cols = lax.dynamic_slice_in_dim(key_values, (lon % 2) * (cols - SIDE), SIDE, 2)
    side_a = swap(near_cols, lats)
    side_b = lax.ppermute(
        far_cols, "lon", [(i, (i + 1 if i % 2 else i - 1) % lons) for i in range(lons)]
    )

    payload = call(
        register_kernel,
        jax.ShapeDtypeStruct((PAIR + STATS, NREG), BF16),
        (place, own, core, reg_queries),
        [SMEM, VMEM, VMEM, VMEM],
        flops=4 * 2 * cells * NREG * 2 * PAIR,
    )

    side_a, side_b, _ = lax.optimization_barrier((side_a, side_b, payload))
    core_first = (1 - lat % 2) * (rows - RADIUS)
    cross_first = (lat % 2) * (rows - RADIUS)

    def edge(shard, start):
        taken = lax.dynamic_slice_in_dim(shard, start, RADIUS, 1)
        return taken.reshape(2, RADIUS * shard.shape[2], channels)

    corner = swap(jnp.concatenate([edge(side_a, core_first), edge(side_b, core_first)], axis=1), 1)
    cross = swap(
        jnp.concatenate(
            [edge(key_values, cross_first), edge(side_a, cross_first), edge(side_b, cross_first)], axis=1
        ),
        3,
    )

    mask = call(
        functools.partial(mask_kernel, rows, cols, nbits),
        jax.ShapeDtypeStruct((sum(s[0] for s in segments(rows, cols)), AUG), BF16),
        (place, pole_mask, sea_mask),
        [SMEM, SMEM, SMEM],
    )

    square = jax.ShapeDtypeStruct((cells, channels), F32)
    acc, scale, reg_weights = call(
        functools.partial(near_kernel, rows, cols, nbits),
        (square, square, jax.ShapeDtypeStruct((HEADS, cells, NREG), BF16)),
        (
            place,
            queries.reshape(cells, channels),
            own,
            core,
            side_a.reshape(2, rows * SIDE, channels),
            side_b.reshape(2, rows * SIDE, channels),
            corner,
            cross,
            mask,
            reg_keys,
        ),
        [SMEM] + [VMEM] * 9,
        scratch=[
            pltpu.VMEM((2, mask.shape[0] + NREG, PAIR + AUG), BF16),
            pltpu.VMEM((mask.shape[0], channels), BF16),
        ],
        flops=2 * 2 * cells * mask.shape[0] * channels * 2,
        limit=32,
    )
    stages = [tuple(range(b, min(b + 2, nbits))) for b in range(1, nbits, 2)]
    for stage in stages:
        gathered = [payload]
        for chosen in range(1, 1 << len(stage)):
            flips = [b for k, b in enumerate(stage) if chosen >> k & 1]
            gathered.append(swap(payload, sum(1 << b for b in flips) + len(flips) % 2))
        last = stage is stages[-1]
        if stage is stages[0]:
            gathered[0], mask = lax.optimization_barrier((gathered[0], mask))
        if last:
            gathered[0], acc, scale, reg_weights = lax.optimization_barrier(
                (gathered[0], acc, scale, reg_weights)
            )
        payload = call(
            functools.partial(merge_kernel, stage, last),
            jax.ShapeDtypeStruct((PAIR if last else PAIR + STATS, NREG), BF16),
            (place, *gathered),
            [SMEM] + [VMEM] * len(gathered),
        )

    other = swap(payload, 1)
    attended, reg_out = call(
        final_kernel,
        (
            jax.ShapeDtypeStruct((cells, channels), BF16),
            jax.ShapeDtypeStruct((NREG, channels), BF16),
        ),
        (place, acc, scale, reg_weights, payload, other),
        [SMEM] + [VMEM] * 5,
        flops=2 * cells * NREG * channels * 2,
    )
    return attended.reshape(rows, cols, channels), reg_out


def solution(mesh):
    return jax.shard_map(
        shards,
        mesh=mesh,
        in_specs=(P("lat", "lon", None), P(None, "lat", "lon", None), P(), P(), P(), P()),
        out_specs=(P("lat", "lon", None), P()),
        check_vma=False,
    )
```

```python
import functools

import jax
import jax.numpy as jnp
from jax import lax
from jax.experimental import pallas as pl
from jax.experimental.pallas import tpu as pltpu
from jax.sharding import PartitionSpec as P

HEADS = 4
HEAD_DIM = 64
NREG = 256
RADIUS = 6
TILE = 8
PAIR = 2 * HEAD_DIM
DEEP = 8
STATS = 16
AUG = 128
MASKED = -8192.0
SCALE = HEAD_DIM ** (-0.5)

BF16 = jnp.bfloat16
F32 = jnp.float32
NT = (((1,), (1,)), ((), ()))
TN = (((0,), (0,)), ((), ()))
VMEM = pl.BlockSpec(memory_space=pltpu.VMEM)
HBM = pl.BlockSpec(memory_space=pltpu.HBM)


def dot(a, b, dims):
    return lax.dot_general(a, b, dims, preferred_element_type=F32)


def place():
    count = lax.axis_size("lon") * lax.axis_size("lat")
    flat = lax.axis_index("lon") * lax.axis_size("lat") + lax.axis_index("lat")
    return [(flat >> b) & 1 for b in range(count.bit_length() - 1)]


def half():
    return functools.reduce(jnp.bitwise_xor, place())


def iota(shape, axis):
    return lax.broadcasted_iota(jnp.int32, shape, axis)


def call(kernel, out, args, specs, scratch=(), flops=0, limit=16):
    size = sum(a.size * a.dtype.itemsize for a in args)
    return pl.pallas_call(
        kernel,
        out_shape=out,
        in_specs=specs,
        out_specs=jax.tree.map(lambda _: VMEM, out),
        scratch_shapes=scratch,
        compiler_params=pltpu.CompilerParams(vmem_limit_bytes=limit * 2**20),
        cost_estimate=pl.CostEstimate(flops=flops, bytes_accessed=size, transcendentals=0),
    )(*args)


def pack(values, tops, sums, out_ref):
    rows = iota((STATS, values.shape[1]), 0)
    stats = jnp.zeros((STATS, values.shape[1]), F32)
    for j in range(2):
        high = sums[j].astype(BF16).astype(F32)
        for row, value in ((j, tops[j]), (2 + 2 * j, high), (3 + 2 * j, sums[j] - high)):
            stats = jnp.where(rows == row, value, stats)
    out_ref[:PAIR] = values.astype(BF16)
    out_ref[PAIR:] = stats.astype(BF16)


def sides_kernel(rows, cols, kv_ref, queries_ref, own, queries, near_ref, far_ref, wide, sem):
    copies = [
        pltpu.make_async_copy(kv_ref, own, sem.at[0]),
        pltpu.make_async_copy(queries_ref, queries, sem.at[1]),
    ]
    for copy in copies:
        copy.start()
    copies[0].wait()
    odd = lax.axis_index("lon") % 2 == 1
    for k in range(2):
        for lane in range(0, own.shape[2], 128):
            lanes = slice(lane, lane + 128)
            wide[...] = own[k, :, lanes].astype(F32)
            for c in range(RADIUS):
                low = wide[pl.ds(c, rows, stride=cols)]
                high = wide[pl.ds(cols - RADIUS + c, rows, stride=cols)]
                near_ref[k, c * rows : (c + 1) * rows, lanes] = jnp.where(odd, low, high).astype(BF16)
                far_ref[k, c * rows : (c + 1) * rows, lanes] = jnp.where(odd, high, low).astype(BF16)
    copies[1].wait()


def register_kernel(own, other, queries, out_ref):
    lanes = pl.ds(pl.multiple_of(half() * PAIR, PAIR), PAIR)
    keys = jnp.concatenate([own[0, :, lanes], other[0, :, lanes]], axis=0)
    vals = jnp.concatenate([own[1, :, lanes], other[1, :, lanes]], axis=0)
    scaled = queries[:, lanes] * jnp.asarray(SCALE, BF16)
    first = iota(scaled.shape, 1) < HEAD_DIM
    parts, tops, sums = [], [], []
    for j in range(2):
        mine = jnp.where(first == (j == 0), scaled, jnp.zeros_like(scaled))
        scores = dot(keys, mine, NT)
        top = jnp.max(scores, axis=0, keepdims=True).astype(BF16).astype(F32)
        weights = jnp.exp(scores - top)
        sums.append(jnp.sum(weights, axis=0, keepdims=True))
        tops.append(top)
        parts.append(dot(vals, weights.astype(BF16), TN))
    upper = iota(parts[0].shape, 0) < HEAD_DIM
    pack(jnp.where(upper, parts[0], parts[1]), tops, sums, out_ref)


def merge_kernel(bits, last, *refs):
    payloads, out_ref = refs[:-1], refs[-1]
    here = place()
    found = [(r[:PAIR].astype(F32), r[PAIR:].astype(F32)) for r in payloads]
    for level, bit in enumerate(bits):
        swap = here[bit] == 1
        step = 1 << level
        for low in range(len(found)):
            if not low & step:
                a, b = found[low], found[low + step]
                found[low] = tuple(jnp.where(swap, v, u) for u, v in zip(a, b))
                found[low + step] = tuple(jnp.where(swap, u, v) for u, v in zip(a, b))
    upper = iota((PAIR, found[0][0].shape[1]), 0) < HEAD_DIM
    tops, sums, factors = [], [], []
    for j in range(2):
        each = [stats[j : j + 1] for _, stats in found]
        top = functools.reduce(jnp.maximum, each)
        factor = [jnp.exp(e - top) for e in each]
        totals = [
            f * (stats[2 + 2 * j : 3 + 2 * j] + stats[3 + 2 * j : 4 + 2 * j])
            for f, (_, stats) in zip(factor, found)
        ]
        tops.append(top)
        sums.append(functools.reduce(jnp.add, totals))
        factors.append(factor)
    merged = functools.reduce(
        jnp.add,
        [values * jnp.where(upper, f, g) for f, g, (values, _) in zip(*factors, found)],
    )
    if last:
        out_ref[...] = (merged / jnp.where(upper, sums[0], sums[1])).astype(BF16)
    else:
        pack(merged, tops, sums, out_ref)


def segments(rows, cols):
    return (
        (rows, cols, False, 0, 0),
        (RADIUS, cols, False, "core", 0),
        (RADIUS, rows, True, 0, "a"),
        (RADIUS, rows, True, 0, "b"),
        (RADIUS, DEEP, True, "core deep", "a"),
        (RADIUS, DEEP, True, "core deep", "b"),
        (RADIUS, cols, False, "cross", 0),
        (RADIUS, DEEP, True, "cross deep", "a"),
        (RADIUS, DEEP, True, "cross deep", "b"),
    )


def closed_tiles(rows, cols, pole, sea):
    lat, lon = lax.axis_index("lat"), lax.axis_index("lon")
    bands, tiles = sea.shape
    down, across = rows // TILE, cols // TILE
    lane = iota((1, AUG), 1)
    closed = jnp.zeros((1, AUG), F32)
    for i in range(down + 2):
        band = lat * down - 1 + i
        inside = (band >= 0) & (band < bands)
        band = jnp.clip(band, 0, bands - 1)
        for j in range(across + 2):
            tile = (lon * across - 1 + j + tiles) % tiles
            kept = inside & (pole[band] * sea[band, tile] > 0)
            at = rows + cols + i * (across + 2) + j
            closed = jnp.where(lane == at, jnp.where(kept, 0.0, MASKED), closed)
    return closed


def masks(rows, cols, closed):
    lat, lon = lax.axis_index("lat"), lax.axis_index("lon")
    across = cols // TILE
    lat_odd, lon_odd = lat % 2 == 1, lon % 2 == 1
    starts = {
        0: 0,
        "core": jnp.where(lat_odd, -RADIUS, rows),
        "core deep": jnp.where(lat_odd, -DEEP, rows),
        "cross": jnp.where(lat_odd, rows, -RADIUS),
        "cross deep": jnp.where(lat_odd, rows, -DEEP),
        "a": jnp.where(lon_odd, -RADIUS, cols),
        "b": jnp.where(lon_odd, cols, -RADIUS),
    }
    lane = iota((1, AUG), 1)
    for slow, fast, fast_rows, row, col in segments(rows, cols):
        index = iota((slow * fast, AUG), 0)
        outer, inner = index >> (fast.bit_length() - 1), index & (fast - 1)
        row = starts[row] + (inner if fast_rows else outer)
        col = starts[col] + (outer if fast_rows else inner)
        apart = jnp.where(lane < rows, lane - row, lane - rows - col)
        far = (lane < rows + cols) & (jnp.abs(apart) > RADIUS)
        cell = ((row + TILE) >> 3) * (across + 2) + ((col + TILE) >> 3)
        value = jnp.where(lane - (rows + cols) == cell, closed, 0.0)
        yield jnp.where(far, MASKED, value).astype(BF16)


def near_kernel(rows, cols, q_ref, own, core, a, b, corner, cross, reg_keys, pole_ref, sea_ref,
                acc_ref, scale_ref, reg_ref, kbuf, vbuf, pole, sea, sem):
    copies = [
        pltpu.make_async_copy(pole_ref, pole, sem.at[0]),
        pltpu.make_async_copy(sea_ref, sea, sem.at[1]),
    ]
    for copy in copies:
        copy.start()
    cells = vbuf.shape[0]
    lat = lax.axis_index("lat")
    taken = pl.ds(pl.multiple_of(jnp.where(lat % 2 == 0, 0, (rows - RADIUS) * cols), 16), RADIUS * cols)
    offset = 0
    for ref, index in ((own, slice(None)), (core, taken), (a, slice(None)), (b, slice(None)),
                       (corner, slice(None)), (cross, slice(None))):
        keys, vals = ref[0, index], ref[1, index]
        end = offset + keys.shape[0]
        for p in range(2):
            kbuf[p, offset:end, :PAIR] = keys[:, p * PAIR : (p + 1) * PAIR]
        vbuf[offset:end] = vals
        offset = end
    for p in range(2):
        kbuf[p, cells:, :PAIR] = reg_keys[:, p * PAIR : (p + 1) * PAIR]
        kbuf[p, cells:, PAIR:] = jnp.zeros((NREG, AUG), BF16)
    for copy in copies:
        copy.wait()
    offset = 0
    for mask in masks(rows, cols, closed_tiles(rows, cols, pole, sea)):
        for p in range(2):
            kbuf[p, offset : offset + mask.shape[0], PAIR:] = mask
        offset += mask.shape[0]
    count = rows * cols
    query = iota((count, AUG), 0)
    lane = iota((count, AUG), 1)
    tiles = (rows // TILE + 2) * (cols // TILE + 2)
    hot = (lane == query >> (cols.bit_length() - 1)) | (lane - rows == query & (cols - 1))
    hot = hot | ((lane >= rows + cols) & (lane < rows + cols + tiles))
    hot = jnp.where(hot, 1.0, 0.0).astype(BF16)
    first = iota((count, PAIR), 1) < HEAD_DIM
    for p in range(2):
        scaled = q_ref[:, p * PAIR : (p + 1) * PAIR] * jnp.asarray(SCALE, BF16)
        mixed, totals = [], []
        for j in range(2):
            mine = jnp.where(first == (j == 0), scaled, jnp.zeros_like(scaled))
            scores = dot(jnp.concatenate([mine, hot], axis=1), kbuf[p], NT)
            weights = jnp.exp(scores - jnp.max(scores, axis=1, keepdims=True))
            totals.append(jnp.sum(weights, axis=1, keepdims=True))
            rounded = weights.astype(BF16)
            reg_ref[2 * p + j] = rounded[:, cells:]
            mixed.append(
                jnp.dot(rounded[:, :cells], vbuf[:, p * PAIR : (p + 1) * PAIR], preferred_element_type=F32)
            )
        acc_ref[:, p * PAIR : (p + 1) * PAIR] = jnp.where(first, *mixed)
        scale_ref[:, p * PAIR : (p + 1) * PAIR] = 1.0 / jnp.where(first, *totals)


def final_kernel(acc, scale, reg_weights, mine, other, out_ref, reg_out_ref):
    here = half() == 0
    first = iota((acc.shape[0], PAIR), 1) < HEAD_DIM
    for p in range(2):
        lanes = slice(p * PAIR, (p + 1) * PAIR)
        vals = jnp.where(here == (p == 0), mine[...], other[...])
        added = jnp.where(first, dot(reg_weights[2 * p], vals, NT), dot(reg_weights[2 * p + 1], vals, NT))
        out_ref[:, lanes] = ((acc[:, lanes] + added) * scale[:, lanes]).astype(BF16)
        reg_out_ref[:, lanes] = vals.astype(F32).T.astype(BF16)


def shards(queries, key_values, pole_mask, sea_mask, reg_queries, reg_keys):
    rows, cols, channels = queries.shape
    lats, lons = lax.axis_size("lat"), lax.axis_size("lon")
    devices = lats * lons
    assert lats == 4 and lons & (lons - 1) == 0 and lons > 1
    assert rows & (rows - 1) == 0 and cols & (cols - 1) == 0 and rows % TILE == 0 and cols % TILE == 0 and TILE == DEEP == 8
    nbits = devices.bit_length() - 1
    lat = lax.axis_index("lat")
    everyone = ("lon", "lat")

    def swap(x, mask):
        return lax.ppermute(x, everyone, [(i, i ^ mask) for i in range(devices)])

    cells = rows * cols
    key_values = key_values.reshape(2, cells, channels)
    core = swap(key_values, 1)

    side = jax.ShapeDtypeStruct((2, RADIUS * rows, channels), BF16)
    own, reg_queries, near_cols, far_cols = call(
        functools.partial(sides_kernel, rows, cols),
        (jax.ShapeDtypeStruct(key_values.shape, BF16), jax.ShapeDtypeStruct(reg_queries.shape, BF16), side, side),
        tuple(pltpu.with_memory_space_constraint(x, pltpu.HBM) for x in (key_values, reg_queries)),
        [HBM] * 2,
        scratch=[pltpu.VMEM((cells, 128), F32), pltpu.SemaphoreType.DMA((2,))],
    )
    side_a = swap(near_cols, lats)
    side_b = lax.ppermute(
        far_cols, "lon", [(i, (i + 1 if i % 2 else i - 1) % lons) for i in range(lons)]
    )

    payload = call(
        register_kernel,
        jax.ShapeDtypeStruct((PAIR + STATS, NREG), BF16),
        (own, core, reg_queries),
        [VMEM] * 3,
        flops=4 * 2 * cells * NREG * 2 * PAIR,
    )

    side_a, side_b, _ = lax.optimization_barrier((side_a, side_b, payload))
    def take(shard, size, start, count):
        taken = lax.dynamic_slice_in_dim(shard.reshape(2, -1, size, channels), start, count, 2)
        return taken.reshape(2, -1, channels)

    core_deep, cross_deep = (1 - lat % 2) * (rows - DEEP), (lat % 2) * (rows - DEEP)
    corner = swap(
        jnp.concatenate([take(s, rows, core_deep, DEEP) for s in (side_a, side_b)], axis=1), 1
    )
    cross = swap(
        jnp.concatenate(
            [
                take(own, cells, (lat % 2) * (rows - RADIUS) * cols, RADIUS * cols),
                *[take(s, rows, cross_deep, DEEP) for s in (side_a, side_b)],
            ],
            axis=1,
        ),
        3,
    )
    keys = sum(segment[0] * segment[1] for segment in segments(rows, cols))
    square = jax.ShapeDtypeStruct((cells, channels), F32)
    acc, scale, reg_weights = call(
        functools.partial(near_kernel, rows, cols),
        (square, square, jax.ShapeDtypeStruct((HEADS, cells, NREG), BF16)),
        (
            queries.reshape(cells, channels),
            own,
            core,
            side_a,
            side_b,
            corner,
            cross,
            reg_keys,
            pole_mask,
            sea_mask,
        ),
        [VMEM] * 8 + [HBM] * 2,
        scratch=[
            pltpu.VMEM((2, keys + NREG, PAIR + AUG), BF16),
            pltpu.VMEM((keys, channels), BF16),
            pltpu.SMEM(pole_mask.shape, jnp.int32),
            pltpu.SMEM(sea_mask.shape, jnp.int32),
            pltpu.SemaphoreType.DMA((2,)),
        ],
        flops=2 * 2 * cells * keys * channels * 2,
        limit=32,
    )
    stages = [tuple(range(b, min(b + 2, nbits))) for b in range(1, nbits, 2)]
    for stage in stages:
        gathered = [payload]
        for chosen in range(1, 1 << len(stage)):
            flips = [b for k, b in enumerate(stage) if chosen >> k & 1]
            gathered.append(swap(payload, sum(1 << b for b in flips) + len(flips) % 2))
        last = stage is stages[-1]
        if last:
            gathered[0], acc, scale, reg_weights = lax.optimization_barrier(
                (gathered[0], acc, scale, reg_weights)
            )
        payload = call(
            functools.partial(merge_kernel, stage, last),
            jax.ShapeDtypeStruct((PAIR if last else PAIR + STATS, NREG), BF16),
            tuple(gathered),
            [VMEM] * len(gathered),
        )

    other = swap(payload, 1)
    attended, reg_out = call(
        final_kernel,
        (
            jax.ShapeDtypeStruct((cells, channels), BF16),
            jax.ShapeDtypeStruct((NREG, channels), BF16),
        ),
        (acc, scale, reg_weights, payload, other),
        [VMEM] * 5,
        flops=2 * cells * NREG * channels * 2,
    )
    return attended.reshape(rows, cols, channels), reg_out


def solution(mesh):
    return jax.shard_map(
        shards,
        mesh=mesh,
        in_specs=(P("lat", "lon", None), P(None, "lat", "lon", None), P(), P(), P(), P()),
        out_specs=(P("lat", "lon", None), P()),
        check_vma=False,
    )
```

```python
import functools

import jax
import jax.numpy as jnp
from jax import lax
from jax.experimental import pallas as pl
from jax.experimental.pallas import tpu as pltpu
from jax.sharding import PartitionSpec as P

HEADS = 4
HEAD_DIM = 64
NREG = 256
RADIUS = 6
TILE = 8
PAIR = 2 * HEAD_DIM
DEEP = 8
STATS = 16
AUG = 128
MASKED = -8192.0
SCALE = HEAD_DIM ** (-0.5)

BF16 = jnp.bfloat16
F32 = jnp.float32
NT = (((1,), (1,)), ((), ()))
TN = (((0,), (0,)), ((), ()))
VMEM = pl.BlockSpec(memory_space=pltpu.VMEM)
HBM = pl.BlockSpec(memory_space=pltpu.HBM)


def dot(a, b, dims):
    return lax.dot_general(a, b, dims, preferred_element_type=F32)


def place():
    count = lax.axis_size("lon") * lax.axis_size("lat")
    flat = lax.axis_index("lon") * lax.axis_size("lat") + lax.axis_index("lat")
    return [(flat >> b) & 1 for b in range(count.bit_length() - 1)]


def half():
    return functools.reduce(jnp.bitwise_xor, place())


def iota(shape, axis):
    return lax.broadcasted_iota(jnp.int32, shape, axis)


def call(kernel, out, args, specs, scratch=(), flops=0, limit=16):
    size = sum(a.size * a.dtype.itemsize for a in args)
    return pl.pallas_call(
        kernel,
        out_shape=out,
        in_specs=specs,
        out_specs=jax.tree.map(lambda _: VMEM, out),
        scratch_shapes=scratch,
        compiler_params=pltpu.CompilerParams(vmem_limit_bytes=limit * 2**20),
        cost_estimate=pl.CostEstimate(flops=flops, bytes_accessed=size, transcendentals=0),
    )(*args)


def pack(values, tops, sums):
    rows = iota((STATS, values.shape[1]), 0)
    stats = jnp.zeros((STATS, values.shape[1]), F32)
    for j in range(2):
        high = sums[j].astype(BF16).astype(F32)
        for row, value in ((j, tops[j]), (2 + 2 * j, high), (3 + 2 * j, sums[j] - high)):
            stats = jnp.where(rows == row, value, stats)
    return jnp.concatenate([values, stats], axis=0)


def sides_kernel(rows, cols, kv_ref, queries_ref, pole_ref, sea_ref, own, queries, near_ref, far_ref, closed_ref,
                 wide, pole, sea, sem):
    pairs = ((pole_ref, pole), (sea_ref, sea), (kv_ref, own), (queries_ref, queries))
    copies = [pltpu.make_async_copy(*pair, sem.at[k]) for k, pair in enumerate(pairs)]
    for copy in copies:
        copy.start()
    copies[0].wait()
    copies[1].wait()
    closed_ref[...] = jnp.broadcast_to(closed_tiles(rows, cols, pole, sea), closed_ref.shape)
    copies[2].wait()
    odd = lax.axis_index("lon") % 2 == 1
    for k in range(2):
        for lane in range(0, own.shape[2], 128):
            lanes = slice(lane, lane + 128)
            wide[...] = own[k, :, lanes].astype(F32)
            for c in range(RADIUS):
                low = wide[pl.ds(c, rows, stride=cols)]
                high = wide[pl.ds(cols - RADIUS + c, rows, stride=cols)]
                near_ref[k, c * rows : (c + 1) * rows, lanes] = jnp.where(odd, low, high).astype(BF16)
                far_ref[k, c * rows : (c + 1) * rows, lanes] = jnp.where(odd, high, low).astype(BF16)
    copies[3].wait()


def register_kernel(own, other, queries, out_ref):
    lanes = pl.ds(pl.multiple_of(half() * PAIR, PAIR), PAIR)
    keys = jnp.concatenate([own[0, :, lanes], other[0, :, lanes]], axis=0)
    vals = jnp.concatenate([own[1, :, lanes], other[1, :, lanes]], axis=0)
    scaled = queries[:, lanes] * jnp.asarray(SCALE, BF16)
    first = iota(scaled.shape, 1) < HEAD_DIM
    parts, tops, sums = [], [], []
    for j in range(2):
        mine = jnp.where(first == (j == 0), scaled, jnp.zeros_like(scaled))
        scores = dot(keys, mine, NT)
        top = jnp.max(scores, axis=0, keepdims=True).astype(BF16).astype(F32)
        weights = jnp.exp(scores - top)
        sums.append(jnp.sum(weights, axis=0, keepdims=True))
        tops.append(top)
        parts.append(dot(vals, weights.astype(BF16), TN))
    upper = iota(parts[0].shape, 0) < HEAD_DIM
    out_ref[...] = pack(jnp.where(upper, parts[0], parts[1]), tops, sums).astype(BF16)


def merge_kernel(bits, last, *refs):
    payloads, out_ref = refs[:-1], refs[-1]
    here = place()
    found = [(r[:PAIR].astype(F32), r[PAIR:].astype(F32)) for r in payloads]
    for level, bit in enumerate(bits):
        swap = here[bit] == 1
        step = 1 << level
        for low in range(len(found)):
            if not low & step:
                a, b = found[low], found[low + step]
                found[low] = tuple(jnp.where(swap, v, u) for u, v in zip(a, b))
                found[low + step] = tuple(jnp.where(swap, u, v) for u, v in zip(a, b))
    upper = iota((PAIR, found[0][0].shape[1]), 0) < HEAD_DIM
    tops, sums, factors = [], [], []
    for j in range(2):
        each = [stats[j : j + 1] for _, stats in found]
        top = functools.reduce(jnp.maximum, each)
        factor = [jnp.exp(e - top) for e in each]
        totals = [
            f * (stats[2 + 2 * j : 3 + 2 * j] + stats[3 + 2 * j : 4 + 2 * j])
            for f, (_, stats) in zip(factor, found)
        ]
        tops.append(top)
        sums.append(functools.reduce(jnp.add, totals))
        factors.append(factor)
    merged = functools.reduce(
        jnp.add,
        [values * jnp.where(upper, f, g) for f, g, (values, _) in zip(*factors, found)],
    )
    if last:
        out_ref[...] = (merged / jnp.where(upper, sums[0], sums[1])).astype(BF16)
    else:
        out_ref[...] = pack(merged, tops, sums).astype(BF16)


def segments(rows, cols):
    inner = (
        (rows, cols, False, 0, 0),
        (RADIUS, cols, False, "core", 0),
    )
    outer = (
        (RADIUS, rows, True, 0, "a"),
        (RADIUS, rows, True, 0, "b"),
        (RADIUS, DEEP, True, "core deep", "a"),
        (RADIUS, DEEP, True, "core deep", "b"),
        (RADIUS, cols, False, "cross", 0),
        (RADIUS, DEEP, True, "cross deep", "a"),
        (RADIUS, DEEP, True, "cross deep", "b"),
    )
    return inner, outer


def count(parts):
    return sum(part[0] * part[1] for part in parts)


def closed_tiles(rows, cols, pole, sea):
    lat, lon = lax.axis_index("lat"), lax.axis_index("lon")
    bands, tiles = sea.shape
    down, across = rows // TILE, cols // TILE
    lane = iota((1, AUG), 1)
    closed = jnp.zeros((1, AUG), F32)
    for i in range(down + 2):
        band = lat * down - 1 + i
        inside = (band >= 0) & (band < bands)
        band = jnp.clip(band, 0, bands - 1)
        for j in range(across + 2):
            tile = (lon * across - 1 + j + tiles) % tiles
            kept = inside & (pole[band] * sea[band, tile] > 0)
            at = rows + cols + i * (across + 2) + j
            closed = jnp.where(lane == at, jnp.where(kept, 0.0, MASKED), closed)
    return closed


def masks(rows, cols, closed, parts):
    lat, lon = lax.axis_index("lat"), lax.axis_index("lon")
    across = cols // TILE
    lat_odd, lon_odd = lat % 2 == 1, lon % 2 == 1
    starts = {
        0: 0,
        "core": jnp.where(lat_odd, -RADIUS, rows),
        "core deep": jnp.where(lat_odd, -DEEP, rows),
        "cross": jnp.where(lat_odd, rows, -RADIUS),
        "cross deep": jnp.where(lat_odd, rows, -DEEP),
        "a": jnp.where(lon_odd, -RADIUS, cols),
        "b": jnp.where(lon_odd, cols, -RADIUS),
    }
    lane = iota((1, AUG), 1)
    for slow, fast, fast_rows, row, col in parts:
        index = iota((slow * fast, AUG), 0)
        outer, inner = index >> (fast.bit_length() - 1), index & (fast - 1)
        row = starts[row] + (inner if fast_rows else outer)
        col = starts[col] + (outer if fast_rows else inner)
        apart = jnp.where(lane < rows, lane - row, lane - rows - col)
        far = (lane < rows + cols) & (jnp.abs(apart) > RADIUS)
        cell = ((row + TILE) >> 3) * (across + 2) + ((col + TILE) >> 3)
        value = jnp.where(lane - (rows + cols) == cell, closed, 0.0)
        yield jnp.where(far, MASKED, value).astype(BF16)


def fill(kbuf, vbuf, blocks, mask_blocks):
    ahead = kbuf.shape[1] - vbuf.shape[0]
    offset = 0
    for keys, vals in blocks:
        end = offset + keys.shape[0]
        for p in range(2):
            kbuf[p, ahead + offset : ahead + end, :PAIR] = keys[:, p * PAIR : (p + 1) * PAIR]
        vbuf[offset:end] = vals
        offset = end
    offset = ahead
    for mask in mask_blocks:
        for p in range(2):
            kbuf[p, offset : offset + mask.shape[0], PAIR:] = mask
        offset += mask.shape[0]


def attend(rows, cols, q_ref, kbuf, vbuf):
    size, ahead = rows * cols, kbuf.shape[1] - vbuf.shape[0]
    query = iota((size, AUG), 0)
    lane = iota((size, AUG), 1)
    tiles = (rows // TILE + 2) * (cols // TILE + 2)
    hot = (lane == query >> (cols.bit_length() - 1)) | (lane - rows == query & (cols - 1))
    hot = hot | ((lane >= rows + cols) & (lane < rows + cols + tiles))
    hot = jnp.where(hot, 1.0, 0.0).astype(BF16)
    first = iota((size, PAIR), 1) < HEAD_DIM
    for p in range(2):
        lanes = slice(p * PAIR, (p + 1) * PAIR)
        scaled = q_ref[:, lanes] * jnp.asarray(SCALE, BF16)
        tops, totals, mixed, weights = [], [], [], []
        for j in range(2):
            mine = jnp.where(first == (j == 0), scaled, jnp.zeros_like(scaled))
            scores = dot(jnp.concatenate([mine, hot], axis=1), kbuf[p], NT)
            tops.append(jnp.max(scores, axis=1, keepdims=True))
            each = jnp.exp(scores - tops[j])
            totals.append(jnp.sum(each, axis=1, keepdims=True))
            weights.append(each.astype(BF16))
            mixed.append(jnp.dot(weights[j][:, ahead:], vbuf[:, lanes], preferred_element_type=F32))
        yield p, lanes, *(jnp.where(first, *x) for x in (tops, totals, mixed)), weights


def inner_kernel(rows, cols, q_ref, own, core, reg_keys, closed_ref,
                 mixed_ref, top_ref, total_ref, reg_ref, kbuf, vbuf):
    first = jnp.where(lax.axis_index("lat") % 2 == 0, 0, (rows - RADIUS) * cols)
    taken = pl.ds(pl.multiple_of(first, 16), RADIUS * cols)
    blocks = [(own[0], own[1]), (core[0, taken], core[1, taken])]
    fill(kbuf, vbuf, blocks, masks(rows, cols, closed_ref[:1], segments(rows, cols)[0]))
    for p in range(2):
        kbuf[p, :NREG, :PAIR] = reg_keys[:, p * PAIR : (p + 1) * PAIR]
        kbuf[p, :NREG, PAIR:] = jnp.zeros((NREG, AUG), BF16)
    for p, lanes, top, total, mixed, weights in attend(rows, cols, q_ref, kbuf, vbuf):
        top_ref[:, lanes], total_ref[:, lanes], mixed_ref[:, lanes] = top, total, mixed
        for j in range(2):
            reg_ref[2 * p + j] = weights[j][:, :NREG]


def outer_kernel(rows, cols, q_ref, a, b, corner, cross, inner_top, inner_total, closed_ref,
                 rest_ref, factor_ref, kbuf, vbuf):
    blocks = [(ref[0], ref[1]) for ref in (a, b, corner, cross)]
    fill(kbuf, vbuf, blocks, masks(rows, cols, closed_ref[:1], segments(rows, cols)[1]))
    for _, lanes, top, total, mixed, _ in attend(rows, cols, q_ref, kbuf, vbuf):
        highest = jnp.maximum(top, inner_top[:, lanes])
        inner, outer = jnp.exp(inner_top[:, lanes] - highest), jnp.exp(top - highest)
        scale = 1.0 / (inner * inner_total[:, lanes] + outer * total)
        factor_ref[:, lanes] = inner * scale
        rest_ref[:, lanes] = mixed * (outer * scale)


def final_kernel(inner, factor, rest, reg_weights, mine, other, out_ref, reg_out_ref):
    here = half() == 0
    first = iota((inner.shape[0], PAIR), 1) < HEAD_DIM
    for p in range(2):
        lanes = slice(p * PAIR, (p + 1) * PAIR)
        vals = jnp.where(here == (p == 0), mine[...], other[...])
        added = jnp.where(first, dot(reg_weights[2 * p], vals, NT), dot(reg_weights[2 * p + 1], vals, NT))
        out_ref[:, lanes] = ((inner[:, lanes] + added) * factor[:, lanes] + rest[:, lanes]).astype(BF16)
        reg_out_ref[:, lanes] = vals.astype(F32).T.astype(BF16)


def shards(queries, key_values, pole_mask, sea_mask, reg_queries, reg_keys):
    rows, cols, channels = queries.shape
    lats, lons = lax.axis_size("lat"), lax.axis_size("lon")
    devices = lats * lons
    assert lats == 4 and lons & (lons - 1) == 0 and lons > 1
    assert rows & (rows - 1) == 0 and cols & (cols - 1) == 0 and rows % TILE == 0 and cols % TILE == 0 and TILE == DEEP == 8
    nbits = devices.bit_length() - 1
    lat = lax.axis_index("lat")
    everyone = ("lon", "lat")

    def swap(x, mask):
        return lax.ppermute(x, everyone, [(i, i ^ mask) for i in range(devices)])

    cells = rows * cols
    key_values = key_values.reshape(2, cells, channels)
    core = swap(key_values, 1)

    side = jax.ShapeDtypeStruct((2, RADIUS * rows, channels), BF16)
    inputs = (key_values, reg_queries, pole_mask, sea_mask)
    own, reg_queries, near_cols, far_cols, closed = call(
        functools.partial(sides_kernel, rows, cols),
        (
            jax.ShapeDtypeStruct(key_values.shape, BF16),
            jax.ShapeDtypeStruct(reg_queries.shape, BF16),
            side,
            side,
            jax.ShapeDtypeStruct((8, AUG), F32),
        ),
        tuple(pltpu.with_memory_space_constraint(x, pltpu.HBM) for x in inputs),
        [HBM] * 4,
        scratch=[
            pltpu.VMEM((cells, 128), F32),
            pltpu.SMEM(pole_mask.shape, jnp.int32),
            pltpu.SMEM(sea_mask.shape, jnp.int32),
            pltpu.SemaphoreType.DMA((4,)),
        ],
    )
    side_a = swap(near_cols, lats)
    side_b = lax.ppermute(
        far_cols, "lon", [(i, (i + 1 if i % 2 else i - 1) % lons) for i in range(lons)]
    )

    payload = call(
        register_kernel,
        jax.ShapeDtypeStruct((PAIR + STATS, NREG), BF16),
        (own, core, reg_queries),
        [VMEM] * 3,
        flops=4 * 2 * cells * NREG * 2 * PAIR,
    )

    queries = queries.reshape(cells, channels)
    square = jax.ShapeDtypeStruct((cells, channels), F32)
    inner, outer = (count(parts) for parts in segments(rows, cols))
    mixed, top, total, reg_weights = call(
        functools.partial(inner_kernel, rows, cols),
        (square, square, square, jax.ShapeDtypeStruct((HEADS, cells, NREG), BF16)),
        (queries, own, core, reg_keys, closed),
        [VMEM] * 5,
        scratch=[
            pltpu.VMEM((2, inner + NREG, PAIR + AUG), BF16),
            pltpu.VMEM((inner, channels), BF16),
        ],
        flops=2 * 2 * cells * inner * channels * 2,
    )

    side_a, side_b, _ = lax.optimization_barrier((side_a, side_b, payload))

    def take(shard, size, start, count):
        taken = lax.dynamic_slice_in_dim(shard.reshape(2, -1, size, channels), start, count, 2)
        return taken.reshape(2, -1, channels)

    core_deep, cross_deep = (1 - lat % 2) * (rows - DEEP), (lat % 2) * (rows - DEEP)
    corner = swap(
        jnp.concatenate([take(s, rows, core_deep, DEEP) for s in (side_a, side_b)], axis=1), 1
    )
    cross = swap(
        jnp.concatenate(
            [
                take(own, cells, (lat % 2) * (rows - RADIUS) * cols, RADIUS * cols),
                *[take(s, rows, cross_deep, DEEP) for s in (side_a, side_b)],
            ],
            axis=1,
        ),
        3,
    )
    rest, factor = call(
        functools.partial(outer_kernel, rows, cols),
        (square, square),
        (queries, side_a, side_b, corner, cross, top, total, closed),
        [VMEM] * 8,
        scratch=[pltpu.VMEM((2, outer, PAIR + AUG), BF16), pltpu.VMEM((outer, channels), BF16)],
        flops=2 * 2 * cells * outer * channels * 2,
    )

    stages = [tuple(range(b, min(b + 2, nbits))) for b in range(3, nbits, 2)] + [(1, 2)]
    for stage in stages:
        first, last = stage is stages[0], stage is stages[-1]
        gathered = [payload]
        for chosen in range(1, 1 << len(stage)):
            flips = [b for k, b in enumerate(stage) if chosen >> k & 1]
            gathered.append(swap(payload, sum(1 << b for b in flips) + len(flips) % 2))
        if first:
            gathered[0], _ = lax.optimization_barrier((gathered[0], mixed))
        if last:
            gathered[0], rest, factor = lax.optimization_barrier((gathered[0], rest, factor))
        payload = call(
            functools.partial(merge_kernel, stage, last),
            jax.ShapeDtypeStruct((PAIR if last else PAIR + STATS, NREG), BF16),
            tuple(gathered),
            [VMEM] * len(gathered),
        )

    attended, reg_out = call(
        final_kernel,
        (
            jax.ShapeDtypeStruct((cells, channels), BF16),
            jax.ShapeDtypeStruct((NREG, channels), BF16),
        ),
        (mixed, factor, rest, reg_weights, payload, swap(payload, 1)),
        [VMEM] * 6,
        flops=2 * cells * NREG * channels * 2,
    )
    return attended.reshape(rows, cols, channels), reg_out


def solution(mesh):
    return jax.shard_map(
        shards,
        mesh=mesh,
        in_specs=(P("lat", "lon", None), P(None, "lat", "lon", None), P(), P(), P(), P()),
        out_specs=(P("lat", "lon", None), P()),
        check_vma=False,
    )
```

```python
import functools

import jax
import jax.numpy as jnp
from jax import lax
from jax.experimental import pallas as pl
from jax.experimental.pallas import tpu as pltpu
from jax.sharding import PartitionSpec as P

HEADS = 4
HEAD_DIM = 64
NREG = 256
RADIUS = 6
TILE = 8
PAIR = 2 * HEAD_DIM
DEEP = 8
STATS = 8
AUG = 128
MASKED = -8192.0
SCALE = HEAD_DIM ** (-0.5)

BF16 = jnp.bfloat16
F32 = jnp.float32
NT = (((1,), (1,)), ((), ()))
TN = (((0,), (0,)), ((), ()))
VMEM = pl.BlockSpec(memory_space=pltpu.VMEM)
HBM = pl.BlockSpec(memory_space=pltpu.HBM)


def dot(a, b, dims):
    return lax.dot_general(a, b, dims, preferred_element_type=F32)


def place():
    count = lax.axis_size("lon") * lax.axis_size("lat")
    flat = lax.axis_index("lon") * lax.axis_size("lat") + lax.axis_index("lat")
    return [(flat >> b) & 1 for b in range(count.bit_length() - 1)]


def half():
    return functools.reduce(jnp.bitwise_xor, place())


def iota(shape, axis):
    return lax.broadcasted_iota(jnp.int32, shape, axis)


def call(kernel, out, args, specs, scratch=(), flops=0, limit=16):
    size = sum(a.size * a.dtype.itemsize for a in args)
    return pl.pallas_call(
        kernel,
        out_shape=out,
        in_specs=specs,
        out_specs=jax.tree.map(lambda _: VMEM, out),
        scratch_shapes=scratch,
        compiler_params=pltpu.CompilerParams(vmem_limit_bytes=limit * 2**20),
        cost_estimate=pl.CostEstimate(flops=flops, bytes_accessed=size, transcendentals=0),
    )(*args)


def pack(values, tops, sums):
    rows = iota((STATS, values.shape[1]), 0)
    stats = jnp.zeros((STATS, values.shape[1]), F32)
    for j in range(2):
        high = sums[j].astype(BF16).astype(F32)
        for row, value in ((j, tops[j]), (2 + 2 * j, high), (3 + 2 * j, sums[j] - high)):
            stats = jnp.where(rows == row, value, stats)
    return jnp.concatenate([values, stats], axis=0)


def sides_kernel(rows, cols, kv_ref, queries_ref, pole_ref, sea_ref, own, queries, near_ref, far_ref, closed_ref,
                 wide, pole, sea, sem):
    pairs = ((pole_ref, pole), (sea_ref, sea), (kv_ref, own), (queries_ref, queries))
    copies = [pltpu.make_async_copy(*pair, sem.at[k]) for k, pair in enumerate(pairs)]
    for copy in copies:
        copy.start()
    copies[0].wait()
    copies[1].wait()
    closed_ref[...] = jnp.broadcast_to(closed_tiles(rows, cols, pole, sea), closed_ref.shape)
    copies[2].wait()
    odd = lax.axis_index("lon") % 2 == 1
    for k in range(2):
        for lane in range(0, own.shape[2], 128):
            lanes = slice(lane, lane + 128)
            wide[...] = own[k, :, lanes].astype(F32)
            for c in range(RADIUS):
                low = wide[pl.ds(c, rows, stride=cols)]
                high = wide[pl.ds(cols - RADIUS + c, rows, stride=cols)]
                near_ref[k, c * rows : (c + 1) * rows, lanes] = jnp.where(odd, low, high).astype(BF16)
                far_ref[k, c * rows : (c + 1) * rows, lanes] = jnp.where(odd, high, low).astype(BF16)
    copies[3].wait()


def register_kernel(own, other, queries, out_ref):
    lanes = pl.ds(pl.multiple_of(half() * PAIR, PAIR), PAIR)
    keys = jnp.concatenate([own[0, :, lanes], other[0, :, lanes]], axis=0)
    vals = jnp.concatenate([own[1, :, lanes], other[1, :, lanes]], axis=0)
    scaled = queries[:, lanes] * jnp.asarray(SCALE, BF16)
    first = iota(scaled.shape, 1) < HEAD_DIM
    asked = [jnp.where(first == (j == 0), scaled, jnp.zeros_like(scaled)) for j in range(2)]
    scores = [dot(keys, each, NT) for each in asked]
    parts, tops, sums = [], [], []
    for j in range(2):
        top = jnp.max(scores[j], axis=0, keepdims=True).astype(BF16).astype(F32)
        weights = jnp.exp(scores[j] - top)
        sums.append(jnp.sum(weights, axis=0, keepdims=True))
        tops.append(top)
        parts.append(dot(vals[:, j * HEAD_DIM : (j + 1) * HEAD_DIM], weights.astype(BF16), TN))
    out_ref[...] = pack(jnp.concatenate(parts, axis=0), tops, sums).astype(BF16)


def merge_kernel(bits, last, *refs):
    payloads, out_ref = refs[:-1], refs[-1]
    here = place()
    found = [(r[:PAIR].astype(F32), r[PAIR:].astype(F32)) for r in payloads]
    for level, bit in enumerate(bits):
        swap = here[bit] == 1
        step = 1 << level
        for low in range(len(found)):
            if not low & step:
                a, b = found[low], found[low + step]
                found[low] = tuple(jnp.where(swap, v, u) for u, v in zip(a, b))
                found[low + step] = tuple(jnp.where(swap, u, v) for u, v in zip(a, b))
    upper = iota((PAIR, found[0][0].shape[1]), 0) < HEAD_DIM
    tops, sums, factors = [], [], []
    for j in range(2):
        each = [stats[j : j + 1] for _, stats in found]
        top = functools.reduce(jnp.maximum, each)
        factor = [jnp.exp(e - top) for e in each]
        totals = [
            f * (stats[2 + 2 * j : 3 + 2 * j] + stats[3 + 2 * j : 4 + 2 * j])
            for f, (_, stats) in zip(factor, found)
        ]
        tops.append(top)
        sums.append(functools.reduce(jnp.add, totals))
        factors.append(factor)
    merged = functools.reduce(
        jnp.add,
        [values * jnp.where(upper, f, g) for f, g, (values, _) in zip(*factors, found)],
    )
    if last:
        out_ref[...] = (merged / jnp.where(upper, sums[0], sums[1])).astype(BF16)
    else:
        out_ref[...] = pack(merged, tops, sums).astype(BF16)


def segments(rows, cols):
    inner = (
        (rows, cols, False, 0, 0),
        (RADIUS, cols, False, "core", 0),
    )
    outer = (
        (RADIUS, rows, True, 0, "a"),
        (RADIUS, rows, True, 0, "b"),
        (RADIUS, DEEP, True, "core deep", "a"),
        (RADIUS, DEEP, True, "core deep", "b"),
        (RADIUS, cols, False, "cross", 0),
        (RADIUS, DEEP, True, "cross deep", "a"),
        (RADIUS, DEEP, True, "cross deep", "b"),
    )
    return inner, outer


def count(parts):
    return sum(part[0] * part[1] for part in parts)


def closed_tiles(rows, cols, pole, sea):
    lat, lon = lax.axis_index("lat"), lax.axis_index("lon")
    bands, tiles = sea.shape
    down, across = rows // TILE, cols // TILE
    lane = iota((1, AUG), 1)
    closed = jnp.zeros((1, AUG), F32)
    for i in range(down + 2):
        band = lat * down - 1 + i
        inside = (band >= 0) & (band < bands)
        band = jnp.clip(band, 0, bands - 1)
        for j in range(across + 2):
            tile = (lon * across - 1 + j + tiles) % tiles
            kept = inside & (pole[band] * sea[band, tile] > 0)
            at = rows + cols + i * (across + 2) + j
            closed = jnp.where(lane == at, jnp.where(kept, 0.0, MASKED), closed)
    return closed


def masks(rows, cols, closed, parts):
    lat, lon = lax.axis_index("lat"), lax.axis_index("lon")
    across = cols // TILE
    lat_odd, lon_odd = lat % 2 == 1, lon % 2 == 1
    starts = {
        0: 0,
        "core": jnp.where(lat_odd, -RADIUS, rows),
        "core deep": jnp.where(lat_odd, -DEEP, rows),
        "cross": jnp.where(lat_odd, rows, -RADIUS),
        "cross deep": jnp.where(lat_odd, rows, -DEEP),
        "a": jnp.where(lon_odd, -RADIUS, cols),
        "b": jnp.where(lon_odd, cols, -RADIUS),
    }
    lane = iota((1, AUG), 1)
    for slow, fast, fast_rows, row, col in parts:
        index = iota((slow * fast, AUG), 0)
        outer, inner = index >> (fast.bit_length() - 1), index & (fast - 1)
        row = starts[row] + (inner if fast_rows else outer)
        col = starts[col] + (outer if fast_rows else inner)
        apart = jnp.where(lane < rows, lane - row, lane - rows - col)
        far = (lane < rows + cols) & (jnp.abs(apart) > RADIUS)
        cell = ((row + TILE) >> 3) * (across + 2) + ((col + TILE) >> 3)
        value = jnp.where(lane - (rows + cols) == cell, closed, 0.0)
        yield jnp.where(far, MASKED, value).astype(BF16)


def fill(kbuf, vbuf, blocks, mask_blocks):
    ahead = kbuf.shape[1] - vbuf.shape[0]
    offset = 0
    for keys, vals in blocks:
        end = offset + keys.shape[0]
        for p in range(2):
            kbuf[p, ahead + offset : ahead + end, :PAIR] = keys[:, p * PAIR : (p + 1) * PAIR]
        vbuf[offset:end] = vals
        offset = end
    offset = ahead
    for mask in mask_blocks:
        for p in range(2):
            kbuf[p, offset : offset + mask.shape[0], PAIR:] = mask
        offset += mask.shape[0]


def attend(rows, cols, q_ref, kbuf, vbuf):
    size, ahead = rows * cols, kbuf.shape[1] - vbuf.shape[0]
    query = iota((size, AUG), 0)
    lane = iota((size, AUG), 1)
    tiles = (rows // TILE + 2) * (cols // TILE + 2)
    hot = (lane == query >> (cols.bit_length() - 1)) | (lane - rows == query & (cols - 1))
    hot = hot | ((lane >= rows + cols) & (lane < rows + cols + tiles))
    hot = jnp.where(hot, 1.0, 0.0).astype(BF16)
    first = iota((size, PAIR), 1) < HEAD_DIM
    for p in range(2):
        lanes = slice(p * PAIR, (p + 1) * PAIR)
        scaled = q_ref[:, lanes] * jnp.asarray(SCALE, BF16)
        tops, totals, mixed, weights = [], [], [], []
        for j in range(2):
            mine = jnp.where(first == (j == 0), scaled, jnp.zeros_like(scaled))
            scores = dot(jnp.concatenate([mine, hot], axis=1), kbuf[p], NT)
            tops.append(jnp.max(scores, axis=1, keepdims=True))
            each = jnp.exp(scores - tops[j])
            totals.append(jnp.sum(each, axis=1, keepdims=True))
            weights.append(each.astype(BF16))
            mixed.append(jnp.dot(weights[j][:, ahead:], vbuf[:, lanes], preferred_element_type=F32))
        yield p, lanes, *(jnp.where(first, *x) for x in (tops, totals, mixed)), weights


def inner_kernel(rows, cols, q_ref, own, core, reg_keys, closed_ref,
                 mixed_ref, top_ref, total_ref, reg_ref, kbuf, vbuf):
    first = jnp.where(lax.axis_index("lat") % 2 == 0, 0, (rows - RADIUS) * cols)
    taken = pl.ds(pl.multiple_of(first, 16), RADIUS * cols)
    blocks = [(own[0], own[1]), (core[0, taken], core[1, taken])]
    fill(kbuf, vbuf, blocks, masks(rows, cols, closed_ref[:1], segments(rows, cols)[0]))
    for p in range(2):
        kbuf[p, :NREG, :PAIR] = reg_keys[:, p * PAIR : (p + 1) * PAIR]
        kbuf[p, :NREG, PAIR:] = jnp.zeros((NREG, AUG), BF16)
    for p, lanes, top, total, mixed, weights in attend(rows, cols, q_ref, kbuf, vbuf):
        top_ref[:, lanes], total_ref[:, lanes], mixed_ref[:, lanes] = top, total, mixed
        for j in range(2):
            reg_ref[2 * p + j] = weights[j][:, :NREG]


def outer_kernel(rows, cols, q_ref, a, b, corner, cross, inner_top, inner_total, closed_ref,
                 rest_ref, factor_ref, kbuf, vbuf):
    blocks = [(ref[0], ref[1]) for ref in (a, b, corner, cross)]
    fill(kbuf, vbuf, blocks, masks(rows, cols, closed_ref[:1], segments(rows, cols)[1]))
    for _, lanes, top, total, mixed, _ in attend(rows, cols, q_ref, kbuf, vbuf):
        highest = jnp.maximum(top, inner_top[:, lanes])
        inner, outer = jnp.exp(inner_top[:, lanes] - highest), jnp.exp(top - highest)
        scale = 1.0 / (inner * inner_total[:, lanes] + outer * total)
        factor_ref[:, lanes] = inner * scale
        rest_ref[:, lanes] = mixed * (outer * scale)


def final_kernel(inner, factor, rest, reg_weights, mine, other, out_ref, reg_out_ref):
    here = half() == 0
    first = iota((inner.shape[0], PAIR), 1) < HEAD_DIM
    for p in range(2):
        lanes = slice(p * PAIR, (p + 1) * PAIR)
        vals = jnp.where(here == (p == 0), mine[...], other[...])
        added = jnp.where(first, dot(reg_weights[2 * p], vals, NT), dot(reg_weights[2 * p + 1], vals, NT))
        out_ref[:, lanes] = ((inner[:, lanes] + added) * factor[:, lanes] + rest[:, lanes]).astype(BF16)
        reg_out_ref[:, lanes] = vals.astype(F32).T.astype(BF16)


def shards(queries, key_values, pole_mask, sea_mask, reg_queries, reg_keys):
    rows, cols, channels = queries.shape
    lats, lons = lax.axis_size("lat"), lax.axis_size("lon")
    devices = lats * lons
    assert lats == 4 and lons & (lons - 1) == 0 and lons > 1
    assert rows & (rows - 1) == 0 and cols & (cols - 1) == 0 and rows % TILE == 0 and cols % TILE == 0 and TILE == DEEP == 8
    nbits = devices.bit_length() - 1
    lat = lax.axis_index("lat")
    everyone = ("lon", "lat")

    def swap(x, mask):
        return lax.ppermute(x, everyone, [(i, i ^ mask) for i in range(devices)])

    cells = rows * cols
    key_values = key_values.reshape(2, cells, channels)
    core = swap(key_values, 1)

    side = jax.ShapeDtypeStruct((2, RADIUS * rows, channels), BF16)
    inputs = (key_values, reg_queries, pole_mask, sea_mask)
    own, reg_queries, near_cols, far_cols, closed = call(
        functools.partial(sides_kernel, rows, cols),
        (
            jax.ShapeDtypeStruct(key_values.shape, BF16),
            jax.ShapeDtypeStruct(reg_queries.shape, BF16),
            side,
            side,
            jax.ShapeDtypeStruct((8, AUG), F32),
        ),
        tuple(pltpu.with_memory_space_constraint(x, pltpu.HBM) for x in inputs),
        [HBM] * 4,
        scratch=[
            pltpu.VMEM((cells, 128), F32),
            pltpu.SMEM(pole_mask.shape, jnp.int32),
            pltpu.SMEM(sea_mask.shape, jnp.int32),
            pltpu.SemaphoreType.DMA((4,)),
        ],
    )
    side_a = swap(near_cols, lats)
    side_b = lax.ppermute(
        far_cols, "lon", [(i, (i + 1 if i % 2 else i - 1) % lons) for i in range(lons)]
    )

    payload = call(
        register_kernel,
        jax.ShapeDtypeStruct((PAIR + STATS, NREG), BF16),
        (own, core, reg_queries),
        [VMEM] * 3,
        flops=4 * 2 * cells * NREG * 2 * PAIR,
    )

    queries = queries.reshape(cells, channels)
    square = jax.ShapeDtypeStruct((cells, channels), F32)
    inner, outer = (count(parts) for parts in segments(rows, cols))
    mixed, top, total, reg_weights = call(
        functools.partial(inner_kernel, rows, cols),
        (square, square, square, jax.ShapeDtypeStruct((HEADS, cells, NREG), BF16)),
        (queries, own, core, reg_keys, closed),
        [VMEM] * 5,
        scratch=[
            pltpu.VMEM((2, inner + NREG, PAIR + AUG), BF16),
            pltpu.VMEM((inner, channels), BF16),
        ],
        flops=2 * 2 * cells * inner * channels * 2,
    )

    side_a, side_b, _ = lax.optimization_barrier((side_a, side_b, payload))

    def take(shard, size, start, count):
        taken = lax.dynamic_slice_in_dim(shard.reshape(2, -1, size, channels), start, count, 2)
        return taken.reshape(2, -1, channels)

    core_deep, cross_deep = (1 - lat % 2) * (rows - DEEP), (lat % 2) * (rows - DEEP)
    corner = swap(
        jnp.concatenate([take(s, rows, core_deep, DEEP) for s in (side_a, side_b)], axis=1), 1
    )
    cross = swap(
        jnp.concatenate(
            [
                take(own, cells, (lat % 2) * (rows - RADIUS) * cols, RADIUS * cols),
                *[take(s, rows, cross_deep, DEEP) for s in (side_a, side_b)],
            ],
            axis=1,
        ),
        3,
    )
    rest, factor = call(
        functools.partial(outer_kernel, rows, cols),
        (square, square),
        (queries, side_a, side_b, corner, cross, top, total, closed),
        [VMEM] * 8,
        scratch=[pltpu.VMEM((2, outer, PAIR + AUG), BF16), pltpu.VMEM((outer, channels), BF16)],
        flops=2 * 2 * cells * outer * channels * 2,
    )

    stages = [tuple(range(b, min(b + 2, nbits))) for b in range(3, nbits, 2)] + [(1, 2)]
    for stage in stages:
        first, last = stage is stages[0], stage is stages[-1]
        gathered = [payload]
        for chosen in range(1, 1 << len(stage)):
            flips = [b for k, b in enumerate(stage) if chosen >> k & 1]
            gathered.append(swap(payload, sum(1 << b for b in flips) + len(flips) % 2))
        if first:
            gathered[0], _ = lax.optimization_barrier((gathered[0], mixed))
        if last:
            gathered[0], rest, factor = lax.optimization_barrier((gathered[0], rest, factor))
        payload = call(
            functools.partial(merge_kernel, stage, last),
            jax.ShapeDtypeStruct((PAIR if last else PAIR + STATS, NREG), BF16),
            tuple(gathered),
            [VMEM] * len(gathered),
        )

    attended, reg_out = call(
        final_kernel,
        (
            jax.ShapeDtypeStruct((cells, channels), BF16),
            jax.ShapeDtypeStruct((NREG, channels), BF16),
        ),
        (mixed, factor, rest, reg_weights, payload, swap(payload, 1)),
        [VMEM] * 6,
        flops=2 * cells * NREG * channels * 2,
    )
    return attended.reshape(rows, cols, channels), reg_out


def solution(mesh):
    return jax.shard_map(
        shards,
        mesh=mesh,
        in_specs=(P("lat", "lon", None), P(None, "lat", "lon", None), P(), P(), P(), P()),
        out_specs=(P("lat", "lon", None), P()),
        check_vma=False,
    )
```

```python
import functools

import jax
import jax.numpy as jnp
from jax import lax
from jax.experimental import pallas as pl
from jax.experimental.pallas import tpu as pltpu
from jax.sharding import PartitionSpec as P

HEADS = 4
HEAD_DIM = 64
NREG = 256
RADIUS = 6
TILE = 8
PAIR = 2 * HEAD_DIM
DEEP = 8
STATS = 8
AUG = 128
MASKED = -8192.0
SCALE = HEAD_DIM ** (-0.5)

BF16 = jnp.bfloat16
F32 = jnp.float32
NT = (((1,), (1,)), ((), ()))
TN = (((0,), (0,)), ((), ()))
VMEM = pl.BlockSpec(memory_space=pltpu.VMEM)
HBM = pl.BlockSpec(memory_space=pltpu.HBM)


def dot(a, b, dims):
    return lax.dot_general(a, b, dims, preferred_element_type=F32)


def place():
    count = lax.axis_size("lon") * lax.axis_size("lat")
    flat = lax.axis_index("lon") * lax.axis_size("lat") + lax.axis_index("lat")
    return [(flat >> b) & 1 for b in range(count.bit_length() - 1)]


def half():
    return functools.reduce(jnp.bitwise_xor, place())


def iota(shape, axis):
    return lax.broadcasted_iota(jnp.int32, shape, axis)


def call(kernel, out, args, specs, scratch=(), flops=0, limit=16):
    size = sum(a.size * a.dtype.itemsize for a in args)
    return pl.pallas_call(
        kernel,
        out_shape=out,
        in_specs=specs,
        out_specs=jax.tree.map(lambda _: VMEM, out),
        scratch_shapes=scratch,
        compiler_params=pltpu.CompilerParams(vmem_limit_bytes=limit * 2**20),
        cost_estimate=pl.CostEstimate(flops=flops, bytes_accessed=size, transcendentals=0),
    )(*args)


def pack(values, tops, sums):
    rows = iota((STATS, values.shape[1]), 0)
    stats = jnp.zeros((STATS, values.shape[1]), F32)
    for j in range(2):
        high = sums[j].astype(BF16).astype(F32)
        for row, value in ((j, tops[j]), (2 + 2 * j, high), (3 + 2 * j, sums[j] - high)):
            stats = jnp.where(rows == row, value, stats)
    return jnp.concatenate([values, stats], axis=0)


def sides_kernel(rows, cols, kv_ref, queries_ref, pole_ref, sea_ref, own, queries, near_ref, far_ref, closed_ref,
                 wide, pole, sea, sem):
    pairs = ((pole_ref, pole), (sea_ref, sea), (kv_ref, own), (queries_ref, queries))
    copies = [pltpu.make_async_copy(*pair, sem.at[k]) for k, pair in enumerate(pairs)]
    for copy in copies:
        copy.start()
    copies[0].wait()
    copies[1].wait()
    closed_ref[...] = jnp.broadcast_to(closed_tiles(rows, cols, pole, sea), closed_ref.shape)
    copies[2].wait()
    odd = lax.axis_index("lon") % 2 == 1
    for k in range(2):
        for lane in range(0, own.shape[2], 128):
            lanes = slice(lane, lane + 128)
            wide[...] = own[k, :, lanes].astype(F32)
            for c in range(RADIUS):
                low = wide[pl.ds(c, rows, stride=cols)]
                high = wide[pl.ds(cols - RADIUS + c, rows, stride=cols)]
                near_ref[k, c * rows : (c + 1) * rows, lanes] = jnp.where(odd, low, high).astype(BF16)
                far_ref[k, c * rows : (c + 1) * rows, lanes] = jnp.where(odd, high, low).astype(BF16)
    copies[3].wait()


def register_kernel(own, other, queries, out_ref):
    lanes = pl.ds(pl.multiple_of(half() * PAIR, PAIR), PAIR)
    keys = jnp.concatenate([own[0, :, lanes], other[0, :, lanes]], axis=0)
    vals = jnp.concatenate([own[1, :, lanes], other[1, :, lanes]], axis=0)
    scaled = queries[:, lanes] * jnp.asarray(SCALE, BF16)
    first = iota(scaled.shape, 1) < HEAD_DIM
    asked = [jnp.where(first == (j == 0), scaled, jnp.zeros_like(scaled)) for j in range(2)]
    scores = [dot(keys, each, NT) for each in asked]
    ones = jnp.ones((keys.shape[0], HEAD_DIM), BF16)
    parts, tops, sums = [], [], []
    for j in range(2):
        top = jnp.max(scores[j], axis=0, keepdims=True).astype(BF16).astype(F32)
        tops.append(top)
        weights = jnp.exp(scores[j] - top).astype(BF16)
        both = dot(jnp.concatenate([vals[:, j * HEAD_DIM : (j + 1) * HEAD_DIM], ones], axis=1), weights, TN)
        parts.append(both[:HEAD_DIM])
        sums.append(both[HEAD_DIM : HEAD_DIM + 1])
    out_ref[...] = pack(jnp.concatenate(parts, axis=0), tops, sums).astype(BF16)


def merge_kernel(stages, last, *refs):
    payloads, out_ref = refs[:-1], refs[-1]
    here = place()
    found = [(r[:PAIR].astype(F32), r[PAIR:].astype(F32)) for r in payloads]
    for level, (first, second) in enumerate(zip(*stages)):
        swap = jnp.where(half() == 0, here[first], here[second]) == 1
        step = 1 << level
        for low in range(len(found)):
            if not low & step:
                a, b = found[low], found[low + step]
                found[low] = tuple(jnp.where(swap, v, u) for u, v in zip(a, b))
                found[low + step] = tuple(jnp.where(swap, u, v) for u, v in zip(a, b))
    upper = iota((PAIR, found[0][0].shape[1]), 0) < HEAD_DIM
    tops, sums, factors = [], [], []
    for j in range(2):
        each = [stats[j : j + 1] for _, stats in found]
        top = functools.reduce(jnp.maximum, each)
        factor = [jnp.exp(e - top) for e in each]
        totals = [
            f * (stats[2 + 2 * j : 3 + 2 * j] + stats[3 + 2 * j : 4 + 2 * j])
            for f, (_, stats) in zip(factor, found)
        ]
        tops.append(top)
        sums.append(functools.reduce(jnp.add, totals))
        factors.append(factor)
    merged = functools.reduce(
        jnp.add,
        [values * jnp.where(upper, f, g) for f, g, (values, _) in zip(*factors, found)],
    )
    if last:
        out_ref[...] = (merged / jnp.where(upper, sums[0], sums[1])).astype(BF16)
    else:
        out_ref[...] = pack(merged, tops, sums).astype(BF16)


def segments(rows, cols):
    inner = (
        (rows, cols, False, 0, 0),
        (RADIUS, cols, False, "core", 0),
    )
    outer = (
        (RADIUS, rows, True, 0, "a"),
        (RADIUS, rows, True, 0, "b"),
        (RADIUS, DEEP, True, "core deep", "a"),
        (RADIUS, DEEP, True, "core deep", "b"),
        (RADIUS, cols, False, "cross", 0),
        (RADIUS, DEEP, True, "cross deep", "a"),
        (RADIUS, DEEP, True, "cross deep", "b"),
    )
    return inner, outer


def count(parts):
    return sum(part[0] * part[1] for part in parts)


def closed_tiles(rows, cols, pole, sea):
    lat, lon = lax.axis_index("lat"), lax.axis_index("lon")
    bands, tiles = sea.shape
    down, across = rows // TILE, cols // TILE
    lane = iota((1, AUG), 1)
    closed = jnp.zeros((1, AUG), F32)
    for i in range(down + 2):
        band = lat * down - 1 + i
        inside = (band >= 0) & (band < bands)
        band = jnp.clip(band, 0, bands - 1)
        for j in range(across + 2):
            tile = (lon * across - 1 + j + tiles) % tiles
            kept = inside & (pole[band] * sea[band, tile] > 0)
            at = rows + cols + i * (across + 2) + j
            closed = jnp.where(lane == at, jnp.where(kept, 0.0, MASKED), closed)
    return closed


def masks(rows, cols, closed, parts):
    lat, lon = lax.axis_index("lat"), lax.axis_index("lon")
    across = cols // TILE
    lat_odd, lon_odd = lat % 2 == 1, lon % 2 == 1
    starts = {
        0: 0,
        "core": jnp.where(lat_odd, -RADIUS, rows),
        "core deep": jnp.where(lat_odd, -DEEP, rows),
        "cross": jnp.where(lat_odd, rows, -RADIUS),
        "cross deep": jnp.where(lat_odd, rows, -DEEP),
        "a": jnp.where(lon_odd, -RADIUS, cols),
        "b": jnp.where(lon_odd, cols, -RADIUS),
    }
    lane = iota((1, AUG), 1)
    for slow, fast, fast_rows, row, col in parts:
        index = iota((slow * fast, AUG), 0)
        outer, inner = index >> (fast.bit_length() - 1), index & (fast - 1)
        row = starts[row] + (inner if fast_rows else outer)
        col = starts[col] + (outer if fast_rows else inner)
        apart = jnp.where(lane < rows, lane - row, lane - rows - col)
        far = (lane < rows + cols) & (jnp.abs(apart) > RADIUS)
        cell = ((row + TILE) >> 3) * (across + 2) + ((col + TILE) >> 3)
        value = jnp.where(lane - (rows + cols) == cell, closed, 0.0)
        yield jnp.where(far, MASKED, value).astype(BF16)


def fill(kbuf, vbuf, blocks, mask_blocks):
    ahead = kbuf.shape[1] - vbuf.shape[0]
    offset = 0
    for keys, vals in blocks:
        end = offset + keys.shape[0]
        for p in range(2):
            kbuf[p, ahead + offset : ahead + end, :PAIR] = keys[:, p * PAIR : (p + 1) * PAIR]
        vbuf[offset:end] = vals
        offset = end
    offset = ahead
    for mask in mask_blocks:
        for p in range(2):
            kbuf[p, offset : offset + mask.shape[0], PAIR:] = mask
        offset += mask.shape[0]


def attend(rows, cols, q_ref, kbuf, vbuf):
    size, ahead = rows * cols, kbuf.shape[1] - vbuf.shape[0]
    query = iota((size, AUG), 0)
    lane = iota((size, AUG), 1)
    tiles = (rows // TILE + 2) * (cols // TILE + 2)
    hot = (lane == query >> (cols.bit_length() - 1)) | (lane - rows == query & (cols - 1))
    hot = hot | ((lane >= rows + cols) & (lane < rows + cols + tiles))
    hot = jnp.where(hot, 1.0, 0.0).astype(BF16)
    first = iota((size, PAIR), 1) < HEAD_DIM
    for p in range(2):
        lanes = slice(p * PAIR, (p + 1) * PAIR)
        scaled = q_ref[:, lanes] * jnp.asarray(SCALE, BF16)
        tops, totals, mixed, weights = [], [], [], []
        for j in range(2):
            mine = jnp.where(first == (j == 0), scaled, jnp.zeros_like(scaled))
            scores = dot(jnp.concatenate([mine, hot], axis=1), kbuf[p], NT)
            tops.append(jnp.max(scores, axis=1, keepdims=True))
            each = jnp.exp(scores - tops[j])
            totals.append(jnp.sum(each, axis=1, keepdims=True))
            weights.append(each.astype(BF16))
            mixed.append(jnp.dot(weights[j][:, ahead:], vbuf[:, lanes], preferred_element_type=F32))
        yield p, lanes, *(jnp.where(first, *x) for x in (tops, totals, mixed)), weights


def inner_kernel(rows, cols, q_ref, own, core, reg_keys, closed_ref,
                 mixed_ref, top_ref, total_ref, reg_ref, kbuf, vbuf):
    first = jnp.where(lax.axis_index("lat") % 2 == 0, 0, (rows - RADIUS) * cols)
    taken = pl.ds(pl.multiple_of(first, 16), RADIUS * cols)
    blocks = [(own[0], own[1]), (core[0, taken], core[1, taken])]
    fill(kbuf, vbuf, blocks, masks(rows, cols, closed_ref[:1], segments(rows, cols)[0]))
    for p in range(2):
        kbuf[p, :NREG, :PAIR] = reg_keys[:, p * PAIR : (p + 1) * PAIR]
        kbuf[p, :NREG, PAIR:] = jnp.zeros((NREG, AUG), BF16)
    for p, lanes, top, total, mixed, weights in attend(rows, cols, q_ref, kbuf, vbuf):
        top_ref[:, lanes], total_ref[:, lanes], mixed_ref[:, lanes] = top, total, mixed
        for j in range(2):
            reg_ref[2 * p + j] = weights[j][:, :NREG]


def outer_kernel(rows, cols, q_ref, a, b, corner, cross, inner_top, inner_total, closed_ref,
                 rest_ref, factor_ref, kbuf, vbuf):
    blocks = [(ref[0], ref[1]) for ref in (a, b, corner, cross)]
    fill(kbuf, vbuf, blocks, masks(rows, cols, closed_ref[:1], segments(rows, cols)[1]))
    for _, lanes, top, total, mixed, _ in attend(rows, cols, q_ref, kbuf, vbuf):
        highest = jnp.maximum(top, inner_top[:, lanes])
        inner, outer = jnp.exp(inner_top[:, lanes] - highest), jnp.exp(top - highest)
        scale = 1.0 / (inner * inner_total[:, lanes] + outer * total)
        factor_ref[:, lanes] = inner * scale
        rest_ref[:, lanes] = mixed * (outer * scale)


def final_kernel(inner, factor, rest, reg_weights, mine, other, out_ref, reg_out_ref):
    here = half() == 0
    first = iota((inner.shape[0], PAIR), 1) < HEAD_DIM
    for p in range(2):
        lanes = slice(p * PAIR, (p + 1) * PAIR)
        vals = jnp.where(here == (p == 0), mine[...], other[...])
        added = jnp.where(first, dot(reg_weights[2 * p], vals, NT), dot(reg_weights[2 * p + 1], vals, NT))
        out_ref[:, lanes] = ((inner[:, lanes] + added) * factor[:, lanes] + rest[:, lanes]).astype(BF16)
        reg_out_ref[:, lanes] = vals.astype(F32).T.astype(BF16)


def shards(queries, key_values, pole_mask, sea_mask, reg_queries, reg_keys):
    rows, cols, channels = queries.shape
    lats, lons = lax.axis_size("lat"), lax.axis_size("lon")
    devices = lats * lons
    assert lats == 4 and lons & (lons - 1) == 0 and lons > 1
    assert rows & (rows - 1) == 0 and cols & (cols - 1) == 0 and rows % TILE == 0 and cols % TILE == 0 and TILE == DEEP == 8
    nbits = devices.bit_length() - 1
    assert nbits % 2 == 1
    lat = lax.axis_index("lat")
    everyone = ("lon", "lat")

    def swap(x, mask):
        return lax.ppermute(x, everyone, [(i, i ^ mask) for i in range(devices)])

    cells = rows * cols
    key_values = key_values.reshape(2, cells, channels)
    core = swap(key_values, 1)

    side = jax.ShapeDtypeStruct((2, RADIUS * rows, channels), BF16)
    inputs = (key_values, reg_queries, pole_mask, sea_mask)
    own, reg_queries, near_cols, far_cols, closed = call(
        functools.partial(sides_kernel, rows, cols),
        (
            jax.ShapeDtypeStruct(key_values.shape, BF16),
            jax.ShapeDtypeStruct(reg_queries.shape, BF16),
            side,
            side,
            jax.ShapeDtypeStruct((8, AUG), F32),
        ),
        tuple(pltpu.with_memory_space_constraint(x, pltpu.HBM) for x in inputs),
        [HBM] * 4,
        scratch=[
            pltpu.VMEM((cells, 128), F32),
            pltpu.SMEM(pole_mask.shape, jnp.int32),
            pltpu.SMEM(sea_mask.shape, jnp.int32),
            pltpu.SemaphoreType.DMA((4,)),
        ],
    )
    side_a = swap(near_cols, lats)
    side_b = lax.ppermute(
        far_cols, "lon", [(i, (i + 1 if i % 2 else i - 1) % lons) for i in range(lons)]
    )

    payload = call(
        register_kernel,
        jax.ShapeDtypeStruct((PAIR + STATS, NREG), BF16),
        (own, core, reg_queries),
        [VMEM] * 3,
        flops=4 * 2 * cells * NREG * 2 * PAIR,
    )

    queries = queries.reshape(cells, channels)
    square = jax.ShapeDtypeStruct((cells, channels), F32)
    inner, outer = (count(parts) for parts in segments(rows, cols))
    mixed, top, total, reg_weights = call(
        functools.partial(inner_kernel, rows, cols),
        (square, square, square, jax.ShapeDtypeStruct((HEADS, cells, NREG), BF16)),
        (queries, own, core, reg_keys, closed),
        [VMEM] * 5,
        scratch=[
            pltpu.VMEM((2, inner + NREG, PAIR + AUG), BF16),
            pltpu.VMEM((inner, channels), BF16),
        ],
        flops=2 * 2 * cells * inner * channels * 2,
    )

    side_a, side_b, _, _ = lax.optimization_barrier((side_a, side_b, payload, mixed))

    def take(shard, size, start, count):
        taken = lax.dynamic_slice_in_dim(shard.reshape(2, -1, size, channels), start, count, 2)
        return taken.reshape(2, -1, channels)

    core_deep, cross_deep = (1 - lat % 2) * (rows - DEEP), (lat % 2) * (rows - DEEP)
    corner = swap(
        jnp.concatenate([take(s, rows, core_deep, DEEP) for s in (side_a, side_b)], axis=1), 1
    )
    cross = lax.ppermute(
        jnp.concatenate(
            [
                take(own, cells, (lat % 2) * (rows - RADIUS) * cols, RADIUS * cols),
                *[take(s, rows, cross_deep, DEEP) for s in (side_a, side_b)],
            ],
            axis=1,
        ),
        everyone,
        [(i, i ^ 3 if i % lats in (1, 2) else i ^ 2 * lats) for i in range(devices)],
    )
    rest, factor = call(
        functools.partial(outer_kernel, rows, cols),
        (square, square),
        (queries, side_a, side_b, corner, cross, top, total, closed),
        [VMEM] * 8,
        scratch=[pltpu.VMEM((2, outer, PAIR + AUG), BF16), pltpu.VMEM((outer, channels), BF16)],
        flops=2 * 2 * cells * outer * channels * 2,
    )

    near_bits, far_bits = (1, 2), [(b, b + 1) for b in range(3, nbits, 2)]
    steps = list(zip([*far_bits, near_bits], [near_bits, *far_bits]))
    for step in steps:
        first, last = step is steps[0], step is steps[-1]
        gathered = [payload]
        for chosen in range(1, 4):
            pairs = []
            for i in range(devices):
                flips = [b for k, b in enumerate(step[bin(i).count("1") % 2]) if chosen >> k & 1]
                pairs.append((i, i ^ (sum(1 << b for b in flips) + len(flips) % 2)))
            gathered.append(lax.ppermute(payload, everyone, pairs))
        if first:
            gathered[0], _ = lax.optimization_barrier((gathered[0], mixed))
        if last:
            gathered[0], rest, factor = lax.optimization_barrier((gathered[0], rest, factor))
        payload = call(
            functools.partial(merge_kernel, step, last),
            jax.ShapeDtypeStruct((PAIR if last else PAIR + STATS, NREG), BF16),
            tuple(gathered),
            [VMEM] * len(gathered),
        )

    attended, reg_out = call(
        final_kernel,
        (
            jax.ShapeDtypeStruct((cells, channels), BF16),
            jax.ShapeDtypeStruct((NREG, channels), BF16),
        ),
        (mixed, factor, rest, reg_weights, payload, swap(payload, 1)),
        [VMEM] * 6,
        flops=2 * cells * NREG * channels * 2,
    )
    return attended.reshape(rows, cols, channels), reg_out


def solution(mesh):
    return jax.shard_map(
        shards,
        mesh=mesh,
        in_specs=(P("lat", "lon", None), P(None, "lat", "lon", None), P(), P(), P(), P()),
        out_specs=(P("lat", "lon", None), P()),
        check_vma=False,
    )
```

```python
import functools

import jax
import jax.numpy as jnp
from jax import lax
from jax.experimental import pallas as pl
from jax.experimental.pallas import tpu as pltpu
from jax.sharding import PartitionSpec as P

HEADS = 4
HEAD_DIM = 64
NREG = 256
RADIUS = 6
TILE = 8
PAIR = 2 * HEAD_DIM
DEEP = 8
STATS = 8
AUG = 128
MASKED = -8192.0
SCALE = HEAD_DIM ** (-0.5)

BF16 = jnp.bfloat16
F32 = jnp.float32
NT = (((1,), (1,)), ((), ()))
TN = (((0,), (0,)), ((), ()))
VMEM = pl.BlockSpec(memory_space=pltpu.VMEM)
HBM = pl.BlockSpec(memory_space=pltpu.HBM)


def dot(a, b, dims):
    return lax.dot_general(a, b, dims, preferred_element_type=F32)


def place():
    count = lax.axis_size("lon") * lax.axis_size("lat")
    flat = lax.axis_index("lon") * lax.axis_size("lat") + lax.axis_index("lat")
    return [(flat >> b) & 1 for b in range(count.bit_length() - 1)]


def half():
    return functools.reduce(jnp.bitwise_xor, place())


def iota(shape, axis):
    return lax.broadcasted_iota(jnp.int32, shape, axis)


def call(kernel, out, args, specs, scratch=(), flops=0, limit=16):
    size = sum(a.size * a.dtype.itemsize for a in args)
    return pl.pallas_call(
        kernel,
        out_shape=out,
        in_specs=specs,
        out_specs=jax.tree.map(lambda _: VMEM, out),
        scratch_shapes=scratch,
        compiler_params=pltpu.CompilerParams(vmem_limit_bytes=limit * 2**20),
        cost_estimate=pl.CostEstimate(flops=flops, bytes_accessed=size, transcendentals=0),
    )(*args)


def pack(values, tops, sums):
    rows = iota((STATS, values.shape[1]), 0)
    stats = jnp.zeros((STATS, values.shape[1]), F32)
    for j in range(2):
        high = sums[j].astype(BF16).astype(F32)
        for row, value in ((j, tops[j]), (2 + 2 * j, high), (3 + 2 * j, sums[j] - high)):
            stats = jnp.where(rows == row, value, stats)
    return jnp.concatenate([values, stats], axis=0)


def sides_kernel(rows, cols, kv_ref, queries_ref, pole_ref, sea_ref, own, queries, near_ref, far_ref, closed_ref,
                 wide, pole, sea, sem):
    pairs = ((pole_ref, pole), (sea_ref, sea), (kv_ref, own), (queries_ref, queries))
    copies = [pltpu.make_async_copy(*pair, sem.at[k]) for k, pair in enumerate(pairs)]
    for copy in copies:
        copy.start()
    copies[0].wait()
    copies[1].wait()
    closed_ref[...] = jnp.broadcast_to(closed_tiles(rows, cols, pole, sea), closed_ref.shape)
    copies[2].wait()
    odd = lax.axis_index("lon") % 2 == 1
    for k in range(2):
        for lane in range(0, own.shape[2], 128):
            lanes = slice(lane, lane + 128)
            wide[...] = own[k, :, lanes].astype(F32)
            for c in range(RADIUS):
                low = wide[pl.ds(c, rows, stride=cols)]
                high = wide[pl.ds(cols - RADIUS + c, rows, stride=cols)]
                near_ref[k, c * rows : (c + 1) * rows, lanes] = jnp.where(odd, low, high).astype(BF16)
                far_ref[k, c * rows : (c + 1) * rows, lanes] = jnp.where(odd, high, low).astype(BF16)
    copies[3].wait()


def register_kernel(own, other, queries, out_ref):
    lanes = pl.ds(pl.multiple_of(half() * PAIR, PAIR), PAIR)
    keys = jnp.concatenate([own[0, :, lanes], other[0, :, lanes]], axis=0)
    vals = jnp.concatenate([own[1, :, lanes], other[1, :, lanes]], axis=0)
    scaled = queries[:, lanes] * jnp.asarray(SCALE, BF16)
    first = iota(scaled.shape, 1) < HEAD_DIM
    asked = [jnp.where(first == (j == 0), scaled, jnp.zeros_like(scaled)) for j in range(2)]
    scores = [dot(keys, each, NT) for each in asked]
    ones = jnp.ones((keys.shape[0], HEAD_DIM), BF16)
    parts, tops, sums = [], [], []
    for j in range(2):
        top = jnp.max(scores[j], axis=0, keepdims=True).astype(BF16).astype(F32)
        tops.append(top)
        weights = jnp.exp(scores[j] - top).astype(BF16)
        both = dot(jnp.concatenate([vals[:, j * HEAD_DIM : (j + 1) * HEAD_DIM], ones], axis=1), weights, TN)
        parts.append(both[:HEAD_DIM])
        sums.append(both[HEAD_DIM : HEAD_DIM + 1])
    out_ref[...] = pack(jnp.concatenate(parts, axis=0), tops, sums).astype(BF16)


def merge_kernel(stages, last, *refs):
    payloads, out_ref = refs[:-1], refs[-1]
    here = place()
    found = [(r[:PAIR].astype(F32), r[PAIR:].astype(F32)) for r in payloads]
    for level, (first, second) in enumerate(zip(*stages)):
        swap = jnp.where(half() == 0, here[first], here[second]) == 1
        step = 1 << level
        for low in range(len(found)):
            if not low & step:
                a, b = found[low], found[low + step]
                found[low] = tuple(jnp.where(swap, v, u) for u, v in zip(a, b))
                found[low + step] = tuple(jnp.where(swap, u, v) for u, v in zip(a, b))
    upper = iota((PAIR, found[0][0].shape[1]), 0) < HEAD_DIM
    tops, sums, factors = [], [], []
    for j in range(2):
        each = [stats[j : j + 1] for _, stats in found]
        top = functools.reduce(jnp.maximum, each)
        factor = [jnp.exp(e - top) for e in each]
        totals = [
            f * (stats[2 + 2 * j : 3 + 2 * j] + stats[3 + 2 * j : 4 + 2 * j])
            for f, (_, stats) in zip(factor, found)
        ]
        tops.append(top)
        sums.append(functools.reduce(jnp.add, totals))
        factors.append(factor)
    merged = functools.reduce(
        jnp.add,
        [values * jnp.where(upper, f, g) for f, g, (values, _) in zip(*factors, found)],
    )
    if last:
        out_ref[...] = (merged / jnp.where(upper, sums[0], sums[1])).astype(BF16)
    else:
        out_ref[...] = pack(merged, tops, sums).astype(BF16)


def segments(rows, cols):
    inner = (
        (rows, cols, False, 0, 0),
        (RADIUS, cols, False, "core", 0),
    )
    outer = (
        (RADIUS, rows, True, 0, "a"),
        (RADIUS, rows, True, 0, "b"),
        (RADIUS, DEEP, True, "core deep", "a"),
        (RADIUS, DEEP, True, "core deep", "b"),
        (RADIUS, cols, False, "cross", 0),
        (RADIUS, DEEP, True, "cross deep", "a"),
        (RADIUS, DEEP, True, "cross deep", "b"),
    )
    return inner, outer


def count(parts):
    return sum(part[0] * part[1] for part in parts)


def closed_tiles(rows, cols, pole, sea):
    lat, lon = lax.axis_index("lat"), lax.axis_index("lon")
    bands, tiles = sea.shape
    down, across = rows // TILE, cols // TILE
    lane = iota((1, AUG), 1)
    closed = jnp.zeros((1, AUG), F32)
    for i in range(down + 2):
        band = lat * down - 1 + i
        inside = (band >= 0) & (band < bands)
        band = jnp.clip(band, 0, bands - 1)
        for j in range(across + 2):
            tile = (lon * across - 1 + j + tiles) % tiles
            kept = inside & (pole[band] * sea[band, tile] > 0)
            at = rows + cols + i * (across + 2) + j
            closed = jnp.where(lane == at, jnp.where(kept, 0.0, MASKED), closed)
    return closed


def masks(rows, cols, closed, parts):
    lat, lon = lax.axis_index("lat"), lax.axis_index("lon")
    across = cols // TILE
    lat_odd, lon_odd = lat % 2 == 1, lon % 2 == 1
    starts = {
        0: 0,
        "core": jnp.where(lat_odd, -RADIUS, rows),
        "core deep": jnp.where(lat_odd, -DEEP, rows),
        "cross": jnp.where(lat_odd, rows, -RADIUS),
        "cross deep": jnp.where(lat_odd, rows, -DEEP),
        "a": jnp.where(lon_odd, -RADIUS, cols),
        "b": jnp.where(lon_odd, cols, -RADIUS),
    }
    lane = iota((1, AUG), 1)
    for slow, fast, fast_rows, row, col in parts:
        index = iota((slow * fast, AUG), 0)
        outer, inner = index >> (fast.bit_length() - 1), index & (fast - 1)
        row = starts[row] + (inner if fast_rows else outer)
        col = starts[col] + (outer if fast_rows else inner)
        apart = jnp.where(lane < rows, lane - row, lane - rows - col)
        far = (lane < rows + cols) & (jnp.abs(apart) > RADIUS)
        cell = ((row + TILE) >> 3) * (across + 2) + ((col + TILE) >> 3)
        value = jnp.where(lane - (rows + cols) == cell, closed, 0.0)
        yield jnp.where(far, MASKED, value).astype(BF16)


def fill(kbuf, vbuf, blocks, mask_blocks):
    ahead = kbuf.shape[1] - vbuf.shape[0]
    offset = 0
    for keys, vals in blocks:
        end = offset + keys.shape[0]
        for p in range(2):
            kbuf[p, ahead + offset : ahead + end, :PAIR] = keys[:, p * PAIR : (p + 1) * PAIR]
        vbuf[offset:end] = vals
        offset = end
    offset = ahead
    for mask in mask_blocks:
        for p in range(2):
            kbuf[p, offset : offset + mask.shape[0], PAIR:] = mask
        offset += mask.shape[0]


def attend(rows, cols, q_ref, kbuf, vbuf):
    size, ahead = rows * cols, kbuf.shape[1] - vbuf.shape[0]
    query = iota((size, AUG), 0)
    lane = iota((size, AUG), 1)
    tiles = (rows // TILE + 2) * (cols // TILE + 2)
    hot = (lane == query >> (cols.bit_length() - 1)) | (lane - rows == query & (cols - 1))
    hot = hot | ((lane >= rows + cols) & (lane < rows + cols + tiles))
    hot = jnp.where(hot, 1.0, 0.0).astype(BF16)
    first = iota((size, PAIR), 1) < HEAD_DIM
    scores = []
    for p in range(2):
        scaled = q_ref[:, p * PAIR : (p + 1) * PAIR] * jnp.asarray(SCALE, BF16)
        for j in range(2):
            mine = jnp.where(first == (j == 0), scaled, jnp.zeros_like(scaled))
            scores.append(dot(jnp.concatenate([mine, hot], axis=1), kbuf[p], NT))
    for p in range(2):
        lanes = slice(p * PAIR, (p + 1) * PAIR)
        tops, totals, mixed, weights = [], [], [], []
        for each in scores[2 * p : 2 * p + 2]:
            top = jnp.max(each, axis=1, keepdims=True)
            each = jnp.exp(each - top)
            tops.append(top)
            totals.append(jnp.sum(each, axis=1, keepdims=True))
            weights.append(each.astype(BF16))
            mixed.append(jnp.dot(weights[-1][:, ahead:], vbuf[:, lanes], preferred_element_type=F32))
        yield p, lanes, *(jnp.where(first, *x) for x in (tops, totals, mixed)), weights


def inner_kernel(rows, cols, q_ref, own, core, reg_keys, closed_ref,
                 mixed_ref, top_ref, total_ref, reg_ref, kbuf, vbuf):
    first = jnp.where(lax.axis_index("lat") % 2 == 0, 0, (rows - RADIUS) * cols)
    taken = pl.ds(pl.multiple_of(first, 16), RADIUS * cols)
    blocks = [(own[0], own[1]), (core[0, taken], core[1, taken])]
    fill(kbuf, vbuf, blocks, masks(rows, cols, closed_ref[:1], segments(rows, cols)[0]))
    for p in range(2):
        kbuf[p, :NREG, :PAIR] = reg_keys[:, p * PAIR : (p + 1) * PAIR]
        kbuf[p, :NREG, PAIR:] = jnp.zeros((NREG, AUG), BF16)
    for p, lanes, top, total, mixed, weights in attend(rows, cols, q_ref, kbuf, vbuf):
        top_ref[:, lanes], total_ref[:, lanes], mixed_ref[:, lanes] = top, total, mixed
        for j in range(2):
            reg_ref[2 * p + j] = weights[j][:, :NREG]


def outer_kernel(rows, cols, q_ref, a, b, corner, cross, inner_top, inner_total, closed_ref,
                 rest_ref, factor_ref, kbuf, vbuf):
    blocks = [(ref[0], ref[1]) for ref in (a, b, corner, cross)]
    fill(kbuf, vbuf, blocks, masks(rows, cols, closed_ref[:1], segments(rows, cols)[1]))
    for _, lanes, top, total, mixed, _ in attend(rows, cols, q_ref, kbuf, vbuf):
        highest = jnp.maximum(top, inner_top[:, lanes])
        inner, outer = jnp.exp(inner_top[:, lanes] - highest), jnp.exp(top - highest)
        scale = 1.0 / (inner * inner_total[:, lanes] + outer * total)
        factor_ref[:, lanes] = inner * scale
        rest_ref[:, lanes] = mixed * (outer * scale)


def final_kernel(inner, factor, rest, reg_weights, mine, other, out_ref, reg_out_ref):
    here = half() == 0
    first = iota((inner.shape[0], PAIR), 1) < HEAD_DIM
    for p in range(2):
        lanes = slice(p * PAIR, (p + 1) * PAIR)
        vals = jnp.where(here == (p == 0), mine[...], other[...])
        added = jnp.where(first, dot(reg_weights[2 * p], vals, NT), dot(reg_weights[2 * p + 1], vals, NT))
        out_ref[:, lanes] = ((inner[:, lanes] + added) * factor[:, lanes] + rest[:, lanes]).astype(BF16)
        reg_out_ref[:, lanes] = vals.astype(F32).T.astype(BF16)


def shards(queries, key_values, pole_mask, sea_mask, reg_queries, reg_keys):
    rows, cols, channels = queries.shape
    lats, lons = lax.axis_size("lat"), lax.axis_size("lon")
    devices = lats * lons
    assert lats == 4 and lons & (lons - 1) == 0 and lons > 1
    assert rows & (rows - 1) == 0 and cols & (cols - 1) == 0 and rows % TILE == 0 and cols % TILE == 0 and TILE == DEEP == 8
    nbits = devices.bit_length() - 1
    assert nbits % 2 == 1
    lat = lax.axis_index("lat")
    everyone = ("lon", "lat")

    def swap(x, mask):
        return lax.ppermute(x, everyone, [(i, i ^ mask) for i in range(devices)])

    cells = rows * cols
    key_values = key_values.reshape(2, cells, channels)
    core = swap(key_values, 1)

    side = jax.ShapeDtypeStruct((2, RADIUS * rows, channels), BF16)
    inputs = (key_values, reg_queries, pole_mask, sea_mask)
    own, reg_queries, near_cols, far_cols, closed = call(
        functools.partial(sides_kernel, rows, cols),
        (
            jax.ShapeDtypeStruct(key_values.shape, BF16),
            jax.ShapeDtypeStruct(reg_queries.shape, BF16),
            side,
            side,
            jax.ShapeDtypeStruct((8, AUG), F32),
        ),
        tuple(pltpu.with_memory_space_constraint(x, pltpu.HBM) for x in inputs),
        [HBM] * 4,
        scratch=[
            pltpu.VMEM((cells, 128), F32),
            pltpu.SMEM(pole_mask.shape, jnp.int32),
            pltpu.SMEM(sea_mask.shape, jnp.int32),
            pltpu.SemaphoreType.DMA((4,)),
        ],
    )
    side_b = lax.ppermute(
        far_cols, "lon", [(i, (i + 1 if i % 2 else i - 1) % lons) for i in range(lons)]
    )

    near_cols, _ = lax.optimization_barrier((near_cols, core))
    side_a = swap(near_cols, lats)

    payload = call(
        register_kernel,
        jax.ShapeDtypeStruct((PAIR + STATS, NREG), BF16),
        (own, core, reg_queries),
        [VMEM] * 3,
        flops=4 * 2 * cells * NREG * 2 * PAIR,
    )

    queries = queries.reshape(cells, channels)
    square = jax.ShapeDtypeStruct((cells, channels), F32)
    inner, outer = (count(parts) for parts in segments(rows, cols))
    mixed, top, total, reg_weights = call(
        functools.partial(inner_kernel, rows, cols),
        (square, square, square, jax.ShapeDtypeStruct((HEADS, cells, NREG), BF16)),
        (queries, own, core, reg_keys, closed),
        [VMEM] * 5,
        scratch=[
            pltpu.VMEM((2, inner + NREG, PAIR + AUG), BF16),
            pltpu.VMEM((inner, channels), BF16),
        ],
        flops=2 * 2 * cells * inner * channels * 2,
    )

    corner_a, corner_b, _ = lax.optimization_barrier((side_a, side_b, payload))
    side_a, side_b, _, _ = lax.optimization_barrier((side_a, side_b, payload, mixed))

    def take(shard, size, start, count):
        taken = lax.dynamic_slice_in_dim(shard.reshape(2, -1, size, channels), start, count, 2)
        return taken.reshape(2, -1, channels)

    core_deep, cross_deep = (1 - lat % 2) * (rows - DEEP), (lat % 2) * (rows - DEEP)
    corner = swap(
        jnp.concatenate([take(s, rows, core_deep, DEEP) for s in (corner_a, corner_b)], axis=1), 1
    )
    cross = lax.ppermute(
        jnp.concatenate(
            [
                take(own, cells, (lat % 2) * (rows - RADIUS) * cols, RADIUS * cols),
                *[take(s, rows, cross_deep, DEEP) for s in (side_a, side_b)],
            ],
            axis=1,
        ),
        everyone,
        [(i, i ^ 3 if i % lats in (1, 2) else i ^ 2 * lats) for i in range(devices)],
    )
    rest, factor = call(
        functools.partial(outer_kernel, rows, cols),
        (square, square),
        (queries, side_a, side_b, corner, cross, top, total, closed),
        [VMEM] * 8,
        scratch=[pltpu.VMEM((2, outer, PAIR + AUG), BF16), pltpu.VMEM((outer, channels), BF16)],
        flops=2 * 2 * cells * outer * channels * 2,
    )

    near_bits, far_bits = (1, 2), [(b, b + 1) for b in range(3, nbits, 2)]
    steps = list(zip([*far_bits, near_bits], [near_bits, *far_bits]))
    for step in steps:
        first, last = step is steps[0], step is steps[-1]
        gathered = [payload]
        for chosen in range(1, 4):
            pairs = []
            for i in range(devices):
                flips = [b for k, b in enumerate(step[bin(i).count("1") % 2]) if chosen >> k & 1]
                pairs.append((i, i ^ (sum(1 << b for b in flips) + len(flips) % 2)))
            gathered.append(lax.ppermute(payload, everyone, pairs))
        if first:
            gathered[0], _ = lax.optimization_barrier((gathered[0], mixed))
        if last:
            gathered[0], rest, factor = lax.optimization_barrier((gathered[0], rest, factor))
        payload = call(
            functools.partial(merge_kernel, step, last),
            jax.ShapeDtypeStruct((PAIR if last else PAIR + STATS, NREG), BF16),
            tuple(gathered),
            [VMEM] * len(gathered),
        )

    attended, reg_out = call(
        final_kernel,
        (
            jax.ShapeDtypeStruct((cells, channels), BF16),
            jax.ShapeDtypeStruct((NREG, channels), BF16),
        ),
        (mixed, factor, rest, reg_weights, payload, swap(payload, 1)),
        [VMEM] * 6,
        flops=2 * cells * NREG * channels * 2,
    )
    return attended.reshape(rows, cols, channels), reg_out


def solution(mesh):
    return jax.shard_map(
        shards,
        mesh=mesh,
        in_specs=(P("lat", "lon", None), P(None, "lat", "lon", None), P(), P(), P(), P()),
        out_specs=(P("lat", "lon", None), P()),
        check_vma=False,
    )
```

```python
import functools

import jax
import jax.numpy as jnp
from jax import lax
from jax.experimental import pallas as pl
from jax.experimental.pallas import tpu as pltpu
from jax.sharding import PartitionSpec as P

HEADS = 4
HEAD_DIM = 64
NREG = 256
RADIUS = 6
TILE = 8
PAIR = 2 * HEAD_DIM
DEEP = 8
STATS = 8
AUG = 128
MASKED = -8192.0
SCALE = HEAD_DIM ** (-0.5)

BF16 = jnp.bfloat16
F32 = jnp.float32
NT = (((1,), (1,)), ((), ()))
TN = (((0,), (0,)), ((), ()))
VMEM = pl.BlockSpec(memory_space=pltpu.VMEM)
HBM = pl.BlockSpec(memory_space=pltpu.HBM)


def dot(a, b, dims):
    return lax.dot_general(a, b, dims, preferred_element_type=F32)


def place():
    count = lax.axis_size("lon") * lax.axis_size("lat")
    flat = lax.axis_index("lon") * lax.axis_size("lat") + lax.axis_index("lat")
    return [(flat >> b) & 1 for b in range(count.bit_length() - 1)]


def half():
    return functools.reduce(jnp.bitwise_xor, place())


def iota(shape, axis):
    return lax.broadcasted_iota(jnp.int32, shape, axis)


def call(kernel, out, args, specs, scratch=(), flops=0, limit=16):
    size = sum(a.size * a.dtype.itemsize for a in args)
    return pl.pallas_call(
        kernel,
        out_shape=out,
        in_specs=specs,
        out_specs=jax.tree.map(lambda _: VMEM, out),
        scratch_shapes=scratch,
        compiler_params=pltpu.CompilerParams(vmem_limit_bytes=limit * 2**20),
        cost_estimate=pl.CostEstimate(flops=flops, bytes_accessed=size, transcendentals=0),
    )(*args)


def pack(values, tops, sums):
    rows = iota((STATS, values.shape[1]), 0)
    stats = jnp.zeros((STATS, values.shape[1]), F32)
    for j in range(2):
        high = sums[j].astype(BF16).astype(F32)
        for row, value in ((j, tops[j]), (2 + 2 * j, high), (3 + 2 * j, sums[j] - high)):
            stats = jnp.where(rows == row, value, stats)
    return jnp.concatenate([values, stats], axis=0)


def sides_kernel(rows, cols, kv_ref, queries_ref, pole_ref, sea_ref, own, queries, near_ref, far_ref, closed_ref,
                 wide, pole, sea, sem):
    pairs = ((pole_ref, pole), (sea_ref, sea), (kv_ref, own), (queries_ref, queries))
    copies = [pltpu.make_async_copy(*pair, sem.at[k]) for k, pair in enumerate(pairs)]
    for copy in copies:
        copy.start()
    copies[0].wait()
    copies[1].wait()
    closed_ref[...] = jnp.broadcast_to(closed_tiles(rows, cols, pole, sea), closed_ref.shape)
    copies[2].wait()
    odd = lax.axis_index("lon") % 2 == 1
    for k in range(2):
        for lane in range(0, own.shape[2], 128):
            lanes = slice(lane, lane + 128)
            wide[: own.shape[1]] = own[k, :, lanes].astype(F32)
            for c in range(RADIUS):
                low = wide[pl.ds(c, rows, stride=cols)]
                high = wide[pl.ds(cols - RADIUS + c, rows, stride=cols)]
                near_ref[k, c * rows : (c + 1) * rows, lanes] = jnp.where(odd, low, high).astype(BF16)
                far_ref[k, c * rows : (c + 1) * rows, lanes] = jnp.where(odd, high, low).astype(BF16)
    copies[3].wait()


def register_kernel(own, other, queries, out_ref):
    lanes = pl.ds(pl.multiple_of(half() * PAIR, PAIR), PAIR)
    keys = jnp.concatenate([own[0, :, lanes], other[0, :, lanes]], axis=0)
    vals = jnp.concatenate([own[1, :, lanes], other[1, :, lanes]], axis=0)
    scaled = queries[:, lanes] * jnp.asarray(SCALE, BF16)
    first = iota(scaled.shape, 1) < HEAD_DIM
    asked = [jnp.where(first == (j == 0), scaled, jnp.zeros_like(scaled)) for j in range(2)]
    scores = [dot(keys, each, NT) for each in asked]
    ones = jnp.ones((keys.shape[0], HEAD_DIM), BF16)
    parts, tops, sums = [], [], []
    for j in range(2):
        top = jnp.max(scores[j], axis=0, keepdims=True).astype(BF16).astype(F32)
        tops.append(top)
        weights = jnp.exp(scores[j] - top).astype(BF16)
        both = dot(jnp.concatenate([vals[:, j * HEAD_DIM : (j + 1) * HEAD_DIM], ones], axis=1), weights, TN)
        parts.append(both[:HEAD_DIM])
        sums.append(both[HEAD_DIM : HEAD_DIM + 1])
    out_ref[...] = pack(jnp.concatenate(parts, axis=0), tops, sums).astype(BF16)


def merge_kernel(stages, last, *refs):
    payloads, out_ref = refs[:-1], refs[-1]
    here = place()
    found = [(r[:PAIR].astype(F32), r[PAIR:].astype(F32)) for r in payloads]
    for level, (first, second) in enumerate(zip(*stages)):
        swap = jnp.where(half() == 0, here[first], here[second]) == 1
        step = 1 << level
        for low in range(len(found)):
            if not low & step:
                a, b = found[low], found[low + step]
                found[low] = tuple(jnp.where(swap, v, u) for u, v in zip(a, b))
                found[low + step] = tuple(jnp.where(swap, u, v) for u, v in zip(a, b))
    upper = iota((PAIR, found[0][0].shape[1]), 0) < HEAD_DIM
    tops, sums, factors = [], [], []
    for j in range(2):
        each = [stats[j : j + 1] for _, stats in found]
        top = functools.reduce(jnp.maximum, each)
        factor = [jnp.exp(e - top) for e in each]
        totals = [
            f * (stats[2 + 2 * j : 3 + 2 * j] + stats[3 + 2 * j : 4 + 2 * j])
            for f, (_, stats) in zip(factor, found)
        ]
        tops.append(top)
        sums.append(functools.reduce(jnp.add, totals))
        factors.append(factor)
    merged = functools.reduce(
        jnp.add,
        [values * jnp.where(upper, f, g) for f, g, (values, _) in zip(*factors, found)],
    )
    if last:
        out_ref[...] = (merged / jnp.where(upper, sums[0], sums[1])).astype(BF16)
    else:
        out_ref[...] = pack(merged, tops, sums).astype(BF16)


def segments(rows, cols):
    inner = (
        (rows, cols, False, 0, 0),
        (RADIUS, cols, False, "core", 0),
    )
    outer = (
        (RADIUS, rows, True, 0, "a"),
        (RADIUS, rows, True, 0, "b"),
        (RADIUS, DEEP, True, "core deep", "a"),
        (RADIUS, DEEP, True, "core deep", "b"),
        (RADIUS, cols, False, "cross", 0),
        (RADIUS, DEEP, True, "cross deep", "a"),
        (RADIUS, DEEP, True, "cross deep", "b"),
    )
    return inner, outer


def count(parts):
    return sum(part[0] * part[1] for part in parts)


def closed_tiles(rows, cols, pole, sea):
    lat, lon = lax.axis_index("lat"), lax.axis_index("lon")
    bands, tiles = sea.shape
    down, across = rows // TILE, cols // TILE
    lane = iota((1, AUG), 1)
    closed = jnp.zeros((1, AUG), F32)
    for i in range(down + 2):
        band = lat * down - 1 + i
        inside = (band >= 0) & (band < bands)
        band = jnp.clip(band, 0, bands - 1)
        for j in range(across + 2):
            tile = (lon * across - 1 + j + tiles) % tiles
            kept = inside & (pole[band] * sea[band, tile] > 0)
            at = rows + cols + i * (across + 2) + j
            closed = jnp.where(lane == at, jnp.where(kept, 0.0, MASKED), closed)
    return closed


def masks(rows, cols, closed, parts):
    lat, lon = lax.axis_index("lat"), lax.axis_index("lon")
    across = cols // TILE
    lat_odd, lon_odd = lat % 2 == 1, lon % 2 == 1
    starts = {
        0: 0,
        "core": jnp.where(lat_odd, -RADIUS, rows),
        "core deep": jnp.where(lat_odd, -DEEP, rows),
        "cross": jnp.where(lat_odd, rows, -RADIUS),
        "cross deep": jnp.where(lat_odd, rows, -DEEP),
        "a": jnp.where(lon_odd, -RADIUS, cols),
        "b": jnp.where(lon_odd, cols, -RADIUS),
    }
    lane = iota((1, AUG), 1)
    for slow, fast, fast_rows, row, col in parts:
        index = iota((slow * fast, AUG), 0)
        outer, inner = index >> (fast.bit_length() - 1), index & (fast - 1)
        row = starts[row] + (inner if fast_rows else outer)
        col = starts[col] + (outer if fast_rows else inner)
        apart = jnp.where(lane < rows, lane - row, lane - rows - col)
        far = (lane < rows + cols) & (jnp.abs(apart) > RADIUS)
        cell = ((row + TILE) >> 3) * (across + 2) + ((col + TILE) >> 3)
        value = jnp.where(lane - (rows + cols) == cell, closed, 0.0)
        yield jnp.where(far, MASKED, value).astype(BF16)


def fill(kbuf, vbuf, blocks, mask_blocks):
    ahead = kbuf.shape[1] - vbuf.shape[0]
    offset = 0
    for keys, vals in blocks:
        end = offset + keys.shape[0]
        for p in range(2):
            kbuf[p, ahead + offset : ahead + end, :PAIR] = keys[:, p * PAIR : (p + 1) * PAIR]
        vbuf[offset:end] = vals
        offset = end
    offset = ahead
    for mask in mask_blocks:
        for p in range(2):
            kbuf[p, offset : offset + mask.shape[0], PAIR:] = mask
        offset += mask.shape[0]


def attend(rows, cols, q_ref, kbuf, vbuf):
    size, ahead = rows * cols, kbuf.shape[1] - vbuf.shape[0]
    query = iota((size, AUG), 0)
    lane = iota((size, AUG), 1)
    tiles = (rows // TILE + 2) * (cols // TILE + 2)
    hot = (lane == query >> (cols.bit_length() - 1)) | (lane - rows == query & (cols - 1))
    hot = hot | ((lane >= rows + cols) & (lane < rows + cols + tiles))
    hot = jnp.where(hot, 1.0, 0.0).astype(BF16)
    first = iota((size, PAIR), 1) < HEAD_DIM
    scores = []
    for p in range(2):
        scaled = q_ref[:, p * PAIR : (p + 1) * PAIR] * jnp.asarray(SCALE, BF16)
        for j in range(2):
            mine = jnp.where(first == (j == 0), scaled, jnp.zeros_like(scaled))
            scores.append(dot(jnp.concatenate([mine, hot], axis=1), kbuf[p], NT))
    for p in range(2):
        lanes = slice(p * PAIR, (p + 1) * PAIR)
        tops, totals, mixed, weights = [], [], [], []
        for each in scores[2 * p : 2 * p + 2]:
            top = jnp.max(each, axis=1, keepdims=True)
            each = jnp.exp(each - top)
            tops.append(top)
            totals.append(jnp.sum(each, axis=1, keepdims=True))
            weights.append(each.astype(BF16))
            mixed.append(jnp.dot(weights[-1][:, ahead:], vbuf[:, lanes], preferred_element_type=F32))
        yield p, lanes, *(jnp.where(first, *x) for x in (tops, totals, mixed)), weights


def inner_kernel(rows, cols, q_ref, own, core, reg_keys, closed_ref,
                 mixed_ref, top_ref, total_ref, reg_ref, kbuf, vbuf):
    first = jnp.where(lax.axis_index("lat") % 2 == 0, 0, (rows - RADIUS) * cols)
    taken = pl.ds(pl.multiple_of(first, 16), RADIUS * cols)
    blocks = [(own[0], own[1]), (core[0, taken], core[1, taken])]
    fill(kbuf, vbuf, blocks, masks(rows, cols, closed_ref[:1], segments(rows, cols)[0]))
    for p in range(2):
        kbuf[p, :NREG, :PAIR] = reg_keys[:, p * PAIR : (p + 1) * PAIR]
        kbuf[p, :NREG, PAIR:] = jnp.zeros((NREG, AUG), BF16)
    for p, lanes, top, total, mixed, weights in attend(rows, cols, q_ref, kbuf, vbuf):
        top_ref[:, lanes], total_ref[:, lanes], mixed_ref[:, lanes] = top, total, mixed
        for j in range(2):
            reg_ref[2 * p + j] = weights[j][:, :NREG]


def outer_kernel(rows, cols, q_ref, a, b, corner, cross, inner_top, inner_total, closed_ref,
                 rest_ref, factor_ref, kbuf, vbuf):
    blocks = [(ref[0], ref[1]) for ref in (a, b, corner, cross)]
    fill(kbuf, vbuf, blocks, masks(rows, cols, closed_ref[:1], segments(rows, cols)[1]))
    for _, lanes, top, total, mixed, _ in attend(rows, cols, q_ref, kbuf, vbuf):
        highest = jnp.maximum(top, inner_top[:, lanes])
        inner, outer = jnp.exp(inner_top[:, lanes] - highest), jnp.exp(top - highest)
        scale = 1.0 / (inner * inner_total[:, lanes] + outer * total)
        factor_ref[:, lanes] = inner * scale
        rest_ref[:, lanes] = mixed * (outer * scale)


def final_kernel(inner, factor, rest, reg_weights, mine, other, out_ref, reg_out_ref):
    here = half() == 0
    first = iota((inner.shape[0], PAIR), 1) < HEAD_DIM
    for p in range(2):
        lanes = slice(p * PAIR, (p + 1) * PAIR)
        vals = jnp.where(here == (p == 0), mine[...], other[...])
        added = jnp.where(first, dot(reg_weights[2 * p], vals, NT), dot(reg_weights[2 * p + 1], vals, NT))
        out_ref[:, lanes] = ((inner[:, lanes] + added) * factor[:, lanes] + rest[:, lanes]).astype(BF16)
        reg_out_ref[:, lanes] = vals.astype(F32).T.astype(BF16)


def shards(queries, key_values, pole_mask, sea_mask, reg_queries, reg_keys):
    rows, cols, channels = queries.shape
    lats, lons = lax.axis_size("lat"), lax.axis_size("lon")
    devices = lats * lons
    assert lats == 4 and lons & (lons - 1) == 0 and lons > 1
    assert rows & (rows - 1) == 0 and cols & (cols - 1) == 0 and rows % TILE == 0 and cols % TILE == 0 and TILE == DEEP == 8
    nbits = devices.bit_length() - 1
    assert nbits % 2 == 1
    lat = lax.axis_index("lat")
    everyone = ("lon", "lat")

    def swap(x, mask):
        return lax.ppermute(x, everyone, [(i, i ^ mask) for i in range(devices)])

    cells = rows * cols
    key_values = key_values.reshape(2, cells, channels)
    core = swap(key_values, 1)

    side = jax.ShapeDtypeStruct((2, RADIUS * rows, channels), BF16)
    inputs = (key_values, reg_queries, pole_mask, sea_mask)
    own, reg_queries, near_cols, far_cols, closed = call(
        functools.partial(sides_kernel, rows, cols),
        (
            jax.ShapeDtypeStruct(key_values.shape, BF16),
            jax.ShapeDtypeStruct(reg_queries.shape, BF16),
            side,
            side,
            jax.ShapeDtypeStruct((8, AUG), F32),
        ),
        tuple(pltpu.with_memory_space_constraint(x, pltpu.HBM) for x in inputs),
        [HBM] * 4,
        scratch=[
            pltpu.VMEM((cells + cols, 128), F32),
            pltpu.SMEM(pole_mask.shape, jnp.int32),
            pltpu.SMEM(sea_mask.shape, jnp.int32),
            pltpu.SemaphoreType.DMA((4,)),
        ],
    )


    side_b = lax.ppermute(
        far_cols, "lon", [(i, (i + 1 if i % 2 else i - 1) % lons) for i in range(lons)]
    )
    near_cols, _ = lax.optimization_barrier((near_cols, core))
    side_a = swap(near_cols, lats)

    payload = call(
        register_kernel,
        jax.ShapeDtypeStruct((PAIR + STATS, NREG), BF16),
        (own, core, reg_queries),
        [VMEM] * 3,
        flops=4 * 2 * cells * NREG * 2 * PAIR,
    )

    queries = queries.reshape(cells, channels)
    square = jax.ShapeDtypeStruct((cells, channels), F32)
    inner, outer = (count(parts) for parts in segments(rows, cols))
    mixed, top, total, reg_weights = call(
        functools.partial(inner_kernel, rows, cols),
        (square, square, square, jax.ShapeDtypeStruct((HEADS, cells, NREG), BF16)),
        (queries, own, core, reg_keys, closed),
        [VMEM] * 5,
        scratch=[
            pltpu.VMEM((2, inner + NREG, PAIR + AUG), BF16),
            pltpu.VMEM((inner, channels), BF16),
        ],
        flops=2 * 2 * cells * inner * channels * 2,
    )

    corner_a, corner_b, _ = lax.optimization_barrier((side_a, side_b, payload))
    side_a, side_b, _, _ = lax.optimization_barrier((side_a, side_b, payload, mixed))

    def take(shard, size, start, count):
        taken = lax.dynamic_slice_in_dim(shard.reshape(2, -1, size, channels), start, count, 2)
        return taken.reshape(2, -1, channels)

    core_deep, cross_deep = (1 - lat % 2) * (rows - DEEP), (lat % 2) * (rows - DEEP)
    corner = swap(
        jnp.concatenate([take(s, rows, core_deep, DEEP) for s in (corner_a, corner_b)], axis=1), 1
    )
    cross = lax.ppermute(
        jnp.concatenate(
            [
                take(own, cells, (lat % 2) * (rows - RADIUS) * cols, RADIUS * cols),
                *[take(s, rows, cross_deep, DEEP) for s in (side_a, side_b)],
            ],
            axis=1,
        ),
        everyone,
        [(i, i ^ 3 if i % lats in (1, 2) else i ^ lats) for i in range(devices)],
    )
    rest, factor = call(
        functools.partial(outer_kernel, rows, cols),
        (square, square),
        (queries, side_a, side_b, corner, cross, top, total, closed),
        [VMEM] * 8,
        scratch=[pltpu.VMEM((2, outer, PAIR + AUG), BF16), pltpu.VMEM((outer, channels), BF16)],
        flops=2 * 2 * cells * outer * channels * 2,
    )

    near_bits, far_bits = (1, 2), [(b, b + 1) for b in range(3, nbits, 2)]
    steps = list(zip([*far_bits, near_bits], [near_bits, *far_bits]))
    for step in steps:
        first, last = step is steps[0], step is steps[-1]
        gathered = [payload]
        for slot in range(3):
            pairs = []
            for i in range(devices):
                stage = step[bin(i).count("1") % 2]
                chosen = ((1, 2, 3) if stage == near_bits else (1, 2, 3))[slot]
                flips = [b for k, b in enumerate(stage) if chosen >> k & 1]
                pairs.append((i, i ^ (sum(1 << b for b in flips) + len(flips) % 2)))
            gathered.append(lax.ppermute(payload, everyone, pairs))
        if first:
            gathered[0], _ = lax.optimization_barrier((gathered[0], mixed))
        if last:
            gathered[0], rest, factor = lax.optimization_barrier((gathered[0], rest, factor))
        payload = call(
            functools.partial(merge_kernel, step, last),
            jax.ShapeDtypeStruct((PAIR if last else PAIR + STATS, NREG), BF16),
            tuple(gathered),
            [VMEM] * len(gathered),
        )

    attended, reg_out = call(
        final_kernel,
        (
            jax.ShapeDtypeStruct((cells, channels), BF16),
            jax.ShapeDtypeStruct((NREG, channels), BF16),
        ),
        (mixed, factor, rest, reg_weights, payload, swap(payload, 1)),
        [VMEM] * 6,
        flops=2 * cells * NREG * channels * 2,
    )
    return attended.reshape(rows, cols, channels), reg_out


def solution(mesh):
    return jax.shard_map(
        shards,
        mesh=mesh,
        in_specs=(P("lat", "lon", None), P(None, "lat", "lon", None), P(), P(), P(), P()),
        out_specs=(P("lat", "lon", None), P()),
        check_vma=False,
    )
```

```python
import functools

import jax
import jax.numpy as jnp
from jax import lax
from jax.experimental import pallas as pl
from jax.experimental.pallas import tpu as pltpu
from jax.sharding import PartitionSpec as P

HEADS = 4
HEAD_DIM = 64
NREG = 256
RADIUS = 6
TILE = 8
PAIR = 2 * HEAD_DIM
DEEP = 8
STATS = 8
AUG = 128
MASKED = -8192.0
SCALE = HEAD_DIM ** (-0.5)

BF16 = jnp.bfloat16
F32 = jnp.float32
NT = (((1,), (1,)), ((), ()))
TN = (((0,), (0,)), ((), ()))
VMEM = pl.BlockSpec(memory_space=pltpu.VMEM)
HBM = pl.BlockSpec(memory_space=pltpu.HBM)


def dot(a, b, dims):
    return lax.dot_general(a, b, dims, preferred_element_type=F32)


def place():
    count = lax.axis_size("lon") * lax.axis_size("lat")
    flat = lax.axis_index("lon") * lax.axis_size("lat") + lax.axis_index("lat")
    return [(flat >> b) & 1 for b in range(count.bit_length() - 1)]


def half():
    return functools.reduce(jnp.bitwise_xor, place())


def iota(shape, axis):
    return lax.broadcasted_iota(jnp.int32, shape, axis)


def call(kernel, out, args, specs, scratch=(), flops=0, limit=16):
    size = sum(a.size * a.dtype.itemsize for a in args)
    return pl.pallas_call(
        kernel,
        out_shape=out,
        in_specs=specs,
        out_specs=jax.tree.map(lambda _: VMEM, out),
        scratch_shapes=scratch,
        compiler_params=pltpu.CompilerParams(vmem_limit_bytes=limit * 2**20),
        cost_estimate=pl.CostEstimate(flops=flops, bytes_accessed=size, transcendentals=0),
    )(*args)


def pack(values, tops, sums):
    rows = iota((STATS, values.shape[1]), 0)
    stats = jnp.zeros((STATS, values.shape[1]), F32)
    for j in range(2):
        high = sums[j].astype(BF16).astype(F32)
        for row, value in ((j, tops[j]), (2 + 2 * j, high), (3 + 2 * j, sums[j] - high)):
            stats = jnp.where(rows == row, value, stats)
    return jnp.concatenate([values, stats], axis=0)


def sides_kernel(rows, cols, kv_ref, queries_ref, pole_ref, sea_ref, own, queries, near_ref, far_ref, closed_ref,
                 wide, pole, sea, sem):
    pairs = ((pole_ref, pole), (sea_ref, sea), (kv_ref, own), (queries_ref, queries))
    copies = [pltpu.make_async_copy(*pair, sem.at[k]) for k, pair in enumerate(pairs)]
    for copy in copies:
        copy.start()
    copies[0].wait()
    copies[1].wait()
    closed_ref[...] = jnp.broadcast_to(closed_tiles(rows, cols, pole, sea), closed_ref.shape)
    copies[2].wait()
    odd = lax.axis_index("lon") % 2 == 1
    for k in range(2):
        for lane in range(0, own.shape[2], 128):
            lanes = slice(lane, lane + 128)
            wide[: own.shape[1]] = own[k, :, lanes].astype(F32)
            for c in range(RADIUS):
                low = wide[pl.ds(c, rows, stride=cols)]
                high = wide[pl.ds(cols - RADIUS + c, rows, stride=cols)]
                near_ref[k, c * rows : (c + 1) * rows, lanes] = jnp.where(odd, low, high).astype(BF16)
                far_ref[k, c * rows : (c + 1) * rows, lanes] = jnp.where(odd, high, low).astype(BF16)
    copies[3].wait()


def register_kernel(own, other, queries, out_ref):
    lanes = pl.ds(pl.multiple_of(half() * PAIR, PAIR), PAIR)
    keys = jnp.concatenate([own[0, :, lanes], other[0, :, lanes]], axis=0)
    vals = jnp.concatenate([own[1, :, lanes], other[1, :, lanes]], axis=0)
    scaled = queries[:, lanes] * jnp.asarray(SCALE, BF16)
    first = iota(scaled.shape, 1) < HEAD_DIM
    asked = [jnp.where(first == (j == 0), scaled, jnp.zeros_like(scaled)) for j in range(2)]
    scores = [dot(keys, each, NT) for each in asked]
    ones = jnp.ones((keys.shape[0], HEAD_DIM), BF16)
    parts, tops, sums = [], [], []
    for j in range(2):
        top = jnp.max(scores[j], axis=0, keepdims=True).astype(BF16).astype(F32)
        tops.append(top)
        weights = jnp.exp(scores[j] - top).astype(BF16)
        both = dot(jnp.concatenate([vals[:, j * HEAD_DIM : (j + 1) * HEAD_DIM], ones], axis=1), weights, TN)
        parts.append(both[:HEAD_DIM])
        sums.append(both[HEAD_DIM : HEAD_DIM + 1])
    out_ref[...] = pack(jnp.concatenate(parts, axis=0), tops, sums).astype(BF16)


def merge_kernel(stages, last, *refs):
    payloads, out_ref = refs[:-1], refs[-1]
    here = place()
    found = [(r[:PAIR].astype(F32), r[PAIR:].astype(F32)) for r in payloads]
    for level, (first, second) in enumerate(zip(*stages)):
        swap = jnp.where(half() == 0, here[first], here[second]) == 1
        step = 1 << level
        for low in range(len(found)):
            if not low & step:
                a, b = found[low], found[low + step]
                found[low] = tuple(jnp.where(swap, v, u) for u, v in zip(a, b))
                found[low + step] = tuple(jnp.where(swap, u, v) for u, v in zip(a, b))
    upper = iota((PAIR, found[0][0].shape[1]), 0) < HEAD_DIM
    tops, sums, factors = [], [], []
    for j in range(2):
        each = [stats[j : j + 1] for _, stats in found]
        top = functools.reduce(jnp.maximum, each)
        factor = [jnp.exp(e - top) for e in each]
        totals = [
            f * (stats[2 + 2 * j : 3 + 2 * j] + stats[3 + 2 * j : 4 + 2 * j])
            for f, (_, stats) in zip(factor, found)
        ]
        tops.append(top)
        sums.append(functools.reduce(jnp.add, totals))
        factors.append(factor)
    merged = functools.reduce(
        jnp.add,
        [values * jnp.where(upper, f, g) for f, g, (values, _) in zip(*factors, found)],
    )
    if last:
        out_ref[...] = (merged / jnp.where(upper, sums[0], sums[1])).astype(BF16)
    else:
        out_ref[...] = pack(merged, tops, sums).astype(BF16)


def segments(rows, cols):
    inner = (
        (rows, cols, False, 0, 0),
        (RADIUS, cols, False, "core", 0),
    )
    outer = (
        (RADIUS, rows, True, 0, "a"),
        (RADIUS, rows, True, 0, "b"),
        (RADIUS, DEEP, True, "core deep", "a"),
        (RADIUS, DEEP, True, "core deep", "b"),
        (RADIUS, cols, False, "cross", 0),
        (RADIUS, DEEP, True, "cross deep", "a"),
        (RADIUS, DEEP, True, "cross deep", "b"),
    )
    return inner, outer


def count(parts):
    return sum(part[0] * part[1] for part in parts)


def closed_tiles(rows, cols, pole, sea):
    lat, lon = lax.axis_index("lat"), lax.axis_index("lon")
    bands, tiles = sea.shape
    down, across = rows // TILE, cols // TILE
    lane = iota((1, AUG), 1)
    closed = jnp.zeros((1, AUG), F32)
    for i in range(down + 2):
        band = lat * down - 1 + i
        inside = (band >= 0) & (band < bands)
        band = jnp.clip(band, 0, bands - 1)
        for j in range(across + 2):
            tile = (lon * across - 1 + j + tiles) % tiles
            kept = inside & (pole[band] * sea[band, tile] > 0)
            at = rows + cols + i * (across + 2) + j
            closed = jnp.where(lane == at, jnp.where(kept, 0.0, MASKED), closed)
    return closed


def masks(rows, cols, closed, parts):
    lat, lon = lax.axis_index("lat"), lax.axis_index("lon")
    across = cols // TILE
    lat_odd, lon_odd = lat % 2 == 1, lon % 2 == 1
    starts = {
        0: 0,
        "core": jnp.where(lat_odd, -RADIUS, rows),
        "core deep": jnp.where(lat_odd, -DEEP, rows),
        "cross": jnp.where(lat_odd, rows, -RADIUS),
        "cross deep": jnp.where(lat_odd, rows, -DEEP),
        "a": jnp.where(lon_odd, -RADIUS, cols),
        "b": jnp.where(lon_odd, cols, -RADIUS),
    }
    lane = iota((1, AUG), 1)
    for slow, fast, fast_rows, row, col in parts:
        index = iota((slow * fast, AUG), 0)
        outer, inner = index >> (fast.bit_length() - 1), index & (fast - 1)
        row = starts[row] + (inner if fast_rows else outer)
        col = starts[col] + (outer if fast_rows else inner)
        apart = jnp.where(lane < rows, lane - row, lane - rows - col)
        far = (lane < rows + cols) & (jnp.abs(apart) > RADIUS)
        cell = ((row + TILE) >> 3) * (across + 2) + ((col + TILE) >> 3)
        value = jnp.where(lane - (rows + cols) == cell, closed, 0.0)
        yield jnp.where(far, MASKED, value).astype(BF16)


def fill(kbuf, vbuf, blocks, mask_blocks):
    ahead = kbuf.shape[1] - vbuf.shape[0]
    offset = 0
    for keys, vals in blocks:
        end = offset + keys.shape[0]
        for p in range(2):
            kbuf[p, ahead + offset : ahead + end, :PAIR] = keys[:, p * PAIR : (p + 1) * PAIR]
        vbuf[offset:end] = vals
        offset = end
    offset = ahead
    for mask in mask_blocks:
        for p in range(2):
            kbuf[p, offset : offset + mask.shape[0], PAIR:] = mask
        offset += mask.shape[0]


def attend(rows, cols, q_ref, kbuf, vbuf):
    size, ahead = rows * cols, kbuf.shape[1] - vbuf.shape[0]
    query = iota((size, AUG), 0)
    lane = iota((size, AUG), 1)
    tiles = (rows // TILE + 2) * (cols // TILE + 2)
    hot = (lane == query >> (cols.bit_length() - 1)) | (lane - rows == query & (cols - 1))
    hot = hot | ((lane >= rows + cols) & (lane < rows + cols + tiles))
    hot = jnp.where(hot, 1.0, 0.0).astype(BF16)
    first = iota((size, PAIR), 1) < HEAD_DIM
    scores = []
    for p in range(2):
        scaled = q_ref[:, p * PAIR : (p + 1) * PAIR] * jnp.asarray(SCALE, BF16)
        for j in range(2):
            mine = jnp.where(first == (j == 0), scaled, jnp.zeros_like(scaled))
            scores.append(dot(jnp.concatenate([mine, hot], axis=1), kbuf[p], NT))
    for p in range(2):
        lanes = slice(p * PAIR, (p + 1) * PAIR)
        tops, totals, mixed, weights = [], [], [], []
        for each in scores[2 * p : 2 * p + 2]:
            top = jnp.max(each, axis=1, keepdims=True)
            each = jnp.exp(each - top)
            tops.append(top)
            totals.append(jnp.sum(each, axis=1, keepdims=True))
            weights.append(each.astype(BF16))
            mixed.append(jnp.dot(weights[-1][:, ahead:], vbuf[:, lanes], preferred_element_type=F32))
        yield p, lanes, *(jnp.where(first, *x) for x in (tops, totals, mixed)), weights


def inner_kernel(rows, cols, q_ref, own, core, reg_keys, closed_ref,
                 mixed_ref, top_ref, total_ref, reg_ref, kbuf, vbuf):
    first = jnp.where(lax.axis_index("lat") % 2 == 0, 0, (rows - RADIUS) * cols)
    taken = pl.ds(pl.multiple_of(first, 16), RADIUS * cols)
    blocks = [(own[0], own[1]), (core[0, taken], core[1, taken])]
    fill(kbuf, vbuf, blocks, masks(rows, cols, closed_ref[:1], segments(rows, cols)[0]))
    for p in range(2):
        kbuf[p, :NREG, :PAIR] = reg_keys[:, p * PAIR : (p + 1) * PAIR]
        kbuf[p, :NREG, PAIR:] = jnp.zeros((NREG, AUG), BF16)
    for p, lanes, top, total, mixed, weights in attend(rows, cols, q_ref, kbuf, vbuf):
        top_ref[:, lanes], total_ref[:, lanes], mixed_ref[:, lanes] = top, total, mixed
        for j in range(2):
            reg_ref[2 * p + j] = weights[j][:, :NREG]


def outer_kernel(rows, cols, q_ref, a, b, corner, cross, inner_top, inner_total, closed_ref,
                 rest_ref, factor_ref, kbuf, vbuf):
    blocks = [(ref[0], ref[1]) for ref in (a, b, corner, cross)]
    fill(kbuf, vbuf, blocks, masks(rows, cols, closed_ref[:1], segments(rows, cols)[1]))
    for _, lanes, top, total, mixed, _ in attend(rows, cols, q_ref, kbuf, vbuf):
        highest = jnp.maximum(top, inner_top[:, lanes])
        inner, outer = jnp.exp(inner_top[:, lanes] - highest), jnp.exp(top - highest)
        scale = 1.0 / (inner * inner_total[:, lanes] + outer * total)
        factor_ref[:, lanes] = inner * scale
        rest_ref[:, lanes] = mixed * (outer * scale)


def final_kernel(inner, factor, rest, reg_weights, mine, other, out_ref, reg_out_ref):
    here = half() == 0
    first = iota((inner.shape[0], PAIR), 1) < HEAD_DIM
    for p in range(2):
        lanes = slice(p * PAIR, (p + 1) * PAIR)
        vals = jnp.where(here == (p == 0), mine[...], other[...])
        added = jnp.where(first, dot(reg_weights[2 * p], vals, NT), dot(reg_weights[2 * p + 1], vals, NT))
        out_ref[:, lanes] = ((inner[:, lanes] + added) * factor[:, lanes] + rest[:, lanes]).astype(BF16)
        reg_out_ref[:, lanes] = vals.astype(F32).T.astype(BF16)


def shards(queries, key_values, pole_mask, sea_mask, reg_queries, reg_keys):
    rows, cols, channels = queries.shape
    lats, lons = lax.axis_size("lat"), lax.axis_size("lon")
    devices = lats * lons
    assert lats == 4 and lons & (lons - 1) == 0 and lons > 1
    assert rows & (rows - 1) == 0 and cols & (cols - 1) == 0 and rows % TILE == 0 and cols % TILE == 0 and TILE == DEEP == 8
    nbits = devices.bit_length() - 1
    assert nbits % 2 == 1
    lat = lax.axis_index("lat")
    everyone = ("lon", "lat")

    def swap(x, mask):
        return lax.ppermute(x, everyone, [(i, i ^ mask) for i in range(devices)])

    cells = rows * cols
    key_values = key_values.reshape(2, cells, channels)
    core = swap(key_values, 1)

    side = jax.ShapeDtypeStruct((2, RADIUS * rows, channels), BF16)
    inputs = (key_values, reg_queries, pole_mask, sea_mask)
    own, reg_queries, near_cols, far_cols, closed = call(
        functools.partial(sides_kernel, rows, cols),
        (
            jax.ShapeDtypeStruct(key_values.shape, BF16),
            jax.ShapeDtypeStruct(reg_queries.shape, BF16),
            side,
            side,
            jax.ShapeDtypeStruct((8, AUG), F32),
        ),
        tuple(pltpu.with_memory_space_constraint(x, pltpu.HBM) for x in inputs),
        [HBM] * 4,
        scratch=[
            pltpu.VMEM((cells + cols, 128), F32),
            pltpu.SMEM(pole_mask.shape, jnp.int32),
            pltpu.SMEM(sea_mask.shape, jnp.int32),
            pltpu.SemaphoreType.DMA((4,)),
        ],
    )
    side_b = lax.ppermute(
        far_cols, "lon", [(i, (i + 1 if i % 2 else i - 1) % lons) for i in range(lons)]
    )
    near_cols, _ = lax.optimization_barrier((near_cols, core))
    side_a = swap(near_cols, lats)

    payload = call(
        register_kernel,
        jax.ShapeDtypeStruct((PAIR + STATS, NREG), BF16),
        (own, core, reg_queries),
        [VMEM] * 3,
        flops=4 * 2 * cells * NREG * 2 * PAIR,
    )

    queries = queries.reshape(cells, channels)
    square = jax.ShapeDtypeStruct((cells, channels), F32)
    inner, outer = (count(parts) for parts in segments(rows, cols))
    mixed, top, total, reg_weights = call(
        functools.partial(inner_kernel, rows, cols),
        (square, square, square, jax.ShapeDtypeStruct((HEADS, cells, NREG), BF16)),
        (queries, own, core, reg_keys, closed),
        [VMEM] * 5,
        scratch=[
            pltpu.VMEM((2, inner + NREG, PAIR + AUG), BF16),
            pltpu.VMEM((inner, channels), BF16),
        ],
        flops=2 * 2 * cells * inner * channels * 2,
    )

    corner_a, corner_b, _ = lax.optimization_barrier((side_a, side_b, payload))
    side_a, side_b, _, _ = lax.optimization_barrier((side_a, side_b, payload, mixed))

    def take(shard, size, start, count):
        taken = lax.dynamic_slice_in_dim(shard.reshape(2, -1, size, channels), start, count, 2)
        return taken.reshape(2, -1, channels)

    core_deep, cross_deep = (1 - lat % 2) * (rows - DEEP), (lat % 2) * (rows - DEEP)
    corner = swap(
        jnp.concatenate([take(s, rows, core_deep, DEEP) for s in (corner_a, corner_b)], axis=1), 1
    )
    cross = lax.ppermute(
        jnp.concatenate(
            [
                take(own, cells, (lat % 2) * (rows - RADIUS) * cols, RADIUS * cols),
                *[take(s, rows, cross_deep, DEEP) for s in (side_a, side_b)],
            ],
            axis=1,
        ),
        everyone,
        [(i, i ^ 3 if i % lats in (1, 2) else i ^ lats) for i in range(devices)],
    )
    rest, factor = call(
        functools.partial(outer_kernel, rows, cols),
        (square, square),
        (queries, side_a, side_b, corner, cross, top, total, closed),
        [VMEM] * 8,
        scratch=[pltpu.VMEM((2, outer, PAIR + AUG), BF16), pltpu.VMEM((outer, channels), BF16)],
        flops=2 * 2 * cells * outer * channels * 2,
    )

    near_bits, far_bits = (1, 2), [(b, b + 1) for b in range(3, nbits, 2)]
    steps = list(zip([*far_bits, near_bits], [near_bits, *far_bits]))
    for step in steps:
        first, last = step is steps[0], step is steps[-1]
        gathered = [payload]
        for chosen in range(1, 4):
            pairs = []
            for i in range(devices):
                flips = [b for k, b in enumerate(step[bin(i).count("1") % 2]) if chosen >> k & 1]
                pairs.append((i, i ^ (sum(1 << b for b in flips) + len(flips) % 2)))
            gathered.append(lax.ppermute(payload, everyone, pairs))
        if first:
            gathered[0], _ = lax.optimization_barrier((gathered[0], mixed))
        if last:
            gathered[0], rest, factor = lax.optimization_barrier((gathered[0], rest, factor))
        payload = call(
            functools.partial(merge_kernel, step, last),
            jax.ShapeDtypeStruct((PAIR if last else PAIR + STATS, NREG), BF16),
            tuple(gathered),
            [VMEM] * len(gathered),
        )

    attended, reg_out = call(
        final_kernel,
        (
            jax.ShapeDtypeStruct((cells, channels), BF16),
            jax.ShapeDtypeStruct((NREG, channels), BF16),
        ),
        (mixed, factor, rest, reg_weights, payload, swap(payload, 1)),
        [VMEM] * 6,
        flops=2 * cells * NREG * channels * 2,
    )
    return attended.reshape(rows, cols, channels), reg_out


def solution(mesh):
    return jax.shard_map(
        shards,
        mesh=mesh,
        in_specs=(P("lat", "lon", None), P(None, "lat", "lon", None), P(), P(), P(), P()),
        out_specs=(P("lat", "lon", None), P()),
        check_vma=False,
    )
```

```python
import functools

import jax
import jax.numpy as jnp
from jax import lax
from jax.experimental import pallas as pl
from jax.experimental.pallas import tpu as pltpu
from jax.sharding import PartitionSpec as P

HEADS = 4
HEAD_DIM = 64
NREG = 256
RADIUS = 6
TILE = 8
PAIR = 2 * HEAD_DIM
DEEP = 8
STATS = 8
TURN = 2
AUG = 128
MASKED = -8192.0
SCALE = HEAD_DIM ** (-0.5)

BF16 = jnp.bfloat16
F32 = jnp.float32
NT = (((1,), (1,)), ((), ()))
TN = (((0,), (0,)), ((), ()))
VMEM = pl.BlockSpec(memory_space=pltpu.VMEM)
HBM = pl.BlockSpec(memory_space=pltpu.HBM)


def dot(a, b, dims):
    return lax.dot_general(a, b, dims, preferred_element_type=F32)


def place():
    count = lax.axis_size("lon") * lax.axis_size("lat")
    flat = lax.axis_index("lon") * lax.axis_size("lat") + lax.axis_index("lat")
    return [(flat >> b) & 1 for b in range(count.bit_length() - 1)]


def half():
    bits = place()
    return bits[0] ^ bits[TURN]


def iota(shape, axis):
    return lax.broadcasted_iota(jnp.int32, shape, axis)


def call(kernel, out, args, specs, scratch=(), flops=0, limit=16):
    size = sum(a.size * a.dtype.itemsize for a in args)
    return pl.pallas_call(
        kernel,
        out_shape=out,
        in_specs=specs,
        out_specs=jax.tree.map(lambda _: VMEM, out),
        scratch_shapes=scratch,
        compiler_params=pltpu.CompilerParams(vmem_limit_bytes=limit * 2**20),
        cost_estimate=pl.CostEstimate(flops=flops, bytes_accessed=size, transcendentals=0),
    )(*args)


def pack(values, tops, sums):
    rows = iota((STATS, values.shape[1]), 0)
    stats = jnp.zeros((STATS, values.shape[1]), F32)
    for j in range(2):
        high = sums[j].astype(BF16).astype(F32)
        for row, value in ((j, tops[j]), (2 + 2 * j, high), (3 + 2 * j, sums[j] - high)):
            stats = jnp.where(rows == row, value, stats)
    return jnp.concatenate([values, stats], axis=0)


def sides_kernel(rows, cols, kv_ref, queries_ref, pole_ref, sea_ref, own, queries, near_ref, far_ref, closed_ref,
                 wide, pole, sea, sem):
    pairs = ((pole_ref, pole), (sea_ref, sea), (kv_ref, own), (queries_ref, queries))
    copies = [pltpu.make_async_copy(*pair, sem.at[k]) for k, pair in enumerate(pairs)]
    for copy in copies:
        copy.start()
    copies[0].wait()
    copies[1].wait()
    closed_ref[...] = jnp.broadcast_to(closed_tiles(rows, cols, pole, sea), closed_ref.shape)
    copies[2].wait()
    odd = lax.axis_index("lon") % 2 == 1
    for k in range(2):
        for lane in range(0, own.shape[2], 128):
            lanes = slice(lane, lane + 128)
            wide[: own.shape[1]] = own[k, :, lanes].astype(F32)
            for c in range(RADIUS):
                low = wide[pl.ds(c, rows, stride=cols)]
                high = wide[pl.ds(cols - RADIUS + c, rows, stride=cols)]
                near_ref[k, c * rows : (c + 1) * rows, lanes] = jnp.where(odd, low, high).astype(BF16)
                far_ref[k, c * rows : (c + 1) * rows, lanes] = jnp.where(odd, high, low).astype(BF16)
    copies[3].wait()


def register_kernel(own, other, queries, out_ref):
    lanes = pl.ds(pl.multiple_of(half() * PAIR, PAIR), PAIR)
    keys = jnp.concatenate([own[0, :, lanes], other[0, :, lanes]], axis=0)
    vals = jnp.concatenate([own[1, :, lanes], other[1, :, lanes]], axis=0)
    scaled = queries[:, lanes] * jnp.asarray(SCALE, BF16)
    first = iota(scaled.shape, 1) < HEAD_DIM
    asked = [jnp.where(first == (j == 0), scaled, jnp.zeros_like(scaled)) for j in range(2)]
    scores = [dot(keys, each, NT) for each in asked]
    ones = jnp.ones((keys.shape[0], HEAD_DIM), BF16)
    parts, tops, sums = [], [], []
    for j in range(2):
        top = jnp.max(scores[j], axis=0, keepdims=True).astype(BF16).astype(F32)
        tops.append(top)
        weights = jnp.exp(scores[j] - top).astype(BF16)
        both = dot(jnp.concatenate([vals[:, j * HEAD_DIM : (j + 1) * HEAD_DIM], ones], axis=1), weights, TN)
        parts.append(both[:HEAD_DIM])
        sums.append(both[HEAD_DIM : HEAD_DIM + 1])
    out_ref[...] = pack(jnp.concatenate(parts, axis=0), tops, sums).astype(BF16)


def merge_kernel(stages, last, *refs):
    payloads, out_ref = refs[:-1], refs[-1]
    here = place()
    found = [(r[:PAIR].astype(F32), r[PAIR:].astype(F32)) for r in payloads]
    for level, (first, second) in enumerate(zip(*stages)):
        swap = jnp.where(half() == 0, here[first], here[second]) == 1
        step = 1 << level
        for low in range(len(found)):
            if not low & step:
                a, b = found[low], found[low + step]
                found[low] = tuple(jnp.where(swap, v, u) for u, v in zip(a, b))
                found[low + step] = tuple(jnp.where(swap, u, v) for u, v in zip(a, b))
    upper = iota((PAIR, found[0][0].shape[1]), 0) < HEAD_DIM
    tops, sums, factors = [], [], []
    for j in range(2):
        each = [stats[j : j + 1] for _, stats in found]
        top = functools.reduce(jnp.maximum, each)
        factor = [jnp.exp(e - top) for e in each]
        totals = [
            f * (stats[2 + 2 * j : 3 + 2 * j] + stats[3 + 2 * j : 4 + 2 * j])
            for f, (_, stats) in zip(factor, found)
        ]
        tops.append(top)
        sums.append(functools.reduce(jnp.add, totals))
        factors.append(factor)
    merged = functools.reduce(
        jnp.add,
        [values * jnp.where(upper, f, g) for f, g, (values, _) in zip(*factors, found)],
    )
    if last:
        out_ref[...] = (merged / jnp.where(upper, sums[0], sums[1])).astype(BF16)
    else:
        out_ref[...] = pack(merged, tops, sums).astype(BF16)


def segments(rows, cols):
    inner = (
        (rows, cols, False, 0, 0),
        (RADIUS, cols, False, "core", 0),
    )
    outer = (
        (RADIUS, rows, True, 0, "a"),
        (RADIUS, rows, True, 0, "b"),
        (RADIUS, DEEP, True, "core deep", "a"),
        (RADIUS, DEEP, True, "core deep", "b"),
        (RADIUS, cols, False, "cross", 0),
        (RADIUS, DEEP, True, "cross deep", "a"),
        (RADIUS, DEEP, True, "cross deep", "b"),
    )
    return inner, outer


def count(parts):
    return sum(part[0] * part[1] for part in parts)


def closed_tiles(rows, cols, pole, sea):
    lat, lon = lax.axis_index("lat"), lax.axis_index("lon")
    bands, tiles = sea.shape
    down, across = rows // TILE, cols // TILE
    lane = iota((1, AUG), 1)
    closed = jnp.zeros((1, AUG), F32)
    for i in range(down + 2):
        band = lat * down - 1 + i
        inside = (band >= 0) & (band < bands)
        band = jnp.clip(band, 0, bands - 1)
        for j in range(across + 2):
            tile = (lon * across - 1 + j + tiles) % tiles
            kept = inside & (pole[band] * sea[band, tile] > 0)
            at = rows + cols + i * (across + 2) + j
            closed = jnp.where(lane == at, jnp.where(kept, 0.0, MASKED), closed)
    return closed


def masks(rows, cols, closed, parts):
    lat, lon = lax.axis_index("lat"), lax.axis_index("lon")
    across = cols // TILE
    lat_odd, lon_odd = lat % 2 == 1, lon % 2 == 1
    starts = {
        0: 0,
        "core": jnp.where(lat_odd, -RADIUS, rows),
        "core deep": jnp.where(lat_odd, -DEEP, rows),
        "cross": jnp.where(lat_odd, rows, -RADIUS),
        "cross deep": jnp.where(lat_odd, rows, -DEEP),
        "a": jnp.where(lon_odd, -RADIUS, cols),
        "b": jnp.where(lon_odd, cols, -RADIUS),
    }
    lane = iota((1, AUG), 1)
    for slow, fast, fast_rows, row, col in parts:
        index = iota((slow * fast, AUG), 0)
        outer, inner = index >> (fast.bit_length() - 1), index & (fast - 1)
        row = starts[row] + (inner if fast_rows else outer)
        col = starts[col] + (outer if fast_rows else inner)
        apart = jnp.where(lane < rows, lane - row, lane - rows - col)
        far = (lane < rows + cols) & (jnp.abs(apart) > RADIUS)
        cell = ((row + TILE) >> 3) * (across + 2) + ((col + TILE) >> 3)
        value = jnp.where(lane - (rows + cols) == cell, closed, 0.0)
        yield jnp.where(far, MASKED, value).astype(BF16)


def fill(kbuf, vbuf, blocks, mask_blocks):
    ahead = kbuf.shape[1] - vbuf.shape[0]
    offset = 0
    for keys, vals in blocks:
        end = offset + keys.shape[0]
        for p in range(2):
            kbuf[p, ahead + offset : ahead + end, :PAIR] = keys[:, p * PAIR : (p + 1) * PAIR]
        vbuf[offset:end] = vals
        offset = end
    offset = ahead
    for mask in mask_blocks:
        for p in range(2):
            kbuf[p, offset : offset + mask.shape[0], PAIR:] = mask
        offset += mask.shape[0]


def attend(rows, cols, q_ref, kbuf, vbuf):
    size, ahead = rows * cols, kbuf.shape[1] - vbuf.shape[0]
    query = iota((size, AUG), 0)
    lane = iota((size, AUG), 1)
    tiles = (rows // TILE + 2) * (cols // TILE + 2)
    hot = (lane == query >> (cols.bit_length() - 1)) | (lane - rows == query & (cols - 1))
    hot = hot | ((lane >= rows + cols) & (lane < rows + cols + tiles))
    hot = jnp.where(hot, 1.0, 0.0).astype(BF16)
    first = iota((size, PAIR), 1) < HEAD_DIM
    scores = []
    for p in range(2):
        scaled = q_ref[:, p * PAIR : (p + 1) * PAIR] * jnp.asarray(SCALE, BF16)
        for j in range(2):
            mine = jnp.where(first == (j == 0), scaled, jnp.zeros_like(scaled))
            scores.append(dot(jnp.concatenate([mine, hot], axis=1), kbuf[p], NT))
    for p in range(2):
        lanes = slice(p * PAIR, (p + 1) * PAIR)
        tops, totals, mixed, weights = [], [], [], []
        for each in scores[2 * p : 2 * p + 2]:
            top = jnp.max(each, axis=1, keepdims=True)
            each = jnp.exp(each - top)
            tops.append(top)
            totals.append(jnp.sum(each, axis=1, keepdims=True))
            weights.append(each.astype(BF16))
            mixed.append(jnp.dot(weights[-1][:, ahead:], vbuf[:, lanes], preferred_element_type=F32))
        yield p, lanes, *(jnp.where(first, *x) for x in (tops, totals, mixed)), weights


def inner_kernel(rows, cols, q_ref, own, core, reg_keys, closed_ref,
                 mixed_ref, top_ref, total_ref, reg_ref, kbuf, vbuf):
    first = jnp.where(lax.axis_index("lat") % 2 == 0, 0, (rows - RADIUS) * cols)
    taken = pl.ds(pl.multiple_of(first, 16), RADIUS * cols)
    blocks = [(own[0], own[1]), (core[0, taken], core[1, taken])]
    fill(kbuf, vbuf, blocks, masks(rows, cols, closed_ref[:1], segments(rows, cols)[0]))
    for p in range(2):
        kbuf[p, :NREG, :PAIR] = reg_keys[:, p * PAIR : (p + 1) * PAIR]
        kbuf[p, :NREG, PAIR:] = jnp.zeros((NREG, AUG), BF16)
    for p, lanes, top, total, mixed, weights in attend(rows, cols, q_ref, kbuf, vbuf):
        top_ref[:, lanes], total_ref[:, lanes], mixed_ref[:, lanes] = top, total, mixed
        for j in range(2):
            reg_ref[2 * p + j] = weights[j][:, :NREG]


def outer_kernel(rows, cols, q_ref, a, b, corner, cross, inner_top, inner_total, closed_ref,
                 rest_ref, factor_ref, kbuf, vbuf):
    blocks = [(ref[0], ref[1]) for ref in (a, b, corner, cross)]
    fill(kbuf, vbuf, blocks, masks(rows, cols, closed_ref[:1], segments(rows, cols)[1]))
    for _, lanes, top, total, mixed, _ in attend(rows, cols, q_ref, kbuf, vbuf):
        highest = jnp.maximum(top, inner_top[:, lanes])
        inner, outer = jnp.exp(inner_top[:, lanes] - highest), jnp.exp(top - highest)
        scale = 1.0 / (inner * inner_total[:, lanes] + outer * total)
        factor_ref[:, lanes] = inner * scale
        rest_ref[:, lanes] = mixed * (outer * scale)


def final_kernel(inner, factor, rest, reg_weights, mine, other, out_ref, reg_out_ref):
    here = half() == 0
    first = iota((inner.shape[0], PAIR), 1) < HEAD_DIM
    for p in range(2):
        lanes = slice(p * PAIR, (p + 1) * PAIR)
        vals = jnp.where(here == (p == 0), mine[...], other[...])
        added = jnp.where(first, dot(reg_weights[2 * p], vals, NT), dot(reg_weights[2 * p + 1], vals, NT))
        out_ref[:, lanes] = ((inner[:, lanes] + added) * factor[:, lanes] + rest[:, lanes]).astype(BF16)
        reg_out_ref[:, lanes] = vals.astype(F32).T.astype(BF16)


def shards(queries, key_values, pole_mask, sea_mask, reg_queries, reg_keys):
    rows, cols, channels = queries.shape
    lats, lons = lax.axis_size("lat"), lax.axis_size("lon")
    devices = lats * lons
    assert lats == 4 and lons & (lons - 1) == 0 and lons > 1
    assert rows & (rows - 1) == 0 and cols & (cols - 1) == 0 and rows % TILE == 0 and cols % TILE == 0 and TILE == DEEP == 8
    nbits = devices.bit_length() - 1
    assert nbits % 2 == 1
    lat = lax.axis_index("lat")
    everyone = ("lon", "lat")

    def swap(x, mask):
        return lax.ppermute(x, everyone, [(i, i ^ mask) for i in range(devices)])

    cells = rows * cols
    key_values = key_values.reshape(2, cells, channels)
    core = swap(key_values, 1)

    side = jax.ShapeDtypeStruct((2, RADIUS * rows, channels), BF16)
    inputs = (key_values, reg_queries, pole_mask, sea_mask)
    own, reg_queries, near_cols, far_cols, closed = call(
        functools.partial(sides_kernel, rows, cols),
        (
            jax.ShapeDtypeStruct(key_values.shape, BF16),
            jax.ShapeDtypeStruct(reg_queries.shape, BF16),
            side,
            side,
            jax.ShapeDtypeStruct((8, AUG), F32),
        ),
        tuple(pltpu.with_memory_space_constraint(x, pltpu.HBM) for x in inputs),
        [HBM] * 4,
        scratch=[
            pltpu.VMEM((cells + cols, 128), F32),
            pltpu.SMEM(pole_mask.shape, jnp.int32),
            pltpu.SMEM(sea_mask.shape, jnp.int32),
            pltpu.SemaphoreType.DMA((4,)),
        ],
    )
    side_b = lax.ppermute(
        far_cols, "lon", [(i, (i + 1 if i % 2 else i - 1) % lons) for i in range(lons)]
    )
    near_cols, _ = lax.optimization_barrier((near_cols, core))
    side_a = swap(near_cols, lats)

    payload = call(
        register_kernel,
        jax.ShapeDtypeStruct((PAIR + STATS, NREG), BF16),
        (own, core, reg_queries),
        [VMEM] * 3,
        flops=4 * 2 * cells * NREG * 2 * PAIR,
    )

    queries = queries.reshape(cells, channels)
    square = jax.ShapeDtypeStruct((cells, channels), F32)
    inner, outer = (count(parts) for parts in segments(rows, cols))
    mixed, top, total, reg_weights = call(
        functools.partial(inner_kernel, rows, cols),
        (square, square, square, jax.ShapeDtypeStruct((HEADS, cells, NREG), BF16)),
        (queries, own, core, reg_keys, closed),
        [VMEM] * 5,
        scratch=[
            pltpu.VMEM((2, inner + NREG, PAIR + AUG), BF16),
            pltpu.VMEM((inner, channels), BF16),
        ],
        flops=2 * 2 * cells * inner * channels * 2,
    )

    corner_a, corner_b, _ = lax.optimization_barrier((side_a, side_b, payload))
    side_a, side_b, _, _ = lax.optimization_barrier((side_a, side_b, payload, mixed))

    def take(shard, size, start, count):
        taken = lax.dynamic_slice_in_dim(shard.reshape(2, -1, size, channels), start, count, 2)
        return taken.reshape(2, -1, channels)

    core_deep, cross_deep = (1 - lat % 2) * (rows - DEEP), (lat % 2) * (rows - DEEP)
    corner = swap(
        jnp.concatenate([take(s, rows, core_deep, DEEP) for s in (corner_a, corner_b)], axis=1), 1
    )
    cross = lax.ppermute(
        jnp.concatenate(
            [
                take(own, cells, (lat % 2) * (rows - RADIUS) * cols, RADIUS * cols),
                *[take(s, rows, cross_deep, DEEP) for s in (side_a, side_b)],
            ],
            axis=1,
        ),
        everyone,
        [(i, i ^ 3 if i % lats in (1, 2) else i ^ lats) for i in range(devices)],
    )
    rest, factor = call(
        functools.partial(outer_kernel, rows, cols),
        (square, square),
        (queries, side_a, side_b, corner, cross, top, total, closed),
        [VMEM] * 8,
        scratch=[pltpu.VMEM((2, outer, PAIR + AUG), BF16), pltpu.VMEM((outer, channels), BF16)],
        flops=2 * 2 * cells * outer * channels * 2,
    )

    near_bits, far_bits = (1, 2), [(b, b + 1) for b in range(3, nbits, 2)]
    steps = list(zip([*far_bits, near_bits], [near_bits, *far_bits]))
    for step in steps:
        first, last = step is steps[0], step is steps[-1]
        gathered = [payload]
        for chosen in range(1, 4):
            pairs = []
            for i in range(devices):
                flips = [b for k, b in enumerate(step[(i ^ i >> TURN) & 1]) if chosen >> k & 1]
                pairs.append((i, i ^ (sum(1 << b for b in flips) + (TURN in flips))))
            gathered.append(lax.ppermute(payload, everyone, pairs))
        if first:
            gathered[0], _ = lax.optimization_barrier((gathered[0], mixed))
        if last:
            gathered[0], rest, factor = lax.optimization_barrier((gathered[0], rest, factor))
        payload = call(
            functools.partial(merge_kernel, step, last),
            jax.ShapeDtypeStruct((PAIR if last else PAIR + STATS, NREG), BF16),
            tuple(gathered),
            [VMEM] * len(gathered),
        )

    attended, reg_out = call(
        final_kernel,
        (
            jax.ShapeDtypeStruct((cells, channels), BF16),
            jax.ShapeDtypeStruct((NREG, channels), BF16),
        ),
        (mixed, factor, rest, reg_weights, payload, swap(payload, 1)),
        [VMEM] * 6,
        flops=2 * cells * NREG * channels * 2,
    )
    return attended.reshape(rows, cols, channels), reg_out


def solution(mesh):
    return jax.shard_map(
        shards,
        mesh=mesh,
        in_specs=(P("lat", "lon", None), P(None, "lat", "lon", None), P(), P(), P(), P()),
        out_specs=(P("lat", "lon", None), P()),
        check_vma=False,
    )
```

```python
import functools

import jax
import jax.numpy as jnp
from jax import lax
from jax.experimental import pallas as pl
from jax.experimental.pallas import tpu as pltpu
from jax.sharding import PartitionSpec as P

HEADS = 4
HEAD_DIM = 64
NREG = 256
RADIUS = 6
TILE = 8
PAIR = 2 * HEAD_DIM
DEEP = 8
STATS = 8
NEAR = (1, 2)
TURN = 2
AUG = 128
MASKED = -8192.0
SCALE = HEAD_DIM ** (-0.5)

BF16 = jnp.bfloat16
F32 = jnp.float32
NT = (((1,), (1,)), ((), ()))
TN = (((0,), (0,)), ((), ()))
VMEM = pl.BlockSpec(memory_space=pltpu.VMEM)
HBM = pl.BlockSpec(memory_space=pltpu.HBM)


def dot(a, b, dims):
    return lax.dot_general(a, b, dims, preferred_element_type=F32)


def place():
    count = lax.axis_size("lon") * lax.axis_size("lat")
    flat = lax.axis_index("lon") * lax.axis_size("lat") + lax.axis_index("lat")
    return [(flat >> b) & 1 for b in range(count.bit_length() - 1)]


def half():
    bits = place()
    return bits[0] ^ bits[TURN]


def iota(shape, axis):
    return lax.broadcasted_iota(jnp.int32, shape, axis)


def call(kernel, out, args, specs, scratch=(), flops=0, limit=16):
    size = sum(a.size * a.dtype.itemsize for a in args)
    return pl.pallas_call(
        kernel,
        out_shape=out,
        in_specs=specs,
        out_specs=jax.tree.map(lambda _: VMEM, out),
        scratch_shapes=scratch,
        compiler_params=pltpu.CompilerParams(vmem_limit_bytes=limit * 2**20),
        cost_estimate=pl.CostEstimate(flops=flops, bytes_accessed=size, transcendentals=0),
    )(*args)


def pack(values, tops, sums):
    rows = iota((STATS, values.shape[1]), 0)
    stats = jnp.zeros((STATS, values.shape[1]), F32)
    for j in range(2):
        high = sums[j].astype(BF16).astype(F32)
        for row, value in ((j, tops[j]), (2 + 2 * j, high), (3 + 2 * j, sums[j] - high)):
            stats = jnp.where(rows == row, value, stats)
    return jnp.concatenate([values, stats], axis=0)


def sides_kernel(rows, cols, kv_ref, queries_ref, pole_ref, sea_ref, own, queries, near_ref, far_ref, closed_ref,
                 wide, pole, sea, sem):
    pairs = ((pole_ref, pole), (sea_ref, sea), (kv_ref, own), (queries_ref, queries))
    copies = [pltpu.make_async_copy(*pair, sem.at[k]) for k, pair in enumerate(pairs)]
    for copy in copies:
        copy.start()
    copies[0].wait()
    copies[1].wait()
    closed_ref[...] = jnp.broadcast_to(closed_tiles(rows, cols, pole, sea), closed_ref.shape)
    copies[2].wait()
    odd = lax.axis_index("lon") % 2 == 1
    for k in range(2):
        for lane in range(0, own.shape[2], 128):
            lanes = slice(lane, lane + 128)
            wide[: own.shape[1]] = own[k, :, lanes].astype(F32)
            for c in range(RADIUS):
                low = wide[pl.ds(c, rows, stride=cols)]
                high = wide[pl.ds(cols - RADIUS + c, rows, stride=cols)]
                near_ref[k, c * rows : (c + 1) * rows, lanes] = jnp.where(odd, low, high).astype(BF16)
                far_ref[k, c * rows : (c + 1) * rows, lanes] = jnp.where(odd, high, low).astype(BF16)
    copies[3].wait()


def register_kernel(own, other, queries, out_ref):
    lanes = pl.ds(pl.multiple_of(half() * PAIR, PAIR), PAIR)
    keys = jnp.concatenate([own[0, :, lanes], other[0, :, lanes]], axis=0)
    vals = jnp.concatenate([own[1, :, lanes], other[1, :, lanes]], axis=0)
    scaled = queries[:, lanes] * jnp.asarray(SCALE, BF16)
    first = iota(scaled.shape, 1) < HEAD_DIM
    asked = [jnp.where(first == (j == 0), scaled, jnp.zeros_like(scaled)) for j in range(2)]
    scores = [dot(keys, each, NT) for each in asked]
    ones = jnp.ones((keys.shape[0], HEAD_DIM), BF16)
    parts, tops, sums = [], [], []
    for j in range(2):
        top = jnp.max(scores[j], axis=0, keepdims=True).astype(BF16).astype(F32)
        tops.append(top)
        weights = jnp.exp(scores[j] - top).astype(BF16)
        both = dot(jnp.concatenate([vals[:, j * HEAD_DIM : (j + 1) * HEAD_DIM], ones], axis=1), weights, TN)
        parts.append(both[:HEAD_DIM])
        sums.append(both[HEAD_DIM : HEAD_DIM + 1])
    out_ref[...] = pack(jnp.concatenate(parts, axis=0), tops, sums).astype(BF16)


def merge_kernel(stages, last, *refs):
    payloads, out_ref = refs[:-1], refs[-1]
    here = place()
    found = [(r[:PAIR].astype(F32), r[PAIR:].astype(F32)) for r in payloads]

    def turned(bits):
        low, high = (here[b] for b in bits)
        return (low, high) if bits == NEAR else (high, low ^ high)

    for level, (first, second) in enumerate(zip(*map(turned, stages))):
        swap = jnp.where(half() == 0, first, second) == 1
        step = 1 << level
        for low in range(len(found)):
            if not low & step:
                a, b = found[low], found[low + step]
                found[low] = tuple(jnp.where(swap, v, u) for u, v in zip(a, b))
                found[low + step] = tuple(jnp.where(swap, u, v) for u, v in zip(a, b))
    upper = iota((PAIR, found[0][0].shape[1]), 0) < HEAD_DIM
    tops, sums, factors = [], [], []
    for j in range(2):
        each = [stats[j : j + 1] for _, stats in found]
        top = functools.reduce(jnp.maximum, each)
        factor = [jnp.exp(e - top) for e in each]
        totals = [
            f * (stats[2 + 2 * j : 3 + 2 * j] + stats[3 + 2 * j : 4 + 2 * j])
            for f, (_, stats) in zip(factor, found)
        ]
        tops.append(top)
        sums.append(functools.reduce(jnp.add, totals))
        factors.append(factor)
    merged = functools.reduce(
        jnp.add,
        [values * jnp.where(upper, f, g) for f, g, (values, _) in zip(*factors, found)],
    )
    if last:
        out_ref[...] = (merged / jnp.where(upper, sums[0], sums[1])).astype(BF16)
    else:
        out_ref[...] = pack(merged, tops, sums).astype(BF16)


def segments(rows, cols):
    inner = (
        (rows, cols, False, 0, 0),
        (RADIUS, cols, False, "core", 0),
    )
    outer = (
        (RADIUS, rows, True, 0, "a"),
        (RADIUS, rows, True, 0, "b"),
        (RADIUS, DEEP, True, "core deep", "a"),
        (RADIUS, DEEP, True, "core deep", "b"),
        (RADIUS, cols, False, "cross", 0),
        (RADIUS, DEEP, True, "cross deep", "a"),
        (RADIUS, DEEP, True, "cross deep", "b"),
    )
    return inner, outer


def count(parts):
    return sum(part[0] * part[1] for part in parts)


def closed_tiles(rows, cols, pole, sea):
    lat, lon = lax.axis_index("lat"), lax.axis_index("lon")
    bands, tiles = sea.shape
    down, across = rows // TILE, cols // TILE
    lane = iota((1, AUG), 1)
    closed = jnp.zeros((1, AUG), F32)
    for i in range(down + 2):
        band = lat * down - 1 + i
        inside = (band >= 0) & (band < bands)
        band = jnp.clip(band, 0, bands - 1)
        for j in range(across + 2):
            tile = (lon * across - 1 + j + tiles) % tiles
            kept = inside & (pole[band] * sea[band, tile] > 0)
            at = rows + cols + i * (across + 2) + j
            closed = jnp.where(lane == at, jnp.where(kept, 0.0, MASKED), closed)
    return closed


def masks(rows, cols, closed, parts):
    lat, lon = lax.axis_index("lat"), lax.axis_index("lon")
    across = cols // TILE
    lat_odd, lon_odd = lat % 2 == 1, lon % 2 == 1
    starts = {
        0: 0,
        "core": jnp.where(lat_odd, -RADIUS, rows),
        "core deep": jnp.where(lat_odd, -DEEP, rows),
        "cross": jnp.where(lat_odd, rows, -RADIUS),
        "cross deep": jnp.where(lat_odd, rows, -DEEP),
        "a": jnp.where(lon_odd, -RADIUS, cols),
        "b": jnp.where(lon_odd, cols, -RADIUS),
    }
    lane = iota((1, AUG), 1)
    for slow, fast, fast_rows, row, col in parts:
        index = iota((slow * fast, AUG), 0)
        outer, inner = index >> (fast.bit_length() - 1), index & (fast - 1)
        row = starts[row] + (inner if fast_rows else outer)
        col = starts[col] + (outer if fast_rows else inner)
        apart = jnp.where(lane < rows, lane - row, lane - rows - col)
        far = (lane < rows + cols) & (jnp.abs(apart) > RADIUS)
        cell = ((row + TILE) >> 3) * (across + 2) + ((col + TILE) >> 3)
        value = jnp.where(lane - (rows + cols) == cell, closed, 0.0)
        yield jnp.where(far, MASKED, value).astype(BF16)


def fill(kbuf, vbuf, blocks, mask_blocks):
    ahead = kbuf.shape[1] - vbuf.shape[0]
    offset = 0
    for keys, vals in blocks:
        end = offset + keys.shape[0]
        for p in range(2):
            kbuf[p, ahead + offset : ahead + end, :PAIR] = keys[:, p * PAIR : (p + 1) * PAIR]
        vbuf[offset:end] = vals
        offset = end
    offset = ahead
    for mask in mask_blocks:
        for p in range(2):
            kbuf[p, offset : offset + mask.shape[0], PAIR:] = mask
        offset += mask.shape[0]


def attend(rows, cols, q_ref, kbuf, vbuf):
    size, ahead = rows * cols, kbuf.shape[1] - vbuf.shape[0]
    query = iota((size, AUG), 0)
    lane = iota((size, AUG), 1)
    tiles = (rows // TILE + 2) * (cols // TILE + 2)
    hot = (lane == query >> (cols.bit_length() - 1)) | (lane - rows == query & (cols - 1))
    hot = hot | ((lane >= rows + cols) & (lane < rows + cols + tiles))
    hot = jnp.where(hot, 1.0, 0.0).astype(BF16)
    first = iota((size, PAIR), 1) < HEAD_DIM
    scores = []
    for p in range(2):
        scaled = q_ref[:, p * PAIR : (p + 1) * PAIR] * jnp.asarray(SCALE, BF16)
        for j in range(2):
            mine = jnp.where(first == (j == 0), scaled, jnp.zeros_like(scaled))
            scores.append(dot(jnp.concatenate([mine, hot], axis=1), kbuf[p], NT))
    for p in range(2):
        lanes = slice(p * PAIR, (p + 1) * PAIR)
        tops, totals, mixed, weights = [], [], [], []
        for each in scores[2 * p : 2 * p + 2]:
            top = jnp.max(each, axis=1, keepdims=True)
            each = jnp.exp(each - top)
            tops.append(top)
            totals.append(jnp.sum(each, axis=1, keepdims=True))
            weights.append(each.astype(BF16))
            mixed.append(jnp.dot(weights[-1][:, ahead:], vbuf[:, lanes], preferred_element_type=F32))
        yield p, lanes, *(jnp.where(first, *x) for x in (tops, totals, mixed)), weights


def inner_kernel(rows, cols, q_ref, own, core, reg_keys, closed_ref,
                 mixed_ref, top_ref, total_ref, reg_ref, kbuf, vbuf):
    first = jnp.where(lax.axis_index("lat") % 2 == 0, 0, (rows - RADIUS) * cols)
    taken = pl.ds(pl.multiple_of(first, 16), RADIUS * cols)
    blocks = [(own[0], own[1]), (core[0, taken], core[1, taken])]
    fill(kbuf, vbuf, blocks, masks(rows, cols, closed_ref[:1], segments(rows, cols)[0]))
    for p in range(2):
        kbuf[p, :NREG, :PAIR] = reg_keys[:, p * PAIR : (p + 1) * PAIR]
        kbuf[p, :NREG, PAIR:] = jnp.zeros((NREG, AUG), BF16)
    for p, lanes, top, total, mixed, weights in attend(rows, cols, q_ref, kbuf, vbuf):
        top_ref[:, lanes], total_ref[:, lanes], mixed_ref[:, lanes] = top, total, mixed
        for j in range(2):
            reg_ref[2 * p + j] = weights[j][:, :NREG]


def outer_kernel(rows, cols, q_ref, a, b, corner, cross, inner_top, inner_total, closed_ref,
                 rest_ref, factor_ref, kbuf, vbuf):
    blocks = [(ref[0], ref[1]) for ref in (a, b, corner, cross)]
    fill(kbuf, vbuf, blocks, masks(rows, cols, closed_ref[:1], segments(rows, cols)[1]))
    for _, lanes, top, total, mixed, _ in attend(rows, cols, q_ref, kbuf, vbuf):
        highest = jnp.maximum(top, inner_top[:, lanes])
        inner, outer = jnp.exp(inner_top[:, lanes] - highest), jnp.exp(top - highest)
        scale = 1.0 / (inner * inner_total[:, lanes] + outer * total)
        factor_ref[:, lanes] = inner * scale
        rest_ref[:, lanes] = mixed * (outer * scale)


def shares(inner, factor, rest, reg_weights, vals, which):
    lanes = pl.ds(pl.multiple_of(which * PAIR, PAIR), PAIR)
    first = iota((inner.shape[0], PAIR), 1) < HEAD_DIM
    added = [dot(reg_weights[2 * which + j], vals, NT) for j in range(2)]
    return (inner[:, lanes] + jnp.where(first, *added)) * factor[:, lanes] + rest[:, lanes]


def own_share_kernel(inner, factor, rest, reg_weights, mine, out_ref, reg_out_ref):
    out_ref[...] = shares(inner, factor, rest, reg_weights, mine[...], half()).astype(BF16)
    reg_out_ref[...] = mine[...].astype(F32).T.astype(BF16)


def final_kernel(inner, factor, rest, reg_weights, own_out, own_reg_out, other, out_ref, reg_out_ref):
    which = half()
    own = pl.ds(pl.multiple_of(which * PAIR, PAIR), PAIR)
    lanes = pl.ds(pl.multiple_of((1 - which) * PAIR, PAIR), PAIR)
    out_ref[:, own] = own_out[...]
    reg_out_ref[:, own] = own_reg_out[...]
    out_ref[:, lanes] = shares(inner, factor, rest, reg_weights, other[...], 1 - which).astype(BF16)
    reg_out_ref[:, lanes] = other[...].astype(F32).T.astype(BF16)


def shards(queries, key_values, pole_mask, sea_mask, reg_queries, reg_keys):
    rows, cols, channels = queries.shape
    lats, lons = lax.axis_size("lat"), lax.axis_size("lon")
    devices = lats * lons
    assert lats == 4 and lons & (lons - 1) == 0 and lons > 1
    assert rows & (rows - 1) == 0 and cols & (cols - 1) == 0 and rows % TILE == 0 and cols % TILE == 0 and TILE == DEEP == 8
    nbits = devices.bit_length() - 1
    assert nbits % 2 == 1
    lat = lax.axis_index("lat")
    everyone = ("lon", "lat")

    def swap(x, mask):
        return lax.ppermute(x, everyone, [(i, i ^ mask) for i in range(devices)])

    cells = rows * cols
    key_values = key_values.reshape(2, cells, channels)
    core = swap(key_values, 1)

    side = jax.ShapeDtypeStruct((2, RADIUS * rows, channels), BF16)
    inputs = (key_values, reg_queries, pole_mask, sea_mask)
    own, reg_queries, near_cols, far_cols, closed = call(
        functools.partial(sides_kernel, rows, cols),
        (
            jax.ShapeDtypeStruct(key_values.shape, BF16),
            jax.ShapeDtypeStruct(reg_queries.shape, BF16),
            side,
            side,
            jax.ShapeDtypeStruct((8, AUG), F32),
        ),
        tuple(pltpu.with_memory_space_constraint(x, pltpu.HBM) for x in inputs),
        [HBM] * 4,
        scratch=[
            pltpu.VMEM((cells + cols, 128), F32),
            pltpu.SMEM(pole_mask.shape, jnp.int32),
            pltpu.SMEM(sea_mask.shape, jnp.int32),
            pltpu.SemaphoreType.DMA((4,)),
        ],
    )
    side_b = lax.ppermute(
        far_cols, "lon", [(i, (i + 1 if i % 2 else i - 1) % lons) for i in range(lons)]
    )
    near_cols, _ = lax.optimization_barrier((near_cols, core))
    side_a = swap(near_cols, lats)

    payload = call(
        register_kernel,
        jax.ShapeDtypeStruct((PAIR + STATS, NREG), BF16),
        (own, core, reg_queries),
        [VMEM] * 3,
        flops=4 * 2 * cells * NREG * 2 * PAIR,
    )

    queries = queries.reshape(cells, channels)
    square = jax.ShapeDtypeStruct((cells, channels), F32)
    inner, outer = (count(parts) for parts in segments(rows, cols))
    mixed, top, total, reg_weights = call(
        functools.partial(inner_kernel, rows, cols),
        (square, square, square, jax.ShapeDtypeStruct((HEADS, cells, NREG), BF16)),
        (queries, own, core, reg_keys, closed),
        [VMEM] * 5,
        scratch=[
            pltpu.VMEM((2, inner + NREG, PAIR + AUG), BF16),
            pltpu.VMEM((inner, channels), BF16),
        ],
        flops=2 * 2 * cells * inner * channels * 2,
    )

    corner_a, corner_b, _ = lax.optimization_barrier((side_a, side_b, payload))
    side_a, side_b, _, _ = lax.optimization_barrier((side_a, side_b, payload, mixed))

    def take(shard, size, start, count):
        taken = lax.dynamic_slice_in_dim(shard.reshape(2, -1, size, channels), start, count, 2)
        return taken.reshape(2, -1, channels)

    core_deep, cross_deep = (1 - lat % 2) * (rows - DEEP), (lat % 2) * (rows - DEEP)
    corner = swap(
        jnp.concatenate([take(s, rows, core_deep, DEEP) for s in (corner_a, corner_b)], axis=1), 1
    )
    cross = lax.ppermute(
        jnp.concatenate(
            [
                take(own, cells, (lat % 2) * (rows - RADIUS) * cols, RADIUS * cols),
                *[take(s, rows, cross_deep, DEEP) for s in (side_a, side_b)],
            ],
            axis=1,
        ),
        everyone,
        [(i, i ^ 3 if i % lats in (1, 2) else i ^ lats) for i in range(devices)],
    )
    rest, factor = call(
        functools.partial(outer_kernel, rows, cols),
        (square, square),
        (queries, side_a, side_b, corner, cross, top, total, closed),
        [VMEM] * 8,
        scratch=[pltpu.VMEM((2, outer, PAIR + AUG), BF16), pltpu.VMEM((outer, channels), BF16)],
        flops=2 * 2 * cells * outer * channels * 2,
    )

    near_bits, far_bits = NEAR, [(b, b + 1) for b in range(3, nbits, 2)]
    steps = list(zip([*far_bits, near_bits], [near_bits, *far_bits]))
    for step in steps:
        first, last = step is steps[0], step is steps[-1]
        gathered = [payload]
        for slot in range(3):
            pairs = []
            for i in range(devices):
                stage = step[(i ^ i >> TURN) & 1]
                chosen = slot + 1 if stage == near_bits else (3, 1, 2)[slot]
                flips = [b for k, b in enumerate(stage) if chosen >> k & 1]
                pairs.append((i, i ^ (sum(1 << b for b in flips) + (TURN in flips))))
            gathered.append(lax.ppermute(payload, everyone, pairs))
        if first:
            gathered[0], _ = lax.optimization_barrier((gathered[0], mixed))
        if last:
            gathered[0], rest, factor = lax.optimization_barrier((gathered[0], rest, factor))
        payload = call(
            functools.partial(merge_kernel, step, last),
            jax.ShapeDtypeStruct((PAIR if last else PAIR + STATS, NREG), BF16),
            tuple(gathered),
            [VMEM] * len(gathered),
        )

    other = swap(payload, 1)
    own_out, own_reg_out = call(
        own_share_kernel,
        (jax.ShapeDtypeStruct((cells, PAIR), BF16), jax.ShapeDtypeStruct((NREG, PAIR), BF16)),
        (mixed, factor, rest, reg_weights, payload),
        [VMEM] * 5,
    )
    attended, reg_out = call(
        final_kernel,
        (
            jax.ShapeDtypeStruct((cells, channels), BF16),
            jax.ShapeDtypeStruct((NREG, channels), BF16),
        ),
        (mixed, factor, rest, reg_weights, own_out, own_reg_out, other),
        [VMEM] * 7,
        flops=2 * cells * NREG * channels * 2,
    )
    return attended.reshape(rows, cols, channels), reg_out


def solution(mesh):
    return jax.shard_map(
        shards,
        mesh=mesh,
        in_specs=(P("lat", "lon", None), P(None, "lat", "lon", None), P(), P(), P(), P()),
        out_specs=(P("lat", "lon", None), P()),
        check_vma=False,
    )
```

```python
import functools

import jax
import jax.numpy as jnp
from jax import lax
from jax.experimental import pallas as pl
from jax.experimental.pallas import tpu as pltpu
from jax.sharding import PartitionSpec as P

HEADS = 4
HEAD_DIM = 64
NREG = 256
RADIUS = 6
TILE = 8
PAIR = 2 * HEAD_DIM
DEEP = 8
STATS = 8
NEAR = (1, 2)
TURN = 2
AUG = 128
MASKED = -8192.0
SCALE = HEAD_DIM ** (-0.5)

BF16 = jnp.bfloat16
F32 = jnp.float32
NT = (((1,), (1,)), ((), ()))
TN = (((0,), (0,)), ((), ()))
VMEM = pl.BlockSpec(memory_space=pltpu.VMEM)
HBM = pl.BlockSpec(memory_space=pltpu.HBM)


def dot(a, b, dims):
    return lax.dot_general(a, b, dims, preferred_element_type=F32)


def place():
    count = lax.axis_size("lon") * lax.axis_size("lat")
    flat = lax.axis_index("lon") * lax.axis_size("lat") + lax.axis_index("lat")
    return [(flat >> b) & 1 for b in range(count.bit_length() - 1)]


def half():
    bits = place()
    return bits[0] ^ bits[TURN]


def iota(shape, axis):
    return lax.broadcasted_iota(jnp.int32, shape, axis)


def call(kernel, out, args, specs, scratch=(), flops=0, limit=16):
    size = sum(a.size * a.dtype.itemsize for a in args)
    return pl.pallas_call(
        kernel,
        out_shape=out,
        in_specs=specs,
        out_specs=jax.tree.map(lambda _: VMEM, out),
        scratch_shapes=scratch,
        compiler_params=pltpu.CompilerParams(vmem_limit_bytes=limit * 2**20),
        cost_estimate=pl.CostEstimate(flops=flops, bytes_accessed=size, transcendentals=0),
    )(*args)


def pack(values, tops, sums):
    rows = iota((STATS, values.shape[1]), 0)
    stats = jnp.zeros((STATS, values.shape[1]), F32)
    for j in range(2):
        high = sums[j].astype(BF16).astype(F32)
        for row, value in ((j, tops[j]), (2 + 2 * j, high), (3 + 2 * j, sums[j] - high)):
            stats = jnp.where(rows == row, value, stats)
    return jnp.concatenate([values, stats], axis=0)


def sides_kernel(rows, cols, kv_ref, queries_ref, pole_ref, sea_ref, own, queries, near_ref, far_ref, closed_ref,
                 wide, pole, sea, sem):
    pairs = ((pole_ref, pole), (sea_ref, sea), (kv_ref, own), (queries_ref, queries))
    copies = [pltpu.make_async_copy(*pair, sem.at[k]) for k, pair in enumerate(pairs)]
    for copy in copies:
        copy.start()
    copies[0].wait()
    copies[1].wait()
    closed_ref[...] = jnp.broadcast_to(closed_tiles(rows, cols, pole, sea), closed_ref.shape)
    copies[2].wait()
    odd = lax.axis_index("lon") % 2 == 1
    for k in range(2):
        for lane in range(0, own.shape[2], 128):
            lanes = slice(lane, lane + 128)
            wide[: own.shape[1]] = own[k, :, lanes].astype(F32)
            for c in range(RADIUS):
                low = wide[pl.ds(c, rows, stride=cols)]
                high = wide[pl.ds(cols - RADIUS + c, rows, stride=cols)]
                near_ref[k, c * rows : (c + 1) * rows, lanes] = jnp.where(odd, low, high).astype(BF16)
                far_ref[k, c * rows : (c + 1) * rows, lanes] = jnp.where(odd, high, low).astype(BF16)
    copies[3].wait()


def register_kernel(own, other, queries, out_ref):
    lanes = pl.ds(pl.multiple_of(half() * PAIR, PAIR), PAIR)
    keys = jnp.concatenate([own[0, :, lanes], other[0, :, lanes]], axis=0)
    vals = jnp.concatenate([own[1, :, lanes], other[1, :, lanes]], axis=0)
    scaled = queries[:, lanes] * jnp.asarray(SCALE, BF16)
    first = iota(scaled.shape, 1) < HEAD_DIM
    asked = [jnp.where(first == (j == 0), scaled, jnp.zeros_like(scaled)) for j in range(2)]
    scores = [dot(keys, each, NT) for each in asked]
    ones = jnp.ones((keys.shape[0], HEAD_DIM), BF16)
    parts, tops, sums = [], [], []
    for j in range(2):
        top = jnp.max(scores[j], axis=0, keepdims=True).astype(BF16).astype(F32)
        tops.append(top)
        weights = jnp.exp(scores[j] - top).astype(BF16)
        both = dot(jnp.concatenate([vals[:, j * HEAD_DIM : (j + 1) * HEAD_DIM], ones], axis=1), weights, TN)
        parts.append(both[:HEAD_DIM])
        sums.append(both[HEAD_DIM : HEAD_DIM + 1])
    out_ref[...] = pack(jnp.concatenate(parts, axis=0), tops, sums).astype(BF16)


def merge_kernel(stages, last, *refs):
    payloads, out_ref = refs[:-1], refs[-1]
    here = place()
    found = [r[...] for r in payloads]

    def turned(bits):
        low, high = (here[b] for b in bits)
        return (low, high) if bits == NEAR else (high, low ^ high)

    for level, (first, second) in enumerate(zip(*map(turned, stages))):
        swap = jnp.where(half() == 0, first, second) == 1
        step = 1 << level
        for low in range(len(found)):
            if not low & step:
                a, b = found[low], found[low + step]
                found[low], found[low + step] = jnp.where(swap, b, a), jnp.where(swap, a, b)
    found = [(x[:PAIR].astype(F32), x[PAIR:].astype(F32)) for x in found]
    upper = iota((PAIR, found[0][0].shape[1]), 0) < HEAD_DIM
    tops, sums, factors = [], [], []
    for j in range(2):
        each = [stats[j : j + 1] for _, stats in found]
        top = functools.reduce(jnp.maximum, each)
        factor = [jnp.exp(e - top) for e in each]
        totals = [
            f * (stats[2 + 2 * j : 3 + 2 * j] + stats[3 + 2 * j : 4 + 2 * j])
            for f, (_, stats) in zip(factor, found)
        ]
        tops.append(top)
        sums.append(functools.reduce(jnp.add, totals))
        factors.append(factor)
    merged = functools.reduce(
        jnp.add,
        [values * jnp.where(upper, f, g) for f, g, (values, _) in zip(*factors, found)],
    )
    if last:
        out_ref[...] = (merged / jnp.where(upper, sums[0], sums[1])).astype(BF16)
    else:
        out_ref[...] = pack(merged, tops, sums).astype(BF16)


def segments(rows, cols):
    inner = (
        (rows, cols, False, 0, 0),
        (RADIUS, cols, False, "core", 0),
    )
    outer = (
        (RADIUS, rows, True, 0, "a"),
        (RADIUS, rows, True, 0, "b"),
        (RADIUS, DEEP, True, "core deep", "a"),
        (RADIUS, DEEP, True, "core deep", "b"),
        (RADIUS, cols, False, "cross", 0),
        (RADIUS, DEEP, True, "cross deep", "a"),
        (RADIUS, DEEP, True, "cross deep", "b"),
    )
    return inner, outer


def count(parts):
    return sum(part[0] * part[1] for part in parts)


def closed_tiles(rows, cols, pole, sea):
    lat, lon = lax.axis_index("lat"), lax.axis_index("lon")
    bands, tiles = sea.shape
    down, across = rows // TILE, cols // TILE
    lane = iota((1, AUG), 1)
    closed = jnp.zeros((1, AUG), F32)
    for i in range(down + 2):
        band = lat * down - 1 + i
        inside = (band >= 0) & (band < bands)
        band = jnp.clip(band, 0, bands - 1)
        for j in range(across + 2):
            tile = (lon * across - 1 + j + tiles) % tiles
            kept = inside & (pole[band] * sea[band, tile] > 0)
            at = rows + cols + i * (across + 2) + j
            closed = jnp.where(lane == at, jnp.where(kept, 0.0, MASKED), closed)
    return closed


def masks(rows, cols, closed, parts):
    lat, lon = lax.axis_index("lat"), lax.axis_index("lon")
    across = cols // TILE
    lat_odd, lon_odd = lat % 2 == 1, lon % 2 == 1
    starts = {
        0: 0,
        "core": jnp.where(lat_odd, -RADIUS, rows),
        "core deep": jnp.where(lat_odd, -DEEP, rows),
        "cross": jnp.where(lat_odd, rows, -RADIUS),
        "cross deep": jnp.where(lat_odd, rows, -DEEP),
        "a": jnp.where(lon_odd, -RADIUS, cols),
        "b": jnp.where(lon_odd, cols, -RADIUS),
    }
    lane = iota((1, AUG), 1)
    for slow, fast, fast_rows, row, col in parts:
        index = iota((slow * fast, AUG), 0)
        outer, inner = index >> (fast.bit_length() - 1), index & (fast - 1)
        row = starts[row] + (inner if fast_rows else outer)
        col = starts[col] + (outer if fast_rows else inner)
        apart = jnp.where(lane < rows, lane - row, lane - rows - col)
        far = (lane < rows + cols) & (jnp.abs(apart) > RADIUS)
        cell = ((row + TILE) >> 3) * (across + 2) + ((col + TILE) >> 3)
        value = jnp.where(lane - (rows + cols) == cell, closed, 0.0)
        yield jnp.where(far, MASKED, value).astype(BF16)


def fill(kbuf, vbuf, blocks, mask_blocks):
    ahead = kbuf.shape[1] - vbuf.shape[0]
    offset = 0
    for keys, vals in blocks:
        end = offset + keys.shape[0]
        for p in range(2):
            kbuf[p, ahead + offset : ahead + end, :PAIR] = keys[:, p * PAIR : (p + 1) * PAIR]
        vbuf[offset:end] = vals
        offset = end
    offset = ahead
    for mask in mask_blocks:
        for p in range(2):
            kbuf[p, offset : offset + mask.shape[0], PAIR:] = mask
        offset += mask.shape[0]


def attend(rows, cols, q_ref, kbuf, vbuf):
    size, ahead = rows * cols, kbuf.shape[1] - vbuf.shape[0]
    query = iota((size, AUG), 0)
    lane = iota((size, AUG), 1)
    tiles = (rows // TILE + 2) * (cols // TILE + 2)
    hot = (lane == query >> (cols.bit_length() - 1)) | (lane - rows == query & (cols - 1))
    hot = hot | ((lane >= rows + cols) & (lane < rows + cols + tiles))
    hot = jnp.where(hot, 1.0, 0.0).astype(BF16)
    first = iota((size, PAIR), 1) < HEAD_DIM
    scores = []
    for p in range(2):
        scaled = q_ref[:, p * PAIR : (p + 1) * PAIR] * jnp.asarray(SCALE, BF16)
        for j in range(2):
            mine = jnp.where(first == (j == 0), scaled, jnp.zeros_like(scaled))
            scores.append(dot(jnp.concatenate([mine, hot], axis=1), kbuf[p], NT))
    for p in range(2):
        lanes = slice(p * PAIR, (p + 1) * PAIR)
        tops, totals, mixed, weights = [], [], [], []
        for each in scores[2 * p : 2 * p + 2]:
            top = jnp.max(each, axis=1, keepdims=True)
            each = jnp.exp(each - top)
            tops.append(top)
            totals.append(jnp.sum(each, axis=1, keepdims=True))
            weights.append(each.astype(BF16))
            mixed.append(jnp.dot(weights[-1][:, ahead:], vbuf[:, lanes], preferred_element_type=F32))
        yield p, lanes, *(jnp.where(first, *x) for x in (tops, totals, mixed)), weights


def inner_kernel(rows, cols, q_ref, own, core, reg_keys, closed_ref,
                 mixed_ref, top_ref, total_ref, reg_ref, kbuf, vbuf):
    first = jnp.where(lax.axis_index("lat") % 2 == 0, 0, (rows - RADIUS) * cols)
    taken = pl.ds(pl.multiple_of(first, 16), RADIUS * cols)
    blocks = [(own[0], own[1]), (core[0, taken], core[1, taken])]
    fill(kbuf, vbuf, blocks, masks(rows, cols, closed_ref[:1], segments(rows, cols)[0]))
    for p in range(2):
        kbuf[p, :NREG, :PAIR] = reg_keys[:, p * PAIR : (p + 1) * PAIR]
        kbuf[p, :NREG, PAIR:] = jnp.zeros((NREG, AUG), BF16)
    for p, lanes, top, total, mixed, weights in attend(rows, cols, q_ref, kbuf, vbuf):
        top_ref[:, lanes], total_ref[:, lanes], mixed_ref[:, lanes] = top, total, mixed
        for j in range(2):
            reg_ref[2 * p + j] = weights[j][:, :NREG]


def outer_kernel(rows, cols, q_ref, a, b, corner, cross, inner_top, inner_total, closed_ref,
                 rest_ref, factor_ref, kbuf, vbuf):
    blocks = [(ref[0], ref[1]) for ref in (a, b, corner, cross)]
    fill(kbuf, vbuf, blocks, masks(rows, cols, closed_ref[:1], segments(rows, cols)[1]))
    for _, lanes, top, total, mixed, _ in attend(rows, cols, q_ref, kbuf, vbuf):
        highest = jnp.maximum(top, inner_top[:, lanes])
        inner, outer = jnp.exp(inner_top[:, lanes] - highest), jnp.exp(top - highest)
        scale = 1.0 / (inner * inner_total[:, lanes] + outer * total)
        factor_ref[:, lanes] = inner * scale
        rest_ref[:, lanes] = mixed * (outer * scale)


def shares(inner, factor, rest, reg_weights, vals, which):
    lanes = pl.ds(pl.multiple_of(which * PAIR, PAIR), PAIR)
    first = iota((inner.shape[0], PAIR), 1) < HEAD_DIM
    added = [dot(reg_weights[2 * which + j], vals, NT) for j in range(2)]
    return (inner[:, lanes] + jnp.where(first, *added)) * factor[:, lanes] + rest[:, lanes]


def own_share_kernel(inner, factor, rest, reg_weights, mine, out_ref, reg_out_ref):
    out_ref[...] = shares(inner, factor, rest, reg_weights, mine[...], half()).astype(BF16)
    reg_out_ref[...] = mine[...].astype(F32).T.astype(BF16)


def final_kernel(inner, factor, rest, reg_weights, own_out, own_reg_out, other, out_ref, reg_out_ref):
    which = half()
    own = pl.ds(pl.multiple_of(which * PAIR, PAIR), PAIR)
    lanes = pl.ds(pl.multiple_of((1 - which) * PAIR, PAIR), PAIR)
    out_ref[:, own] = own_out[...]
    reg_out_ref[:, own] = own_reg_out[...]
    out_ref[:, lanes] = shares(inner, factor, rest, reg_weights, other[...], 1 - which).astype(BF16)
    reg_out_ref[:, lanes] = other[...].astype(F32).T.astype(BF16)


def shards(queries, key_values, pole_mask, sea_mask, reg_queries, reg_keys):
    rows, cols, channels = queries.shape
    lats, lons = lax.axis_size("lat"), lax.axis_size("lon")
    devices = lats * lons
    assert lats == 4 and lons & (lons - 1) == 0 and lons > 1
    assert rows & (rows - 1) == 0 and cols & (cols - 1) == 0 and rows % TILE == 0 and cols % TILE == 0 and TILE == DEEP == 8
    nbits = devices.bit_length() - 1
    assert nbits % 2 == 1
    lat = lax.axis_index("lat")
    everyone = ("lon", "lat")

    def swap(x, mask):
        return lax.ppermute(x, everyone, [(i, i ^ mask) for i in range(devices)])

    cells = rows * cols
    key_values = key_values.reshape(2, cells, channels)
    core = swap(key_values, 1)

    side = jax.ShapeDtypeStruct((2, RADIUS * rows, channels), BF16)
    inputs = (key_values, reg_queries, pole_mask, sea_mask)
    own, reg_queries, near_cols, far_cols, closed = call(
        functools.partial(sides_kernel, rows, cols),
        (
            jax.ShapeDtypeStruct(key_values.shape, BF16),
            jax.ShapeDtypeStruct(reg_queries.shape, BF16),
            side,
            side,
            jax.ShapeDtypeStruct((8, AUG), F32),
        ),
        tuple(pltpu.with_memory_space_constraint(x, pltpu.HBM) for x in inputs),
        [HBM] * 4,
        scratch=[
            pltpu.VMEM((cells + cols, 128), F32),
            pltpu.SMEM(pole_mask.shape, jnp.int32),
            pltpu.SMEM(sea_mask.shape, jnp.int32),
            pltpu.SemaphoreType.DMA((4,)),
        ],
    )
    side_b = lax.ppermute(
        far_cols, "lon", [(i, (i + 1 if i % 2 else i - 1) % lons) for i in range(lons)]
    )
    near_cols, _ = lax.optimization_barrier((near_cols, core))
    side_a = swap(near_cols, lats)

    payload = call(
        register_kernel,
        jax.ShapeDtypeStruct((PAIR + STATS, NREG), BF16),
        (own, core, reg_queries),
        [VMEM] * 3,
        flops=4 * 2 * cells * NREG * 2 * PAIR,
    )

    queries = queries.reshape(cells, channels)
    square = jax.ShapeDtypeStruct((cells, channels), F32)
    inner, outer = (count(parts) for parts in segments(rows, cols))
    mixed, top, total, reg_weights = call(
        functools.partial(inner_kernel, rows, cols),
        (square, square, square, jax.ShapeDtypeStruct((HEADS, cells, NREG), BF16)),
        (queries, own, core, reg_keys, closed),
        [VMEM] * 5,
        scratch=[
            pltpu.VMEM((2, inner + NREG, PAIR + AUG), BF16),
            pltpu.VMEM((inner, channels), BF16),
        ],
        flops=2 * 2 * cells * inner * channels * 2,
    )

    corner_a, corner_b, _ = lax.optimization_barrier((side_a, side_b, payload))
    side_a, side_b, _, _ = lax.optimization_barrier((side_a, side_b, payload, mixed))

    def take(shard, size, start, count):
        taken = lax.dynamic_slice_in_dim(shard.reshape(2, -1, size, channels), start, count, 2)
        return taken.reshape(2, -1, channels)

    core_deep, cross_deep = (1 - lat % 2) * (rows - DEEP), (lat % 2) * (rows - DEEP)
    corner = swap(
        jnp.concatenate([take(s, rows, core_deep, DEEP) for s in (corner_a, corner_b)], axis=1), 1
    )
    cross = lax.ppermute(
        jnp.concatenate(
            [
                take(own, cells, (lat % 2) * (rows - RADIUS) * cols, RADIUS * cols),
                *[take(s, rows, cross_deep, DEEP) for s in (side_a, side_b)],
            ],
            axis=1,
        ),
        everyone,
        [(i, i ^ 3 if i % lats in (1, 2) else i ^ lats) for i in range(devices)],
    )
    rest, factor = call(
        functools.partial(outer_kernel, rows, cols),
        (square, square),
        (queries, side_a, side_b, corner, cross, top, total, closed),
        [VMEM] * 8,
        scratch=[pltpu.VMEM((2, outer, PAIR + AUG), BF16), pltpu.VMEM((outer, channels), BF16)],
        flops=2 * 2 * cells * outer * channels * 2,
    )

    near_bits, far_bits = NEAR, [(b, b + 1) for b in range(3, nbits, 2)]
    steps = list(zip([*far_bits, near_bits], [near_bits, *far_bits]))
    for step in steps:
        first, last = step is steps[0], step is steps[-1]
        gathered = [payload]
        for slot in range(3):
            pairs = []
            for i in range(devices):
                stage = step[(i ^ i >> TURN) & 1]
                chosen = slot + 1 if stage == near_bits else (3, 1, 2)[slot]
                flips = [b for k, b in enumerate(stage) if chosen >> k & 1]
                pairs.append((i, i ^ (sum(1 << b for b in flips) + (TURN in flips))))
            gathered.append(lax.ppermute(payload, everyone, pairs))
        if first:
            gathered[0], _ = lax.optimization_barrier((gathered[0], mixed))
        if last:
            gathered[0], rest, factor = lax.optimization_barrier((gathered[0], rest, factor))
        payload = call(
            functools.partial(merge_kernel, step, last),
            jax.ShapeDtypeStruct((PAIR if last else PAIR + STATS, NREG), BF16),
            tuple(gathered),
            [VMEM] * len(gathered),
        )

    other = swap(payload, 1)
    own_out, own_reg_out = call(
        own_share_kernel,
        (jax.ShapeDtypeStruct((cells, PAIR), BF16), jax.ShapeDtypeStruct((NREG, PAIR), BF16)),
        (mixed, factor, rest, reg_weights, payload),
        [VMEM] * 5,
    )
    attended, reg_out = call(
        final_kernel,
        (
            jax.ShapeDtypeStruct((cells, channels), BF16),
            jax.ShapeDtypeStruct((NREG, channels), BF16),
        ),
        (mixed, factor, rest, reg_weights, own_out, own_reg_out, other),
        [VMEM] * 7,
        flops=2 * cells * NREG * channels * 2,
    )
    return attended.reshape(rows, cols, channels), reg_out


def solution(mesh):
    return jax.shard_map(
        shards,
        mesh=mesh,
        in_specs=(P("lat", "lon", None), P(None, "lat", "lon", None), P(), P(), P(), P()),
        out_specs=(P("lat", "lon", None), P()),
        check_vma=False,
    )
```

```python
import functools

import jax
import jax.numpy as jnp
from jax import lax
from jax.experimental import pallas as pl
from jax.experimental.pallas import tpu as pltpu
from jax.sharding import PartitionSpec as P

HEADS = 4
HEAD_DIM = 64
NREG = 256
RADIUS = 6
TILE = 8
PAIR = 2 * HEAD_DIM
DEEP = 8
STATS = 8
NEAR = (1, 2)
TURN = 2
AUG = 128
MASKED = -8192.0
SCALE = HEAD_DIM ** (-0.5)

BF16 = jnp.bfloat16
F32 = jnp.float32
NT = (((1,), (1,)), ((), ()))
TN = (((0,), (0,)), ((), ()))
VMEM = pl.BlockSpec(memory_space=pltpu.VMEM)
HBM = pl.BlockSpec(memory_space=pltpu.HBM)


def dot(a, b, dims):
    return lax.dot_general(a, b, dims, preferred_element_type=F32)


def place():
    count = lax.axis_size("lon") * lax.axis_size("lat")
    flat = lax.axis_index("lon") * lax.axis_size("lat") + lax.axis_index("lat")
    return [(flat >> b) & 1 for b in range(count.bit_length() - 1)]


def half():
    bits = place()
    return bits[0] ^ bits[TURN]


def iota(shape, axis):
    return lax.broadcasted_iota(jnp.int32, shape, axis)


def call(kernel, out, args, specs, scratch=(), flops=0, limit=16):
    size = sum(a.size * a.dtype.itemsize for a in args)
    return pl.pallas_call(
        kernel,
        out_shape=out,
        in_specs=specs,
        out_specs=jax.tree.map(lambda _: VMEM, out),
        scratch_shapes=scratch,
        compiler_params=pltpu.CompilerParams(vmem_limit_bytes=limit * 2**20),
        cost_estimate=pl.CostEstimate(flops=flops, bytes_accessed=size, transcendentals=0),
    )(*args)


def pack(values, tops, sums):
    rows = iota((STATS, values.shape[1]), 0)
    stats = jnp.zeros((STATS, values.shape[1]), F32)
    for j in range(2):
        high = sums[j].astype(BF16).astype(F32)
        for row, value in ((j, tops[j]), (2 + 2 * j, high), (3 + 2 * j, sums[j] - high)):
            stats = jnp.where(rows == row, value, stats)
    return jnp.concatenate([values, stats], axis=0)


def sides_kernel(rows, cols, kv_ref, queries_ref, pole_ref, sea_ref, own, queries, near_ref, far_ref, closed_ref,
                 wide, pole, sea, sem):
    pairs = ((pole_ref, pole), (sea_ref, sea), (kv_ref, own), (queries_ref, queries))
    copies = [pltpu.make_async_copy(*pair, sem.at[k]) for k, pair in enumerate(pairs)]
    for copy in copies:
        copy.start()
    copies[0].wait()
    copies[1].wait()
    closed_ref[...] = jnp.broadcast_to(closed_tiles(rows, cols, pole, sea), closed_ref.shape)
    copies[2].wait()
    odd = lax.axis_index("lon") % 2 == 1
    for k in range(2):
        for lane in range(0, own.shape[2], 128):
            lanes = slice(lane, lane + 128)
            wide[: own.shape[1]] = own[k, :, lanes].astype(F32)
            for c in range(RADIUS):
                low = wide[pl.ds(c, rows, stride=cols)]
                high = wide[pl.ds(cols - RADIUS + c, rows, stride=cols)]
                near_ref[k, c * rows : (c + 1) * rows, lanes] = jnp.where(odd, low, high).astype(BF16)
                far_ref[k, c * rows : (c + 1) * rows, lanes] = jnp.where(odd, high, low).astype(BF16)
    copies[3].wait()


def register_kernel(own, other, queries, out_ref):
    lanes = pl.ds(pl.multiple_of(half() * PAIR, PAIR), PAIR)
    keys = jnp.concatenate([own[0, :, lanes], other[0, :, lanes]], axis=0)
    vals = jnp.concatenate([own[1, :, lanes], other[1, :, lanes]], axis=0)
    scaled = queries[:, lanes] * jnp.asarray(SCALE, BF16)
    first = iota(scaled.shape, 1) < HEAD_DIM
    asked = [jnp.where(first == (j == 0), scaled, jnp.zeros_like(scaled)) for j in range(2)]
    scores = [dot(keys, each, NT) for each in asked]
    ones = jnp.ones((keys.shape[0], HEAD_DIM), BF16)
    parts, tops, sums = [], [], []
    for j in range(2):
        top = jnp.max(scores[j], axis=0, keepdims=True).astype(BF16).astype(F32)
        tops.append(top)
        weights = jnp.exp(scores[j] - top).astype(BF16)
        both = dot(jnp.concatenate([vals[:, j * HEAD_DIM : (j + 1) * HEAD_DIM], ones], axis=1), weights, TN)
        parts.append(both[:HEAD_DIM])
        sums.append(both[HEAD_DIM : HEAD_DIM + 1])
    out_ref[...] = pack(jnp.concatenate(parts, axis=0), tops, sums).astype(BF16)


def merge_kernel(stages, last, *refs):
    payloads, out_ref = refs[:-1], refs[-1]
    here = place()
    found = [r[...] for r in payloads]

    def turned(bits):
        low, high = (here[b] for b in bits)
        return (low, high) if bits == NEAR else (high, low ^ high)

    for level, (first, second) in enumerate(zip(*map(turned, stages))):
        swap = jnp.where(half() == 0, first, second) == 1
        step = 1 << level
        for low in range(len(found)):
            if not low & step:
                a, b = found[low], found[low + step]
                found[low], found[low + step] = jnp.where(swap, b, a), jnp.where(swap, a, b)
    found = [(x[:PAIR].astype(F32), x[PAIR:].astype(F32)) for x in found]
    upper = iota((PAIR, found[0][0].shape[1]), 0) < HEAD_DIM
    tops, sums, factors = [], [], []
    for j in range(2):
        each = [stats[j : j + 1] for _, stats in found]
        top = functools.reduce(jnp.maximum, each)
        factor = [jnp.exp(e - top) for e in each]
        totals = [
            f * (stats[2 + 2 * j : 3 + 2 * j] + stats[3 + 2 * j : 4 + 2 * j])
            for f, (_, stats) in zip(factor, found)
        ]
        tops.append(top)
        sums.append(functools.reduce(jnp.add, totals))
        factors.append(factor)
    merged = functools.reduce(
        jnp.add,
        [values * jnp.where(upper, f, g) for f, g, (values, _) in zip(*factors, found)],
    )
    if last:
        out_ref[...] = (merged / jnp.where(upper, sums[0], sums[1])).astype(BF16)
    else:
        out_ref[...] = pack(merged, tops, sums).astype(BF16)


def segments(rows, cols):
    inner = (
        (rows, cols, False, 0, 0),
        (RADIUS, cols, False, "core", 0),
    )
    outer = (
        (RADIUS, rows, True, 0, "a"),
        (RADIUS, rows, True, 0, "b"),
        (RADIUS, DEEP, True, "core deep", "a"),
        (RADIUS, DEEP, True, "core deep", "b"),
        (RADIUS, cols, False, "cross", 0),
        (RADIUS, DEEP, True, "cross deep", "a"),
        (RADIUS, DEEP, True, "cross deep", "b"),
    )
    return inner, outer


def count(parts):
    return sum(part[0] * part[1] for part in parts)


def closed_tiles(rows, cols, pole, sea):
    lat, lon = lax.axis_index("lat"), lax.axis_index("lon")
    bands, tiles = sea.shape
    down, across = rows // TILE, cols // TILE
    lane = iota((1, AUG), 1)
    closed = jnp.zeros((1, AUG), F32)
    for i in range(down + 2):
        band = lat * down - 1 + i
        inside = (band >= 0) & (band < bands)
        band = jnp.clip(band, 0, bands - 1)
        for j in range(across + 2):
            tile = (lon * across - 1 + j + tiles) % tiles
            kept = inside & (pole[band] * sea[band, tile] > 0)
            at = rows + cols + i * (across + 2) + j
            closed = jnp.where(lane == at, jnp.where(kept, 0.0, MASKED), closed)
    return closed


def masks(rows, cols, closed, parts):
    lat, lon = lax.axis_index("lat"), lax.axis_index("lon")
    across = cols // TILE
    lat_odd, lon_odd = lat % 2 == 1, lon % 2 == 1
    starts = {
        0: 0,
        "core": jnp.where(lat_odd, -RADIUS, rows),
        "core deep": jnp.where(lat_odd, -DEEP, rows),
        "cross": jnp.where(lat_odd, rows, -RADIUS),
        "cross deep": jnp.where(lat_odd, rows, -DEEP),
        "a": jnp.where(lon_odd, -RADIUS, cols),
        "b": jnp.where(lon_odd, cols, -RADIUS),
    }
    lane = iota((1, AUG), 1)
    for slow, fast, fast_rows, row, col in parts:
        index = iota((slow * fast, AUG), 0)
        outer, inner = index >> (fast.bit_length() - 1), index & (fast - 1)
        row = starts[row] + (inner if fast_rows else outer)
        col = starts[col] + (outer if fast_rows else inner)
        apart = jnp.where(lane < rows, lane - row, lane - rows - col)
        far = (lane < rows + cols) & (jnp.abs(apart) > RADIUS)
        cell = ((row + TILE) >> 3) * (across + 2) + ((col + TILE) >> 3)
        value = jnp.where(lane - (rows + cols) == cell, closed, 0.0)
        yield jnp.where(far, MASKED, value).astype(BF16)


def fill(kbuf, vbuf, blocks, mask_blocks):
    ahead = kbuf.shape[1] - vbuf.shape[0]
    offset = 0
    for keys, vals in blocks:
        end = offset + keys.shape[0]
        for p in range(2):
            kbuf[p, ahead + offset : ahead + end, :PAIR] = keys[:, p * PAIR : (p + 1) * PAIR]
        vbuf[offset:end] = vals
        offset = end
    offset = ahead
    for mask in mask_blocks:
        for p in range(2):
            kbuf[p, offset : offset + mask.shape[0], PAIR:] = mask
        offset += mask.shape[0]


def attend(rows, cols, q_ref, kbuf, vbuf):
    size, ahead = rows * cols, kbuf.shape[1] - vbuf.shape[0]
    query = iota((size, AUG), 0)
    lane = iota((size, AUG), 1)
    tiles = (rows // TILE + 2) * (cols // TILE + 2)
    hot = (lane == query >> (cols.bit_length() - 1)) | (lane - rows == query & (cols - 1))
    hot = hot | ((lane >= rows + cols) & (lane < rows + cols + tiles))
    hot = jnp.where(hot, 1.0, 0.0).astype(BF16)
    first = iota((size, PAIR), 1) < HEAD_DIM
    scores = []
    for p in range(2):
        scaled = q_ref[:, p * PAIR : (p + 1) * PAIR] * jnp.asarray(SCALE, BF16)
        for j in range(2):
            mine = jnp.where(first == (j == 0), scaled, jnp.zeros_like(scaled))
            scores.append(dot(jnp.concatenate([mine, hot], axis=1), kbuf[p], NT))
    for p in range(2):
        lanes = slice(p * PAIR, (p + 1) * PAIR)
        tops, totals, mixed, weights = [], [], [], []
        for each in scores[2 * p : 2 * p + 2]:
            top = jnp.max(each, axis=1, keepdims=True)
            each = jnp.exp(each - top)
            tops.append(top)
            totals.append(jnp.sum(each, axis=1, keepdims=True))
            weights.append(each.astype(BF16))
            mixed.append(jnp.dot(weights[-1][:, ahead:], vbuf[:, lanes], preferred_element_type=F32))
        yield p, lanes, *(jnp.where(first, *x) for x in (tops, totals, mixed)), weights


def inner_kernel(rows, cols, q_ref, own, core, reg_keys, closed_ref,
                 mixed_ref, top_ref, total_ref, reg_ref, kbuf, vbuf):
    first = jnp.where(lax.axis_index("lat") % 2 == 0, 0, (rows - RADIUS) * cols)
    taken = pl.ds(pl.multiple_of(first, 16), RADIUS * cols)
    blocks = [(own[0], own[1]), (core[0, taken], core[1, taken])]
    fill(kbuf, vbuf, blocks, masks(rows, cols, closed_ref[:1], segments(rows, cols)[0]))
    for p in range(2):
        kbuf[p, :NREG, :PAIR] = reg_keys[:, p * PAIR : (p + 1) * PAIR]
        kbuf[p, :NREG, PAIR:] = jnp.zeros((NREG, AUG), BF16)
    for p, lanes, top, total, mixed, weights in attend(rows, cols, q_ref, kbuf, vbuf):
        top_ref[:, lanes], total_ref[:, lanes], mixed_ref[:, lanes] = top, total, mixed
        for j in range(2):
            reg_ref[2 * p + j] = weights[j][:, :NREG]


def outer_kernel(rows, cols, q_ref, a, b, corner, cross, inner_top, inner_total, closed_ref,
                 rest_ref, factor_ref, kbuf, vbuf):
    blocks = [(ref[0], ref[1]) for ref in (a, b, corner, cross)]
    fill(kbuf, vbuf, blocks, masks(rows, cols, closed_ref[:1], segments(rows, cols)[1]))
    for _, lanes, top, total, mixed, _ in attend(rows, cols, q_ref, kbuf, vbuf):
        highest = jnp.maximum(top, inner_top[:, lanes])
        inner, outer = jnp.exp(inner_top[:, lanes] - highest), jnp.exp(top - highest)
        scale = 1.0 / (inner * inner_total[:, lanes] + outer * total)
        factor_ref[:, lanes] = inner * scale
        rest_ref[:, lanes] = mixed * (outer * scale)


def shares(inner, factor, rest, reg_weights, vals, which):
    lanes = pl.ds(pl.multiple_of(which * PAIR, PAIR), PAIR)
    first = iota((inner.shape[0], PAIR), 1) < HEAD_DIM
    added = [dot(reg_weights[2 * which + j], vals, NT) for j in range(2)]
    return (inner[:, lanes] + jnp.where(first, *added)) * factor[:, lanes] + rest[:, lanes]


def own_share_kernel(inner, factor, rest, reg_weights, mine, out_ref, reg_out_ref):
    out_ref[...] = shares(inner, factor, rest, reg_weights, mine[...], half()).astype(BF16)
    reg_out_ref[...] = mine[...].astype(F32).T.astype(BF16)


def final_kernel(inner, factor, rest, reg_weights, own_out, own_reg_out, other, out_ref, reg_out_ref):
    which = half()
    own = pl.ds(pl.multiple_of(which * PAIR, PAIR), PAIR)
    lanes = pl.ds(pl.multiple_of((1 - which) * PAIR, PAIR), PAIR)
    out_ref[:, own] = own_out[...]
    reg_out_ref[:, own] = own_reg_out[...]
    out_ref[:, lanes] = shares(inner, factor, rest, reg_weights, other[...], 1 - which).astype(BF16)
    reg_out_ref[:, lanes] = other[...].astype(F32).T.astype(BF16)


def shards(queries, key_values, pole_mask, sea_mask, reg_queries, reg_keys):
    rows, cols, channels = queries.shape
    lats, lons = lax.axis_size("lat"), lax.axis_size("lon")
    devices = lats * lons
    assert lats == 4 and lons & (lons - 1) == 0 and lons > 1
    assert rows & (rows - 1) == 0 and cols & (cols - 1) == 0 and rows % TILE == 0 and cols % TILE == 0 and TILE == DEEP == 8
    nbits = devices.bit_length() - 1
    assert nbits % 2 == 1
    lat = lax.axis_index("lat")
    everyone = ("lon", "lat")

    def swap(x, mask):
        return lax.ppermute(x, everyone, [(i, i ^ mask) for i in range(devices)])

    cells = rows * cols
    key_values = key_values.reshape(2, cells, channels)
    core = swap(key_values, 1)

    side = jax.ShapeDtypeStruct((2, RADIUS * rows, channels), BF16)
    inputs = (key_values, reg_queries, pole_mask, sea_mask)
    own, reg_queries, near_cols, far_cols, closed = call(
        functools.partial(sides_kernel, rows, cols),
        (
            jax.ShapeDtypeStruct(key_values.shape, BF16),
            jax.ShapeDtypeStruct(reg_queries.shape, BF16),
            side,
            side,
            jax.ShapeDtypeStruct((8, AUG), F32),
        ),
        tuple(pltpu.with_memory_space_constraint(x, pltpu.HBM) for x in inputs),
        [HBM] * 4,
        scratch=[
            pltpu.VMEM((cells + cols, 128), F32),
            pltpu.SMEM(pole_mask.shape, jnp.int32),
            pltpu.SMEM(sea_mask.shape, jnp.int32),
            pltpu.SemaphoreType.DMA((4,)),
        ],
    )
    side_b = lax.ppermute(
        far_cols, "lon", [(i, (i + 1 if i % 2 else i - 1) % lons) for i in range(lons)]
    )

    payload = call(
        register_kernel,
        jax.ShapeDtypeStruct((PAIR + STATS, NREG), BF16),
        (own, core, reg_queries),
        [VMEM] * 3,
        flops=4 * 2 * cells * NREG * 2 * PAIR,
    )

    near_cols, _ = lax.optimization_barrier((near_cols, payload))
    side_a = swap(near_cols, lats)
    queries = queries.reshape(cells, channels)
    square = jax.ShapeDtypeStruct((cells, channels), F32)
    inner, outer = (count(parts) for parts in segments(rows, cols))
    mixed, top, total, reg_weights = call(
        functools.partial(inner_kernel, rows, cols),
        (square, square, square, jax.ShapeDtypeStruct((HEADS, cells, NREG), BF16)),
        (queries, own, core, reg_keys, closed),
        [VMEM] * 5,
        scratch=[
            pltpu.VMEM((2, inner + NREG, PAIR + AUG), BF16),
            pltpu.VMEM((inner, channels), BF16),
        ],
        flops=2 * 2 * cells * inner * channels * 2,
    )

    corner_a, corner_b, _ = lax.optimization_barrier((side_a, side_b, payload))
    side_a, side_b, _, _ = lax.optimization_barrier((side_a, side_b, payload, mixed))

    def take(shard, size, start, count):
        taken = lax.dynamic_slice_in_dim(shard.reshape(2, -1, size, channels), start, count, 2)
        return taken.reshape(2, -1, channels)

    core_deep, cross_deep = (1 - lat % 2) * (rows - DEEP), (lat % 2) * (rows - DEEP)
    corner = swap(
        jnp.concatenate([take(s, rows, core_deep, DEEP) for s in (corner_a, corner_b)], axis=1), 1
    )
    cross = lax.ppermute(
        jnp.concatenate(
            [
                take(own, cells, (lat % 2) * (rows - RADIUS) * cols, RADIUS * cols),
                *[take(s, rows, cross_deep, DEEP) for s in (side_a, side_b)],
            ],
            axis=1,
        ),
        everyone,
        [(i, i ^ 3 if i % lats in (1, 2) else i ^ lats) for i in range(devices)],
    )
    rest, factor = call(
        functools.partial(outer_kernel, rows, cols),
        (square, square),
        (queries, side_a, side_b, corner, cross, top, total, closed),
        [VMEM] * 8,
        scratch=[pltpu.VMEM((2, outer, PAIR + AUG), BF16), pltpu.VMEM((outer, channels), BF16)],
        flops=2 * 2 * cells * outer * channels * 2,
    )

    near_bits, far_bits = NEAR, [(b, b + 1) for b in range(3, nbits, 2)]
    steps = list(zip([*far_bits, near_bits], [near_bits, *far_bits]))
    for step in steps:
        first, last = step is steps[0], step is steps[-1]
        gathered = [payload]
        for slot in range(3):
            pairs = []
            for i in range(devices):
                stage = step[(i ^ i >> TURN) & 1]
                chosen = slot + 1 if stage == near_bits else (3, 1, 2)[slot]
                flips = [b for k, b in enumerate(stage) if chosen >> k & 1]
                pairs.append((i, i ^ (sum(1 << b for b in flips) + (TURN in flips))))
            gathered.append(lax.ppermute(payload, everyone, pairs))
        if first:
            gathered[0], _ = lax.optimization_barrier((gathered[0], mixed))
        if last:
            gathered[0], rest, factor = lax.optimization_barrier((gathered[0], rest, factor))
        payload = call(
            functools.partial(merge_kernel, step, last),
            jax.ShapeDtypeStruct((PAIR if last else PAIR + STATS, NREG), BF16),
            tuple(gathered),
            [VMEM] * len(gathered),
        )

    other = swap(payload, 1)
    own_out, own_reg_out = call(
        own_share_kernel,
        (jax.ShapeDtypeStruct((cells, PAIR), BF16), jax.ShapeDtypeStruct((NREG, PAIR), BF16)),
        (mixed, factor, rest, reg_weights, payload),
        [VMEM] * 5,
    )
    attended, reg_out = call(
        final_kernel,
        (
            jax.ShapeDtypeStruct((cells, channels), BF16),
            jax.ShapeDtypeStruct((NREG, channels), BF16),
        ),
        (mixed, factor, rest, reg_weights, own_out, own_reg_out, other),
        [VMEM] * 7,
        flops=2 * cells * NREG * channels * 2,
    )
    return attended.reshape(rows, cols, channels), reg_out


def solution(mesh):
    return jax.shard_map(
        shards,
        mesh=mesh,
        in_specs=(P("lat", "lon", None), P(None, "lat", "lon", None), P(), P(), P(), P()),
        out_specs=(P("lat", "lon", None), P()),
        check_vma=False,
    )
```
